128 devices in a mesh: dp: 16 (over x_lo, y, core), expert: 8 (over z, x_hi).
Axes of the slice: x: 4 (x_hi: 2, x_lo: 2; x = x_hi * 2 + x_lo), y: 4, z: 4, core: 2. Of those that a mesh axis runs over, the one named last changes fastest.
Arguments:
- tokens: bfloat16 [16384, 1536], P(('dp', 'expert')), may hold values from -6 to 6
- cotangent: bfloat16 [16384, 1536], P(('dp', 'expert')), may hold values from -6 to 6
- seq_lengths: int32 [16, 4], P('dp'), may hold values from 1 to 1021, as said below
- expert_ids: int32 [16384, 8], P(('dp', 'expert')), may hold values from 0 to 39, all different within a row; in each aligned block of 128 rows (0 to 127, 128 to 255, ...) at most 32 rows name the same one
- w_query: bfloat16 [1536, 1536], P(('dp', 'expert')), may hold values from -0.15625 to 0.15625
- w_key: bfloat16 [1536, 512], P(('dp', 'expert')), may hold values from -0.15625 to 0.15625
- w_value: bfloat16 [1536, 512], P(('dp', 'expert')), may hold values from -0.15625 to 0.15625
- w_output: bfloat16 [1536, 1536], P(('dp', 'expert')), may hold values from -2.5 to 2.5
- norm_one: bfloat16 [1536], P(('dp', 'expert')), may hold values from 0.5 to 1.5
- norm_two: bfloat16 [1536], P(('dp', 'expert')), may hold values from 0.5 to 1.5
- w_router: bfloat16 [1536, 40], P(('dp', 'expert')), may hold values from -0.078125 to 0.078125
- w_gate: bfloat16 [40, 1536, 512], P('expert', 'dp'), may hold values from -0.15625 to 0.15625
- w_up: bfloat16 [40, 1536, 512], P('expert', 'dp'), may hold values from -0.15625 to 0.15625
- w_down: bfloat16 [40, 512, 1536], P('expert', 'dp'), may hold values from -1 to 1
Outputs:
- mixed: bfloat16 [16384, 1536], P(('dp', 'expert'))
- grad_tokens: float32 [16384, 1536], P(('dp', 'expert'))
- grad_w_query: float32 [1536, 1536], P(('dp', 'expert'))
- grad_w_key: float32 [1536, 512], P(('dp', 'expert'))
- grad_w_value: float32 [1536, 512], P(('dp', 'expert'))
- grad_w_output: float32 [1536, 1536], P(('dp', 'expert'))
- grad_norm_one: float32 [1536], P(('dp', 'expert'))
- grad_norm_two: float32 [1536], P(('dp', 'expert'))
- grad_w_router: float32 [1536, 40], P(('dp', 'expert'))
- grad_w_gate: float32 [40, 1536, 512], P('expert', 'dp')
- grad_w_up: float32 [40, 1536, 512], P('expert', 'dp')
- grad_w_down: float32 [40, 512, 1536], P('expert', 'dp')
The draws below stay inside these ranges and needn't reach their ends.
Inputs may be any that keep to these rules, and one draw needn't show every extreme that they name: `seq_lengths`: each row lists the lengths of the 4 sequences of one group in order; they sum to 1024. One of them, at a place drawn from the seed, holds all but at most 3 * (32) of the group's tokens. In one group, drawn from the seed, all the others have length 1. `expert_ids`: A token's 8 experts differ. Among the 128 rows of one device each expert is named at most 32 times.
All inputs are finite; a program needn't handle non-finite values.
Results may differ from the reference program's by a relative error of at most 0.02.
Values may be sent and summed in bfloat16 or wider, within the bound.
A program may use at most 256 MiB of HBM per device.

```python
import math
from functools import partial
import jax
import jax.numpy as jnp
import numpy as np
from jax import lax

D = 1536
HEADS = 24
KV_HEADS = 8
HEAD = 64
FFE = 512
TOP = 8
TOK_DEV = 128
NSEQ = 4
EXPERTS = 40
CAP = 32
GROUP = 1024
TOKENS = 16384
QW = 1536
KW = 512
N_DP = 16


def draw_seq_lengths(key, part):
    key = jax.random.fold_in(key, 11)
    short_key, place_key, group_key = jax.random.split(key, 3)
    shorter = jax.random.randint(short_key, (N_DP, NSEQ - 1), 1, TOK_DEV // 4 + 1, dtype=jnp.int32)
    chosen_group = jax.random.randint(group_key, (), 0, N_DP, dtype=jnp.int32)
    group_rows = jnp.arange(N_DP, dtype=jnp.int32)[:, None]
    shorter = jnp.where(group_rows == chosen_group, jnp.ones_like(shorter), shorter)
    longest = GROUP - jnp.sum(shorter, axis=1, keepdims=True)
    ordered = jnp.concatenate([longest, shorter], axis=1)
    ranking = jax.random.randint(place_key, (N_DP, NSEQ), 0, 1 << 20, dtype=jnp.int32) * NSEQ + jnp.arange(NSEQ, dtype=jnp.int32)[None, :]
    order = jnp.argsort(ranking, axis=1, stable=True)
    return jnp.take_along_axis(ordered, order, axis=1).astype(jnp.int32)


def block_scale(key, dims, cuts, low, high):
    def one(axis_at, shards_of):
        draws = jax.random.uniform(jax.random.fold_in(jax.random.fold_in(key, 6), axis_at), (shards_of,), jnp.float32, low / len(cuts), high / len(cuts))
        return jnp.repeat(jnp.exp(draws), dims[axis_at] // shards_of).reshape((-1,) + (1,) * (len(dims) - axis_at - 1))

    loudness = one(*cuts[0])
    for cut in cuts[1:]:
        loudness = loudness * one(*cut)
    return loudness


def shared_out(stream_key, own, number, rows, amount, top, limit, lean):
    order = jax.random.permutation(stream_key, amount)
    crowded, usual = load_shares(amount, rows * top, limit, lean, True), load_shares(amount, rows * top, limit, lean, False)
    places = jnp.arange(amount)

    def named(tallies, rotation):
        used = int((tallies > 0).sum())
        fixed = max(1, used // 4)
        moved = fixed + (places - fixed + rotation * (used - fixed)) % max(1, amount - fixed)
        return jnp.zeros((amount,), jnp.int32).at[order[jnp.where(places < fixed, places, moved)]].set(jnp.asarray(tallies, jnp.int32))

    tallies = jnp.where(number % 4 == 0, named(crowded, number // 4), named(usual, number - number // 4 - 1))
    mixed = jax.random.permutation(jax.random.fold_in(own, 3), amount)
    donor, receiver = mixed[0:amount // 2 * 2:2], mixed[1:amount // 2 * 2:2]
    room = jnp.minimum(tallies[donor] - 1, limit - tallies[receiver]) // 2
    room = jnp.where((donor == order[0]) | (receiver == order[0]) | (tallies[receiver] == 0), 0, jnp.maximum(room, 0))
    moved = jax.random.randint(jax.random.fold_in(own, 4), (amount // 2,), 0, 1 << 20) % (room + 1)
    tallies = tallies.at[donor].add(-moved).at[receiver].add(moved)
    labels = jnp.searchsorted(jnp.cumsum(tallies), jnp.arange(rows * top), side="right").astype(jnp.int32)
    listing = labels.reshape(top, rows).T
    listing = listing[jax.random.permutation(jax.random.fold_in(own, 1), rows)]
    rotation = jax.random.randint(jax.random.fold_in(own, 2), (rows, 1), 0, top)
    return jnp.take_along_axis(listing, (jnp.arange(top)[None, :] + rotation) % top, axis=1)


def load_shares(amount, total, reach, slope, full):
    portions = [(1 << 20) // math.isqrt(rank ** slope) + 1 for rank in range(1, amount + 1)]
    largest = reach if full else min(reach, max(-(-total // amount), total * portions[0] // sum(portions)))
    least = 1 if total - largest >= amount - 1 else 0
    holding, rest = [largest] + [least] * (amount - 1), total - largest - least * (amount - 1)
    while rest > 0:
        free = [i for i in range(1, amount) if holding[i] < largest] or [i for i in range(1, amount) if holding[i] < reach]
        mass, remaining = sum([portions[i] for i in free]), rest
        for i in free:
            extra = min(reach - holding[i], max(1, remaining * portions[i] // mass), rest)
            holding[i] = holding[i] + extra
            rest = rest - extra
    return np.array(holding)


def centred(own_key, shape, scale, limit, cuts=(), kind=jnp.bfloat16):
    values = jax.random.normal(own_key, shape, jnp.float32) * scale
    if len(cuts) > 0:
        values = block_scale(own_key, shape, cuts, -0.22, 0.18) * values
    return jnp.clip(values, min=-limit, max=limit).astype(kind)


def setup_inputs(seed: int = 0) -> dict:
    key_list = jax.random.split(jax.random.key(seed), 15)
    tokens = centred(key_list[0], (TOKENS, D), 1.0, 6.0, ((0, 128),))
    cotangent = centred(key_list[1], (TOKENS, D), 1.0, 6.0, ((0, 128),))
    seq_lengths = draw_seq_lengths(jax.random.fold_in(key_list[14], 71), 0)
    expert_ids_keys = jax.random.split(jax.random.fold_in(key_list[3], 1), TOKENS // TOK_DEV)
    expert_ids_turns = jax.random.permutation(jax.random.fold_in(key_list[3], 3), TOKENS // TOK_DEV)
    expert_ids = jax.vmap(lambda own, number: shared_out(jax.random.fold_in(key_list[3], 2), own, number, TOK_DEV, EXPERTS, TOP, CAP, 1))(expert_ids_keys, expert_ids_turns).reshape((TOKENS, TOP))
    w_query = centred(key_list[4], (D, QW), D ** -0.5, 0.15625, ((0, 128),))
    w_key = centred(key_list[5], (D, KW), D ** -0.5, 0.15625, ((0, 128),))
    w_value = centred(key_list[6], (D, KW), D ** -0.5, 0.15625, ((0, 128),))
    w_output = centred(key_list[7], (QW, D), (max(QW // 256, 1)) ** -0.5, 2.5, ((0, 128),))
    norm_one = jnp.clip(1.0 + 0.1 * jax.random.normal(key_list[8], (D,), jnp.float32), 0.5, 1.5).astype(jnp.bfloat16)
    norm_two = jnp.clip(1.0 + 0.1 * jax.random.normal(key_list[9], (D,), jnp.float32), 0.5, 1.5).astype(jnp.bfloat16)
    w_router = centred(key_list[10], (D, EXPERTS), (4 * D) ** -0.5, 0.078125, ((0, 128),))
    w_gate = centred(key_list[11], (EXPERTS, D, FFE), D ** -0.5, 0.15625, ((0, 8), (1, 16)))
    w_up = centred(key_list[12], (EXPERTS, D, FFE), D ** -0.5, 0.15625, ((0, 8), (1, 16)))
    w_down = centred(key_list[13], (EXPERTS, FFE, D), (FFE // 16) ** -0.5, 1.0, ((0, 8), (1, 16)))
    return {"tokens": tokens, "cotangent": cotangent, "seq_lengths": seq_lengths, "expert_ids": expert_ids, "w_query": w_query, "w_key": w_key, "w_value": w_value, "w_output": w_output, "norm_one": norm_one, "norm_two": norm_two, "w_router": w_router, "w_gate": w_gate, "w_up": w_up, "w_down": w_down}


@jax.custom_vjp
def low(v):
    return lax.optimization_barrier(v.astype(jnp.bfloat16)).astype(jnp.float32)

@jax.custom_vjp
def low_back(v):
    return v

def low_keep(v):
    return (low(v), None)

def low_pass(kept, grad):
    return (grad,)

def back_keep(v):
    return (v, None)

def back_low(kept, grad):
    return (low(grad),)
low.defvjp(low_keep, low_pass)
low_back.defvjp(back_keep, back_low)
epsilon = 1e-06
rope_base = 10000.0
highest = lax.Precision.HIGHEST

def matmul(left_side, right_side):
    return jnp.dot(left_side, right_side, precision=highest, preferred_element_type=jnp.float32)

def rms_scale(values):
    return lax.rsqrt(lax.optimization_barrier(jnp.mean(values * values, axis=-1, keepdims=True)) + epsilon)

def rope_tables(offsets, head_width):
    exponent = jnp.arange(head_width // 2, dtype=jnp.float32) * (2.0 / head_width)
    frequency = jnp.exp(-exponent * math.log(rope_base))
    phase_angles = offsets.astype(jnp.float32)[:, None] * frequency[None, :]
    return (jnp.cos(phase_angles)[:, None, :], jnp.sin(phase_angles)[:, None, :])

def rotate(values, cosine, sine_table):
    half_width = values.shape[-1] // 2
    first_half = values[..., :half_width]
    second_half = values[..., half_width:]
    return jnp.concatenate([first_half * cosine - second_half * sine_table, second_half * cosine + first_half * sine_table], axis=-1)

def layout(lengths, group_count):
    seq_ends = jnp.cumsum(lengths)
    starts = seq_ends - lengths
    places = jnp.arange(group_count, dtype=jnp.int32)
    member = ((places[:, None] >= starts[None, :]) & (places[:, None] < seq_ends[None, :])).astype(jnp.int32)
    numbers = jnp.arange(lengths.shape[0], dtype=jnp.int32)
    segment = lax.optimization_barrier(jnp.sum(member * numbers[None, :], axis=1))
    offsets = places - lax.optimization_barrier(jnp.sum(member * starts[None, :], axis=1))
    return (segment, offsets)

def slot_of(expert_rows, expert_count):
    flat_ids = expert_rows.reshape(-1)
    one_hot = (flat_ids[:, None] == jnp.arange(expert_count, dtype=jnp.int32)[None, :]).astype(jnp.int32)
    earlier = jnp.cumsum(one_hot, axis=0) - one_hot
    return lax.optimization_barrier(jnp.sum(earlier * one_hot, axis=1))

def group_forward(weights, group_block):
    w_query, w_key, w_value, w_output, gain_one, gain_two, w_router, w_gate, w_up, w_down = weights
    inputs, expert_ids, lengths = group_block
    group_count = inputs.shape[0]
    segment, offsets = layout(lengths, group_count)
    cosine, sine_table = rope_tables(offsets, HEAD)
    normed = low(inputs * rms_scale(inputs) * gain_one)
    query_raw = low_back(matmul(normed, w_query)).reshape(group_count, HEADS, HEAD)
    query_heads = low(rotate(query_raw, cosine, sine_table)).reshape(group_count, KV_HEADS, HEADS // KV_HEADS, HEAD)
    key_raw = low_back(matmul(normed, w_key)).reshape(group_count, KV_HEADS, HEAD)
    key_heads = low(rotate(key_raw, cosine, sine_table))
    value_heads = low_back(low(matmul(normed, w_value))).reshape(group_count, KV_HEADS, HEAD)
    scores = low_back(jnp.einsum('qgrh,kgh->grqk', query_heads, key_heads, precision=highest) * HEAD ** (-0.5))
    places = jnp.arange(group_count, dtype=jnp.int32)
    allowed = (segment[:, None] == segment[None, :]) & (places[None, :] <= places[:, None])
    scores = jnp.where(allowed, scores, -1e+30)
    probabilities = low(jax.nn.softmax(scores, axis=-1))
    attended = jnp.einsum('grqk,kgh->qgrh', probabilities, value_heads, precision=highest).reshape(group_count, HEADS * HEAD)
    attended = low(low_back(attended))
    middle = inputs + low_back(matmul(attended, w_output))
    normed_two = low(middle * rms_scale(middle) * gain_two)
    logits = low_back(matmul(normed_two, w_router))
    gate_values = jax.nn.softmax(jnp.take_along_axis(logits, expert_ids, axis=1), axis=-1)
    blocks = group_count // TOK_DEV
    slot_index = jax.vmap(partial(slot_of, expert_count=EXPERTS))(expert_ids.reshape(blocks, TOK_DEV, TOP)).reshape(group_count, TOP)
    column = (places // TOK_DEV)[:, None] * CAP + slot_index
    token_rows = low_back(jnp.broadcast_to(normed_two[:, None, :], (group_count, TOP, D)))
    buffer = jnp.zeros((EXPERTS, blocks * CAP, D), jnp.float32).at[expert_ids, column].set(token_rows)
    gate_act = low_back(jnp.einsum('ecd,edf->ecf', buffer, w_gate, precision=highest))
    up_act = low_back(jnp.einsum('ecd,edf->ecf', buffer, w_up, precision=highest))
    hidden = low(jax.nn.silu(gate_act) * up_act)
    expert_out = low_back(low(jnp.einsum('ecf,efd->ecd', hidden, w_down, precision=highest)))
    returned = expert_out[expert_ids, column]
    return middle + lax.optimization_barrier(jnp.sum(gate_values[:, :, None] * returned, axis=1))

def reference(tokens, cotangent, seq_lengths, expert_ids, w_query, w_key, w_value, w_output, norm_one, norm_two, w_router, w_gate, w_up, w_down):
    weights = tuple((weight.astype(jnp.float32) for weight in (w_query, w_key, w_value, w_output, norm_one, norm_two, w_router, w_gate, w_up, w_down)))
    inputs = tokens.astype(jnp.float32).reshape(N_DP, GROUP, D)
    grouped_ids = expert_ids.reshape(N_DP, GROUP, TOP)

    def forward(group_inputs, all_weights):

        def one_group(group_block):
            return jax.checkpoint(group_forward)(all_weights, group_block)
        return lax.map(one_group, (group_inputs, grouped_ids, seq_lengths))
    output, pullback = jax.vjp(forward, inputs, weights)
    grad_inputs, grad_weights = pullback(cotangent.astype(jnp.float32).reshape(N_DP, GROUP, D))
    grad_query, grad_key, grad_value, grad_output, grad_gain_one, grad_gain_two, grad_router, grad_gate, grad_up, grad_down = grad_weights
    return (output.reshape(TOKENS, D).astype(jnp.bfloat16), grad_inputs.reshape(TOKENS, D), grad_query, grad_key, grad_value, grad_output, grad_gain_one, grad_gain_two, grad_router, grad_gate, grad_up, grad_down)
```

```python
import math

import jax
import jax.numpy as jnp
from jax import lax
from jax.experimental import pallas as pl
from jax.experimental.pallas import tpu as pltpu
from jax.sharding import PartitionSpec as P

HEADS = 24
KV_HEADS = 8
HEAD = 64
DIM = 1536
FFE = 512
EXPERTS = 40
LOCAL = 5
CAP = 32
TOK = 128
PEERS = 8
DP = 16
GROUP = TOK * PEERS
REP = HEADS // KV_HEADS
SLICE = 384
QS = REP * HEAD
ROWS = 96

epsilon = 1e-06
rope_base = 10000.0
masked_score = -1e30
MESH = pl.DeviceIdType.MESH
BF = jnp.bfloat16
F32 = jnp.float32

RELATIVE = ((2, 1), (2, 0), (1, 1), (3, 1), (0, 1), (1, 0), (3, 0))
SLOTS = ((0, 0), (1, 0), (0, 1), (0, 3), (1, 1), (1, 3), (0, 2), (1, 2))


def expert_peers():
    me = lax.axis_index("expert")
    z, x = me // 2, me % 2
    return me, [(z + rz) % 4 * 2 + (x + rx) % 2 for rz, rx in RELATIVE]


def dp_place():
    d = lax.axis_index("dp")
    return d // 8, (d // 2) % 4, d % 2


def dp_index(x, y, core):
    return (x % 2 * 4 + y % 4) * 2 + core % 2


def signal_all(expert_ids, dp_ids):
    barrier = pltpu.get_barrier_semaphore()
    for p in expert_ids:
        pl.semaphore_signal(barrier, inc=1, device_id={"expert": p}, device_id_type=MESH)
    for p in dp_ids:
        pl.semaphore_signal(barrier, inc=1, device_id={"dp": p}, device_id_type=MESH)
    pl.semaphore_wait(barrier, len(expert_ids) + len(dp_ids))


def any_specs(count):
    return [pl.BlockSpec(memory_space=pl.ANY)] * count


def expert_copies(ins, outs, modes, send, recv):
    me, peers = expert_peers()
    copies = []
    for r, p in enumerate(peers):
        for i, mode in enumerate(modes):
            copies.append(
                pltpu.make_async_remote_copy(
                    src_ref=ins[i] if mode == "gather" else ins[i].at[p],
                    dst_ref=outs[i].at[me],
                    send_sem=send.at[i, r],
                    recv_sem=recv.at[i, r],
                    device_id={"expert": p},
                    device_id_type=MESH,
                )
            )
    return copies


def own_copies(ins, outs, modes, sems):
    me = lax.axis_index("expert")
    return [
        pltpu.make_async_copy(
            ins[i] if mode == "gather" else ins[i].at[me], outs[i].at[me], sems.at[i]
        )
        for i, mode in enumerate(modes)
    ]


def exchange(arrays, modes, cid):
    n = len(arrays)

    def kernel(*refs):
        ins, outs = refs[:n], refs[n : 2 * n]
        send, recv, local = refs[2 * n :]
        _, peers = expert_peers()
        signal_all(peers, [])
        copies = expert_copies(ins, outs, modes, send, recv) + own_copies(ins, outs, modes, local)
        for c in copies:
            c.start()
        for c in copies:
            c.wait()

    shapes = [
        jax.ShapeDtypeStruct(((PEERS,) + a.shape) if m == "gather" else a.shape, a.dtype)
        for a, m in zip(arrays, modes)
    ]
    return pl.pallas_call(
        kernel,
        out_shape=shapes,
        in_specs=any_specs(n),
        out_specs=any_specs(n),
        scratch_shapes=[
            pltpu.SemaphoreType.DMA((n, 7)),
            pltpu.SemaphoreType.DMA((n, 7)),
            pltpu.SemaphoreType.DMA((n,)),
        ],
        compiler_params=pltpu.CompilerParams(collective_id=cid, has_side_effects=True),
    )(*arrays)


def gather_start(dense, arrays, modes, cid):
    m, n = len(dense), len(arrays)

    def kernel(*refs):
        dins, ins = refs[:m], refs[m : m + n]
        douts, outs = refs[m + n : 2 * m + n], refs[2 * m + n : 2 * (m + n)]
        dsend, drecv, dlocal, send, recv, local = refs[2 * (m + n) :]
        x, y, core = dp_place()
        mine = dp_index(x, y, core)
        to_x, to_up, to_down, to_core = (
            dp_index(x + 1, y, core),
            dp_index(x, y + 1, core),
            dp_index(x, y + 3, core),
            dp_index(x, y, core + 1),
        )
        _, peers = expert_peers()
        signal_all(peers, [to_x, to_up, to_down, to_core])

        def move(i, k, slot, target, src=None):
            return pltpu.make_async_remote_copy(
                src_ref=douts[i].at[slot] if src is None else src,
                dst_ref=douts[i].at[slot],
                send_sem=dsend.at[i, k],
                recv_sem=drecv.at[i, k],
                device_id={"dp": target},
                device_id_type=MESH,
            )

        def arrived(i, k, slot):
            move(i, k, slot, to_x).wait_recv()

        started = []

        def go(c):
            c.start()
            started.append(c)

        sibling = [dp_index(x + rx, y + ry, core) for rx, ry in SLOTS]
        locals_ = []
        for i in range(m):
            c = pltpu.make_async_copy(dins[i], douts[i].at[mine], dlocal.at[i])
            c.start()
            locals_.append(c)
            go(move(i, 0, mine, to_x, dins[i]))
            go(move(i, 1, mine, to_up, dins[i]))
            go(move(i, 2, mine, to_down, dins[i]))
            go(move(i, 7, mine, to_core, dins[i]))
        more = expert_copies(ins, outs, modes, send, recv) + own_copies(ins, outs, modes, local)
        for c in more:
            c.start()
        for i in range(m):
            arrived(i, 0, sibling[1])
            go(move(i, 3, sibling[1], to_up))
            go(move(i, 4, sibling[1], to_down))
            go(move(i, 8, sibling[1], to_core))
            arrived(i, 1, sibling[3])
            go(move(i, 5, sibling[3], to_up))
            go(move(i, 10, sibling[3], to_core))
            arrived(i, 2, sibling[2])
            go(move(i, 9, sibling[2], to_core))
        for i in range(m):
            arrived(i, 4, sibling[4])
            go(move(i, 6, sibling[4], to_down))
            go(move(i, 11, sibling[4], to_core))
            arrived(i, 3, sibling[5])
            go(move(i, 12, sibling[5], to_core))
        for i in range(m):
            arrived(i, 5, sibling[6])
            go(move(i, 13, sibling[6], to_core))
            arrived(i, 6, sibling[7])
            go(move(i, 14, sibling[7], to_core))
        for i in range(m):
            for k in range(8):
                rx, ry = SLOTS[k]
                arrived(i, 7 + k, dp_index(x + rx, y + ry, core + 1))
        for c in started:
            c.wait_send()
        for c in more + locals_:
            c.wait()

    shapes = [jax.ShapeDtypeStruct((DP,) + a.shape, a.dtype) for a in dense] + [
        jax.ShapeDtypeStruct(((PEERS,) + a.shape) if k == "gather" else a.shape, a.dtype)
        for a, k in zip(arrays, modes)
    ]
    return pl.pallas_call(
        kernel,
        out_shape=shapes,
        in_specs=any_specs(m + n),
        out_specs=any_specs(m + n),
        scratch_shapes=[
            pltpu.SemaphoreType.DMA((m, 15)),
            pltpu.SemaphoreType.DMA((m, 15)),
            pltpu.SemaphoreType.DMA((m,)),
            pltpu.SemaphoreType.DMA((n, 7)),
            pltpu.SemaphoreType.DMA((n, 7)),
            pltpu.SemaphoreType.DMA((n,)),
        ],
        compiler_params=pltpu.CompilerParams(collective_id=cid, has_side_effects=True),
    )(*dense, *arrays)


def exchange_and_share(arrays, modes, pieces, cid):
    n, m = len(arrays), len(pieces)

    def kernel(*refs):
        ins, parts = refs[:n], refs[n : n + m]
        outs, shared = refs[n + m : 2 * n + m], refs[2 * n + m]
        send, recv, local, csend, crecv = refs[2 * n + m + 1 :]
        x, y, core = dp_place()
        other = dp_index(x, y, core + 1)
        _, peers = expert_peers()
        signal_all(peers, [other])
        copies = expert_copies(ins, outs, modes, send, recv) + own_copies(ins, outs, modes, local)
        for k in range(m):
            copies.append(
                pltpu.make_async_remote_copy(
                    src_ref=parts[k],
                    dst_ref=shared.at[k],
                    send_sem=csend.at[k],
                    recv_sem=crecv.at[k],
                    device_id={"dp": other},
                    device_id_type=MESH,
                )
            )
        for c in copies:
            c.start()
        for c in copies:
            c.wait()

    shapes = [
        jax.ShapeDtypeStruct(((PEERS,) + a.shape) if k == "gather" else a.shape, a.dtype)
        for a, k in zip(arrays, modes)
    ] + [jax.ShapeDtypeStruct((m,) + pieces[0].shape, pieces[0].dtype)]
    return pl.pallas_call(
        kernel,
        out_shape=shapes,
        in_specs=any_specs(n + m),
        out_specs=any_specs(n + 1),
        scratch_shapes=[
            pltpu.SemaphoreType.DMA((n, 7)),
            pltpu.SemaphoreType.DMA((n, 7)),
            pltpu.SemaphoreType.DMA((n,)),
            pltpu.SemaphoreType.DMA((m,)),
            pltpu.SemaphoreType.DMA((m,)),
        ],
        compiler_params=pltpu.CompilerParams(collective_id=cid, has_side_effects=True),
    )(*arrays, *pieces)


def scatter_sum(arrays, dense, cid):
    n = len(arrays)
    _, rows, cols = dense.shape

    def kernel(*refs):
        ins, dref = refs[:n], refs[n]
        outs, total = refs[n + 1 : 2 * n + 1], refs[2 * n + 1]
        send, recv, local, mine, theirs, summed, got, lsem, csend, crecv, dsend, drecv = refs[
            2 * n + 2 :
        ]
        x, y, core = dp_place()
        to_core = dp_index(x, y, core + 1)
        targets = [dp_index(x + rx, y + ry, core) for rx, ry in SLOTS[1:]]
        _, peers = expert_peers()
        signal_all(peers, [to_core] + targets)
        modes = ["exchange"] * n
        loads, shares = [], []
        for k, (rx, ry) in enumerate(SLOTS):
            c = pltpu.make_async_remote_copy(
                src_ref=dref.at[dp_index(x + rx, y + ry, core + 1)],
                dst_ref=theirs.at[k],
                send_sem=csend.at[k],
                recv_sem=crecv.at[k],
                device_id={"dp": to_core},
                device_id_type=MESH,
            )
            c.start()
            shares.append(c)
            c = pltpu.make_async_copy(
                dref.at[dp_index(x + rx, y + ry, core)], mine.at[k], lsem.at[k]
            )
            c.start()
            loads.append(c)
        copies = expert_copies(ins, outs, modes, send, recv) + own_copies(ins, outs, modes, local)
        for c in copies:
            c.start()
        moves = []
        for k in range(8):
            loads[k].wait()
            shares[k].wait_recv()
            summed[k] = (mine[k].astype(F32) + theirs[k].astype(F32)).astype(BF)
            if k > 0:
                c = pltpu.make_async_remote_copy(
                    src_ref=summed.at[k],
                    dst_ref=got.at[k - 1],
                    send_sem=dsend.at[k - 1],
                    recv_sem=drecv.at[k - 1],
                    device_id={"dp": targets[k - 1]},
                    device_id_type=MESH,
                )
                c.start()
                moves.append(c)
        acc = summed[0].astype(F32)
        for k, c in enumerate(moves):
            c.wait_recv()
            acc = acc + got[k].astype(F32)
        total[...] = acc
        for c in moves:
            c.wait_send()
        for c in shares:
            c.wait_send()
        for c in copies:
            c.wait()

    shapes = [jax.ShapeDtypeStruct(a.shape, a.dtype) for a in arrays] + [
        jax.ShapeDtypeStruct((rows, cols), F32)
    ]
    return pl.pallas_call(
        kernel,
        out_shape=shapes,
        in_specs=any_specs(n + 1),
        out_specs=any_specs(n) + [pl.BlockSpec(memory_space=pltpu.VMEM)],
        scratch_shapes=[
            pltpu.SemaphoreType.DMA((n, 7)),
            pltpu.SemaphoreType.DMA((n, 7)),
            pltpu.SemaphoreType.DMA((n,)),
            pltpu.VMEM((8, rows, cols), BF),
            pltpu.VMEM((8, rows, cols), BF),
            pltpu.VMEM((8, rows, cols), BF),
            pltpu.VMEM((7, rows, cols), BF),
            pltpu.SemaphoreType.DMA((8,)),
            pltpu.SemaphoreType.DMA((8,)),
            pltpu.SemaphoreType.DMA((8,)),
            pltpu.SemaphoreType.DMA((7,)),
            pltpu.SemaphoreType.DMA((7,)),
        ],
        compiler_params=pltpu.CompilerParams(
            collective_id=cid, has_side_effects=True, vmem_limit_bytes=40 << 20
        ),
    )(*arrays, dense)


def dot(a, b, contract):
    return lax.dot_general(a, b, ((contract[0], contract[1]), ((), ())), preferred_element_type=F32)


def experts_kernel(*refs):
    (rows_ref, cot_ref, slot_ref, gate_ref), refs = refs[:4], refs[4:]
    pieces, shared, refs = refs[:8], refs[8], refs[9:]
    (out_ref, back_ref, inner_ref, keep_ref, give_ref), refs = refs[:5], refs[5:]
    xg, cg, weights, grads, gates, inners, wsem, gsem = refs
    x, y, core = dp_place()

    def loads(e, b):
        copies = []
        for k, (rx, ry) in enumerate(SLOTS):
            for c in range(2):
                src = pieces[k].at[e] if c == 0 else shared.at[k, e]
                copies.append(
                    pltpu.make_async_copy(
                        src,
                        weights.at[b, dp_index(x + rx, y + ry, core + c)],
                        wsem.at[b, 2 * k + c],
                    )
                )
        return copies

    def stores(e, b):
        copies = []
        for k, (rx, ry) in enumerate(SLOTS):
            for c in range(2):
                dst = keep_ref.at[k, e] if c == 0 else give_ref.at[k, e]
                copies.append(
                    pltpu.make_async_copy(
                        grads.at[b, dp_index(x + rx, y + ry, core + c)],
                        dst,
                        gsem.at[b, 2 * k + c],
                    )
                )
        return copies

    for c in loads(0, 0):
        c.start()

    def onehot(b):
        places = lax.broadcasted_iota(jnp.int32, (CAP, TOK), 0).astype(F32)
        return [(places == slot_ref[b, e : e + 1, :]) for e in range(LOCAL)]

    def collect(b, _):
        hot = onehot(b)
        pick = jnp.concatenate([h.astype(F32) for h in hot], axis=0).astype(BF)
        xg[b] = dot(pick, rows_ref[b], ((1,), (0,))).astype(BF)
        cg[b] = dot(pick, cot_ref[b], ((1,), (0,))).astype(BF)
        for e in range(LOCAL):
            g = jnp.sum(jnp.where(hot[e], gate_ref[b, e : e + 1, :], 0.0), axis=1, keepdims=True)
            gates[e, pl.ds(b * CAP, CAP), :] = jnp.broadcast_to(g, (CAP, 128))
        return _

    lax.fori_loop(0, PEERS, collect, 0)

    def expert(e, _):
        b = lax.rem(e, 2)
        for c in loads(e, b):
            c.wait()

        @pl.when(e + 1 < LOCAL)
        def _next():
            for c in loads(e + 1, 1 - b):
                c.start()

        @pl.when(e >= 2)
        def _free():
            for c in stores(e - 2, b):
                c.wait()

        span = pl.ds(pl.multiple_of(e * CAP, CAP), CAP)
        rows = xg[:, span, :].reshape(PEERS * CAP, DIM)
        cot = cg[:, span, :].reshape(PEERS * CAP, DIM)
        gate = gates[e][:, :1]
        w_gate = weights[b, :, 0:96, :].reshape(DIM, FFE)
        gate_act = dot(rows, w_gate, ((1,), (0,)))
        w_up = weights[b, :, 96:192, :].reshape(DIM, FFE)
        up_act = dot(rows, w_up, ((1,), (0,)))
        sig = 1.0 / (1.0 + jnp.exp(-gate_act))
        silu = gate_act * sig
        hidden = (silu * up_act).astype(BF)
        grad_out = (cot.astype(F32) * gate).astype(BF)
        inner = jnp.zeros((PEERS * CAP, 1), F32)
        grad_hidden = jnp.zeros((PEERS * CAP, FFE), F32)
        gated = []
        for k in range(3):
            lanes = slice(k * FFE, (k + 1) * FFE)
            w_down = weights[b, :, 192 + 32 * k : 224 + 32 * k, :].reshape(FFE, FFE)
            part = dot(hidden, w_down, ((1,), (0,))).astype(BF).astype(F32)
            inner = inner + jnp.sum(part * cot[:, lanes].astype(F32), axis=1, keepdims=True)
            gated.append((part * gate).astype(BF))
            grad_hidden = grad_hidden + dot(grad_out[:, lanes], w_down, ((1,), (1,)))
            grads[b, :, 192 + 32 * k : 224 + 32 * k, :] = (
                dot(hidden, grad_out[:, lanes], ((0,), (0,))).astype(BF).reshape(DP, 32, FFE)
            )
        inners[e] = jnp.broadcast_to(inner, (PEERS * CAP, 128))
        grad_gate = (grad_hidden * up_act * sig * (1.0 + gate_act * (1.0 - sig))).astype(BF)
        grad_up = (grad_hidden * silu).astype(BF)
        grads[b, :, 0:96, :] = (
            dot(rows, grad_gate, ((0,), (0,))).astype(BF).reshape(DP, ROWS, FFE)
        )
        grads[b, :, 96:192, :] = (
            dot(rows, grad_up, ((0,), (0,))).astype(BF).reshape(DP, ROWS, FFE)
        )
        for c in stores(e, b):
            c.start()
        back = dot(grad_gate, w_gate, ((1,), (1,))) + dot(grad_up, w_up, ((1,), (1,)))
        xg[:, span, :] = back.astype(BF).reshape(PEERS, CAP, DIM)
        for k in range(3):
            cg[:, span, k * FFE : (k + 1) * FFE] = gated[k].reshape(PEERS, CAP, FFE)
        return _

    lax.fori_loop(0, LOCAL, expert, 0)

    def combine(b, _):
        hot = onehot(b)
        pick = jnp.concatenate([h.astype(F32) for h in hot], axis=0).astype(BF)
        out_ref[b] = dot(pick, cg[b], ((0,), (0,))).astype(BF)
        back_ref[b] = dot(pick, xg[b], ((0,), (0,))).astype(BF)
        lines = []
        for e in range(LOCAL):
            value = inners[e, pl.ds(b * CAP, CAP), :][:, :1]
            lines.append(jnp.sum(jnp.where(hot[e], value, 0.0), axis=0, keepdims=True))
        inner_ref[b] = jnp.concatenate(lines + [jnp.zeros((8 - LOCAL, TOK), F32)], axis=0)
        return _

    lax.fori_loop(0, PEERS, combine, 0)
    for e in (LOCAL - 2, LOCAL - 1):
        for c in stores(e, e % 2):
            c.wait()


def run_experts(rows, cot, slots, gates, pieces, shared):
    vmem = pl.BlockSpec(memory_space=pltpu.VMEM)
    piece = (LOCAL, 3 * ROWS, FFE)
    return pl.pallas_call(
        experts_kernel,
        out_shape=[
            jax.ShapeDtypeStruct((PEERS, TOK, DIM), BF),
            jax.ShapeDtypeStruct((PEERS, TOK, DIM), BF),
            jax.ShapeDtypeStruct((PEERS, 8, TOK), F32),
            jax.ShapeDtypeStruct((8,) + piece, BF),
            jax.ShapeDtypeStruct((8,) + piece, BF),
        ],
        in_specs=[vmem] * 4 + any_specs(9),
        out_specs=[vmem] * 3 + any_specs(2),
        scratch_shapes=[
            pltpu.VMEM((PEERS, LOCAL * CAP, DIM), BF),
            pltpu.VMEM((PEERS, LOCAL * CAP, DIM), BF),
            pltpu.VMEM((2, DP, 3 * ROWS, FFE), BF),
            pltpu.VMEM((2, DP, 3 * ROWS, FFE), BF),
            pltpu.VMEM((LOCAL, PEERS * CAP, 128), F32),
            pltpu.VMEM((LOCAL, PEERS * CAP, 128), F32),
            pltpu.SemaphoreType.DMA((2, 16)),
            pltpu.SemaphoreType.DMA((2, 16)),
        ],
        compiler_params=pltpu.CompilerParams(vmem_limit_bytes=60 << 20),
        cost_estimate=pl.CostEstimate(
            flops=20_000_000_000, bytes_accessed=60_000_000, transcendentals=700_000
        ),
    )(rows, cot, slots, gates, *pieces, shared)


def shift(value, move):
    pairs = []
    for d in range(DP):
        x, y, core = move(d // 8, d // 2 % 4, d % 2)
        pairs.append((d, (x % 2 * 4 + y % 4) * 2 + core % 2))
    return lax.ppermute(value, "dp", pairs)


def up(value):
    return shift(value, lambda x, y, c: (x, y + 1, c))


def down(value):
    return shift(value, lambda x, y, c: (x, y + 3, c))


def across(value):
    return shift(value, lambda x, y, c: (x + 1, y, c))


def other_core(value):
    return shift(value, lambda x, y, c: (x, y, c + 1))


def add(a, b):
    return (a.astype(F32) + b.astype(F32)).astype(BF)


def rms_scale(values):
    return lax.rsqrt(jnp.mean(values * values, axis=-1, keepdims=True) + epsilon)


def rope_tables(offsets, head_width):
    exponent = jnp.arange(head_width // 2, dtype=jnp.float32) * (2.0 / head_width)
    frequency = jnp.exp(-exponent * math.log(rope_base))
    phase_angles = offsets.astype(jnp.float32)[:, None] * frequency[None, :]
    return (jnp.cos(phase_angles)[:, None, :], jnp.sin(phase_angles)[:, None, :])


def rotate(values, cosine, sine_table):
    half = values.shape[-1] // 2
    first, second = values[..., :half], values[..., half:]
    return jnp.concatenate(
        [first * cosine - second * sine_table, second * cosine + first * sine_table], axis=-1
    )


def layout(lengths, group_count):
    seq_ends = jnp.cumsum(lengths)
    starts = seq_ends - lengths
    places = jnp.arange(group_count, dtype=jnp.int32)
    member = ((places[:, None] >= starts[None, :]) & (places[:, None] < seq_ends[None, :])).astype(
        jnp.int32
    )
    numbers = jnp.arange(lengths.shape[0], dtype=jnp.int32)
    segment = jnp.sum(member * numbers[None, :], axis=1)
    offsets = places - jnp.sum(member * starts[None, :], axis=1)
    return (segment, offsets)


def norm_back(values, row_scale, gain_vector, grad_normed):
    weighted = grad_normed * gain_vector
    return row_scale * weighted - values * row_scale**3 * jnp.mean(
        weighted * values, axis=-1, keepdims=True
    )


def by_peer(table):
    return jnp.pad(table.reshape(PEERS, LOCAL, TOK), ((0, 0), (0, 8 - LOCAL), (0, 0)))


def local(
    tokens,
    cotangent,
    seq_lengths,
    expert_ids,
    w_query,
    w_key,
    w_value,
    w_output,
    norm_one,
    norm_two,
    w_router,
    w_gate,
    w_up,
    w_down,
):
    score_scale = HEAD ** (-0.5)
    down_piece = w_down.reshape(LOCAL, 32, 3, FFE).transpose(0, 2, 1, 3).reshape(LOCAL, ROWS, FFE)
    piece = jnp.concatenate([w_gate, w_up, down_piece], axis=1)

    slices = jnp.concatenate(
        [
            w_query.reshape(12, PEERS, QS).transpose(1, 0, 2),
            w_key.reshape(12, PEERS, HEAD).transpose(1, 0, 2),
            w_value.reshape(12, PEERS, HEAD).transpose(1, 0, 2),
            jnp.broadcast_to(
                jnp.concatenate(
                    [
                        norm_one[:, None],
                        norm_two[:, None],
                        w_router,
                        jnp.zeros((12, SLICE - QS - 2 * HEAD - 2 - EXPERTS), BF),
                    ],
                    axis=1,
                )[None],
                (PEERS, 12, SLICE - QS - 2 * HEAD),
            ),
        ],
        axis=2,
    )
    slices_rows, output_rows = exchange([slices, w_output], ["exchange", "gather"], 1)
    slices_rows = slices_rows.reshape(ROWS, SLICE)
    output_rows = output_rows.reshape(ROWS, DIM)

    member = jnp.any(
        expert_ids[None, :, :] == jnp.arange(EXPERTS, dtype=jnp.int32)[:, None, None], axis=-1
    )
    before = jnp.arange(TOK)[:, None] < jnp.arange(TOK)[None, :]
    places = jnp.dot(member.astype(BF), before.astype(BF), preferred_element_type=F32)
    slot_table = by_peer(jnp.where(member, places, -1.0))

    slices_all, output_all, tokens_all, cot_all, slots_all = gather_start(
        [slices_rows, output_rows],
        [tokens, cotangent, slot_table],
        ["gather", "gather", "exchange"],
        2,
    )
    piece, _ = lax.optimization_barrier((piece, slots_all))
    x1 = across(piece)
    y3, y1 = up(piece), down(piece)
    x1y3, x1y1 = up(x1), down(x1)
    y2, x1y2 = up(y3), down(x1y1)
    pieces = [piece, x1, y1, y3, x1y1, x1y3, y2, x1y2]

    slices_all = slices_all.reshape(DIM, SLICE)
    output_all = output_all.reshape(DIM, DIM)
    qkv_all = slices_all[:, : QS + 2 * HEAD]
    gains = slices_all[:, QS + 2 * HEAD : QS + 2 * HEAD + 2].astype(F32).T
    gain_one, gain_two = gains[0], gains[1]
    router_all = slices_all[:, QS + 2 * HEAD + 2 : QS + 2 * HEAD + 2 + EXPERTS]

    segment, offsets = layout(seq_lengths[0], GROUP)
    cosine, sine_table = rope_tables(offsets, HEAD)
    places = jnp.arange(GROUP, dtype=jnp.int32)
    allowed = (segment[:, None] == segment[None, :]) & (places[None, :] <= places[:, None])

    inputs_all = tokens_all.reshape(GROUP, DIM).astype(F32)
    scale_all = rms_scale(inputs_all)
    normed_all = (inputs_all * scale_all * gain_one).astype(BF)
    qkv = jnp.dot(normed_all, qkv_all, preferred_element_type=F32)
    heads = rotate(
        qkv[:, : QS + HEAD].reshape(GROUP, REP + 1, HEAD), cosine, sine_table
    ).astype(BF)
    query, key = heads[:, :REP], heads[:, REP]
    value = qkv[:, QS + HEAD :].astype(BF)
    scores = jnp.einsum("qrh,kh->rqk", query, key, preferred_element_type=F32) * score_scale
    scores = jnp.where(allowed, scores, masked_score)
    highest = jnp.max(scores, axis=-1, keepdims=True)
    terms = jnp.exp(scores - highest)
    probs = terms / jnp.sum(terms, axis=-1, keepdims=True)
    probs_low = probs.astype(BF)
    attended = jnp.einsum("rqk,kh->qrh", probs_low, value, preferred_element_type=F32).astype(BF)
    (attended,) = exchange([attended.reshape(PEERS, TOK, QS)], ["exchange"], 3)
    attended = attended.transpose(1, 0, 2).reshape(TOK, DIM)

    inputs = tokens.astype(F32)
    middle = inputs + jnp.dot(attended, output_all, preferred_element_type=F32)
    scale_two = rms_scale(middle)
    normed_two = (middle * scale_two * gain_two).astype(BF)
    logits = lax.dot_general(
        router_all, normed_two, (((0,), (1,)), ((), ())), preferred_element_type=F32
    )
    chosen = jnp.where(member, logits, masked_score)
    weight = jnp.where(member, jnp.exp(chosen - jnp.max(chosen, axis=0, keepdims=True)), 0.0)
    gate_values = weight / jnp.sum(weight, axis=0, keepdims=True)

    rows_all, gates_all, shared = exchange_and_share(
        [normed_two, by_peer(gate_values)], ["gather", "exchange"], pieces, 4
    )
    out_part, back_part, inner_part, keep, give = run_experts(
        rows_all, cot_all, slots_all, gates_all, pieces, shared
    )

    given = other_core(give)
    sums = {s: add(keep[k], given[k]) for k, s in enumerate(SLOTS)}
    sums[(0, 1)] = add(sums[(0, 1)], up(sums[(0, 2)]))
    sums[(1, 3)] = add(sums[(1, 3)], down(sums[(1, 2)]))
    halves = [
        (
            sums[(r, 0)].astype(F32)
            + up(sums[(r, 1)]).astype(F32)
            + down(sums[(r, 3)]).astype(F32)
        )
        for r in (0, 1)
    ]
    expert_grads = halves[0] + across(halves[1].astype(BF)).astype(F32)

    back_all, inner_all = exchange([back_part, inner_part], ["exchange", "exchange"], 5)
    grad_normed_two = jnp.sum(back_all.astype(F32), axis=0)
    grad_gates = inner_all[:, :LOCAL, :].reshape(EXPERTS, TOK)
    grad_chosen = gate_values * (
        grad_gates - jnp.sum(gate_values * grad_gates, axis=0, keepdims=True)
    )
    grad_logits = grad_chosen.astype(BF)
    grad_out = cotangent.astype(F32)
    grad_router = lax.dot_general(
        normed_two, grad_logits, (((0,), (1,)), ((), ())), preferred_element_type=F32
    )
    grad_normed_two = grad_normed_two + lax.dot_general(
        grad_logits, router_all, (((0,), (1,)), ((), ())), preferred_element_type=F32
    )
    grad_gain_two = jnp.sum(grad_normed_two * middle * scale_two, axis=0)
    grad_middle = grad_out + norm_back(middle, scale_two, gain_two, grad_normed_two)
    grad_branch = grad_middle.astype(BF)
    grad_attended = lax.dot_general(
        grad_branch, output_all, (((1,), (1,)), ((), ())), preferred_element_type=F32
    ).astype(BF)
    grad_attended = grad_attended.reshape(TOK, PEERS, QS).transpose(1, 0, 2)
    (grad_attended,) = exchange([grad_attended], ["exchange"], 6)
    grad_attended = grad_attended.reshape(GROUP, REP, HEAD)
    grad_output = lax.dot_general(
        attended, grad_branch, (((0,), (0,)), ((), ())), preferred_element_type=F32
    )

    grad_probs = jnp.einsum("qrh,kh->rqk", grad_attended, value, preferred_element_type=F32)
    grad_scores = (
        probs * (grad_probs - jnp.sum(probs * grad_probs, axis=-1, keepdims=True))
    ).astype(BF)
    grad_query = (
        jnp.einsum("rqk,kh->qrh", grad_scores, key, preferred_element_type=F32) * score_scale
    )
    grad_key = (
        jnp.einsum("rqk,qrh->kh", grad_scores, query, preferred_element_type=F32) * score_scale
    )
    grad_value = jnp.einsum("rqk,qrh->kh", probs_low, grad_attended, preferred_element_type=F32)
    grad_heads = rotate(
        jnp.concatenate([grad_query, grad_key[:, None, :]], axis=1), cosine, -sine_table
    ).reshape(GROUP, QS + HEAD)
    grad_qkv = jnp.concatenate([grad_heads, grad_value], axis=1).astype(BF)
    grad_slices = lax.dot_general(
        normed_all, grad_qkv, (((0,), (0,)), ((), ())), preferred_element_type=F32
    )
    grad_normed = lax.dot_general(
        grad_qkv, qkv_all, (((1,), (1,)), ((), ())), preferred_element_type=F32
    )
    grad_gain_one = jnp.sum(grad_normed * inputs_all * scale_all, axis=0)
    dense = jnp.concatenate(
        [
            grad_slices,
            grad_gain_one[:, None],
            grad_gain_two[:, None],
            grad_router,
            jnp.zeros((DIM, SLICE - QS - 2 * HEAD - 2 - EXPERTS), F32),
            grad_output,
        ],
        axis=1,
    ).astype(BF)
    normed_back, out_all, dense_rows = scatter_sum(
        [grad_normed.astype(BF).reshape(PEERS, TOK, DIM), out_part],
        dense.reshape(DP, ROWS, SLICE + DIM),
        7,
    )
    mixed = middle + jnp.sum(out_all.astype(F32), axis=0)
    grad_tokens = grad_middle + norm_back(
        inputs, scale_all_own(scale_all), gain_one, jnp.sum(normed_back.astype(F32), axis=0)
    )
    (dense_own,) = exchange([dense_rows.reshape(PEERS, 12, SLICE + DIM)], ["exchange"], 8)
    own_sum = jnp.sum(dense_own[:, :, QS + 2 * HEAD :], axis=0)
    last = QS + 2 * HEAD
    return (
        mixed.astype(BF),
        grad_tokens,
        dense_own[:, :, :QS].transpose(1, 0, 2).reshape(12, DIM),
        dense_own[:, :, QS : QS + HEAD].transpose(1, 0, 2).reshape(12, KV_HEADS * HEAD),
        dense_own[:, :, QS + HEAD : last].transpose(1, 0, 2).reshape(12, KV_HEADS * HEAD),
        own_sum[:, SLICE - last :],
        own_sum[:, 0],
        own_sum[:, 1],
        own_sum[:, 2 : 2 + EXPERTS],
        expert_grads[:, :ROWS],
        expert_grads[:, ROWS : 2 * ROWS],
        expert_grads[:, 2 * ROWS :]
        .reshape(LOCAL, 3, 32, FFE)
        .transpose(0, 2, 1, 3)
        .reshape(LOCAL, 32, DIM),
    )


def scale_all_own(scale_all):
    return lax.dynamic_slice_in_dim(scale_all, lax.axis_index("expert") * TOK, TOK)


def solution(mesh):
    both = P(("dp", "expert"), None)
    line = P(("dp", "expert"))
    cube = P("expert", "dp", None)
    in_specs = (both, both, P("dp", None), both, both, both, both, both)
    in_specs = in_specs + (line, line, both, cube, cube, cube)
    out_specs = (both,) * 6 + (line, line, both, cube, cube, cube)
    return jax.shard_map(local, mesh=mesh, in_specs=in_specs, out_specs=out_specs, check_vma=False)
```

```python
import math

import jax
import jax.numpy as jnp
from jax import lax
from jax.experimental import pallas as pl
from jax.experimental.pallas import tpu as pltpu
from jax.sharding import PartitionSpec as P

HEADS = 24
KV_HEADS = 8
HEAD = 64
DIM = 1536
FFE = 512
EXPERTS = 40
LOCAL = 5
CAP = 32
TOK = 128
PEERS = 8
DP = 16
GROUP = TOK * PEERS
REP = HEADS // KV_HEADS
SLICE = 384
QS = REP * HEAD
ROWS = 96

epsilon = 1e-06
rope_base = 10000.0
masked_score = -1e30
MESH = pl.DeviceIdType.MESH
BF = jnp.bfloat16
F32 = jnp.float32

RELATIVE = ((2, 1), (2, 0), (1, 1), (3, 1), (0, 1), (1, 0), (3, 0))
SLOTS = ((0, 0), (1, 0), (0, 1), (0, 3), (1, 1), (1, 3), (0, 2), (1, 2))


def expert_peers():
    me = lax.axis_index("expert")
    z, x = me // 2, me % 2
    return me, [(z + rz) % 4 * 2 + (x + rx) % 2 for rz, rx in RELATIVE]


def dp_place():
    d = lax.axis_index("dp")
    return d // 8, (d // 2) % 4, d % 2


def dp_index(x, y, core):
    return (x % 2 * 4 + y % 4) * 2 + core % 2


def signal_all(expert_ids, dp_ids):
    barrier = pltpu.get_barrier_semaphore()
    for p in expert_ids:
        pl.semaphore_signal(barrier, inc=1, device_id={"expert": p}, device_id_type=MESH)
    for p in dp_ids:
        pl.semaphore_signal(barrier, inc=1, device_id={"dp": p}, device_id_type=MESH)
    pl.semaphore_wait(barrier, len(expert_ids) + len(dp_ids))


def any_specs(count):
    return [pl.BlockSpec(memory_space=pl.ANY)] * count


def expert_copies(ins, outs, modes, send, recv):
    me, peers = expert_peers()
    copies = []
    for r, p in enumerate(peers):
        for i, mode in enumerate(modes):
            copies.append(
                pltpu.make_async_remote_copy(
                    src_ref=ins[i] if mode == "gather" else ins[i].at[p],
                    dst_ref=outs[i].at[me],
                    send_sem=send.at[i, r],
                    recv_sem=recv.at[i, r],
                    device_id={"expert": p},
                    device_id_type=MESH,
                )
            )
    return copies


def own_copies(ins, outs, modes, sems):
    me = lax.axis_index("expert")
    return [
        pltpu.make_async_copy(
            ins[i] if mode == "gather" else ins[i].at[me], outs[i].at[me], sems.at[i]
        )
        for i, mode in enumerate(modes)
    ]


def lasting(us):
    return pl.CostEstimate(flops=us * 1_000_000_000, bytes_accessed=0, transcendentals=0)


def exchange(arrays, modes, cid, us=10):
    n = len(arrays)

    def kernel(*refs):
        ins, outs = refs[:n], refs[n : 2 * n]
        send, recv, local = refs[2 * n :]
        _, peers = expert_peers()
        signal_all(peers, [])
        copies = expert_copies(ins, outs, modes, send, recv) + own_copies(ins, outs, modes, local)
        for c in copies:
            c.start()
        for c in copies:
            c.wait()

    shapes = [
        jax.ShapeDtypeStruct(((PEERS,) + a.shape) if m == "gather" else a.shape, a.dtype)
        for a, m in zip(arrays, modes)
    ]
    return pl.pallas_call(
        kernel,
        out_shape=shapes,
        in_specs=any_specs(n),
        out_specs=any_specs(n),
        scratch_shapes=[
            pltpu.SemaphoreType.DMA((n, 7)),
            pltpu.SemaphoreType.DMA((n, 7)),
            pltpu.SemaphoreType.DMA((n,)),
        ],
        compiler_params=pltpu.CompilerParams(collective_id=cid, has_side_effects=True),
        cost_estimate=lasting(us),
    )(*arrays)


def gather_start(slices, output, arrays, modes, cid):
    n = len(arrays)
    small = (slices, output)
    widths = (slices.shape[-1], output.shape[-1])

    def kernel(*refs):
        sins, ins = refs[:2], refs[2 : 2 + n]
        douts, outs = refs[2 + n : 4 + n], refs[4 + n : 4 + 2 * n]
        pieces, rows = refs[4 + 2 * n : 6 + 2 * n], refs[6 + 2 * n : 8 + 2 * n]
        ssend, srecv, slocal, dsend, drecv, dlocal, send, recv, local = refs[8 + 2 * n :]
        x, y, core = dp_place()
        mine = dp_index(x, y, core)
        to_x, to_up, to_down, to_core = (
            dp_index(x + 1, y, core),
            dp_index(x, y + 1, core),
            dp_index(x, y + 3, core),
            dp_index(x, y, core + 1),
        )
        _, peers = expert_peers()
        signal_all(peers, [to_x, to_up, to_down, to_core])

        def move(i, k, slot, target, src=None):
            return pltpu.make_async_remote_copy(
                src_ref=douts[i].at[slot] if src is None else src,
                dst_ref=douts[i].at[slot],
                send_sem=dsend.at[i, k],
                recv_sem=drecv.at[i, k],
                device_id={"dp": target},
                device_id_type=MESH,
            )

        def arrived(i, k, slot):
            move(i, k, slot, to_x).wait_recv()

        started = []

        def go(c):
            c.start()
            started.append(c)

        sibling = [dp_index(x + rx, y + ry, core) for rx, ry in SLOTS]
        first = []
        for i, mode in enumerate(("exchange", "gather")):
            part = expert_copies(
                [sins[i]], [pieces[i]], [mode], ssend.at[pl.ds(i, 1)], srecv.at[pl.ds(i, 1)]
            ) + own_copies([sins[i]], [pieces[i]], [mode], slocal.at[pl.ds(i, 1)])
            for c in part:
                c.start()
            first.append(part)
        more = expert_copies(ins, outs, modes, send, recv) + own_copies(ins, outs, modes, local)
        for c in more:
            c.start()
        locals_ = []
        for i in range(2):
            for c in first[i]:
                c.wait()
            rows[i][...] = jnp.concatenate([pieces[i][j] for j in range(PEERS)], axis=0)
            c = pltpu.make_async_copy(rows[i], douts[i].at[mine], dlocal.at[i])
            c.start()
            locals_.append(c)
            go(move(i, 0, mine, to_x, rows[i]))
            go(move(i, 1, mine, to_up, rows[i]))
            go(move(i, 2, mine, to_down, rows[i]))
            go(move(i, 7, mine, to_core, rows[i]))
        for i in range(2):
            arrived(i, 0, sibling[1])
            go(move(i, 3, sibling[1], to_up))
            go(move(i, 4, sibling[1], to_down))
            go(move(i, 8, sibling[1], to_core))
            arrived(i, 1, sibling[3])
            go(move(i, 5, sibling[3], to_up))
            go(move(i, 10, sibling[3], to_core))
            arrived(i, 2, sibling[2])
            go(move(i, 9, sibling[2], to_core))
        for i in range(2):
            arrived(i, 4, sibling[4])
            go(move(i, 6, sibling[4], to_down))
            go(move(i, 11, sibling[4], to_core))
            arrived(i, 3, sibling[5])
            go(move(i, 12, sibling[5], to_core))
        for i in range(2):
            arrived(i, 5, sibling[6])
            go(move(i, 13, sibling[6], to_core))
            arrived(i, 6, sibling[7])
            go(move(i, 14, sibling[7], to_core))
        for i in range(2):
            for k in range(8):
                rx, ry = SLOTS[k]
                arrived(i, 7 + k, dp_index(x + rx, y + ry, core + 1))
        for c in started:
            c.wait_send()
        for c in more + locals_:
            c.wait()

    shapes = [jax.ShapeDtypeStruct((DP, ROWS, w), BF) for w in widths] + [
        jax.ShapeDtypeStruct(((PEERS,) + a.shape) if k == "gather" else a.shape, a.dtype)
        for a, k in zip(arrays, modes)
    ]
    return pl.pallas_call(
        kernel,
        out_shape=shapes,
        in_specs=any_specs(2 + n),
        out_specs=any_specs(2 + n),
        scratch_shapes=[pltpu.VMEM((PEERS, 12, w), BF) for w in widths]
        + [pltpu.VMEM((ROWS, w), BF) for w in widths]
        + [
            pltpu.SemaphoreType.DMA((2, 7)),
            pltpu.SemaphoreType.DMA((2, 7)),
            pltpu.SemaphoreType.DMA((2,)),
            pltpu.SemaphoreType.DMA((2, 15)),
            pltpu.SemaphoreType.DMA((2, 15)),
            pltpu.SemaphoreType.DMA((2,)),
            pltpu.SemaphoreType.DMA((n, 7)),
            pltpu.SemaphoreType.DMA((n, 7)),
            pltpu.SemaphoreType.DMA((n,)),
        ],
        compiler_params=pltpu.CompilerParams(collective_id=cid, has_side_effects=True),
        cost_estimate=lasting(45),
    )(*small, *arrays)


def exchange_and_share(arrays, modes, pieces, cid):
    n, m = len(arrays), len(pieces)

    def kernel(*refs):
        ins, parts = refs[:n], refs[n : n + m]
        outs, shared = refs[n + m : 2 * n + m], refs[2 * n + m]
        send, recv, local, csend, crecv = refs[2 * n + m + 1 :]
        x, y, core = dp_place()
        other = dp_index(x, y, core + 1)
        _, peers = expert_peers()
        signal_all(peers, [other])
        copies = expert_copies(ins, outs, modes, send, recv) + own_copies(ins, outs, modes, local)
        for k in range(m):
            copies.append(
                pltpu.make_async_remote_copy(
                    src_ref=parts[k],
                    dst_ref=shared.at[k],
                    send_sem=csend.at[k],
                    recv_sem=crecv.at[k],
                    device_id={"dp": other},
                    device_id_type=MESH,
                )
            )
        for c in copies:
            c.start()
        for c in copies:
            c.wait()

    shapes = [
        jax.ShapeDtypeStruct(((PEERS,) + a.shape) if k == "gather" else a.shape, a.dtype)
        for a, k in zip(arrays, modes)
    ] + [jax.ShapeDtypeStruct((m,) + pieces[0].shape, pieces[0].dtype)]
    return pl.pallas_call(
        kernel,
        out_shape=shapes,
        in_specs=any_specs(n + m),
        out_specs=any_specs(n + 1),
        scratch_shapes=[
            pltpu.SemaphoreType.DMA((n, 7)),
            pltpu.SemaphoreType.DMA((n, 7)),
            pltpu.SemaphoreType.DMA((n,)),
            pltpu.SemaphoreType.DMA((m,)),
            pltpu.SemaphoreType.DMA((m,)),
        ],
        compiler_params=pltpu.CompilerParams(collective_id=cid, has_side_effects=True),
        cost_estimate=lasting(38),
    )(*arrays, *pieces)


def scatter_sum(arrays, dense, cid):
    n, m = len(arrays), len(dense)
    shapes = [(d.shape[1], d.shape[2]) for d in dense]

    def kernel(*refs):
        ins, dins = refs[:n], refs[n : n + m]
        outs, totals = refs[n + m : 2 * n + m], refs[2 * n + m : 2 * (n + m)]
        refs = refs[2 * (n + m) :]
        mine, theirs, along, last = refs[:m], refs[m : 2 * m], refs[2 * m : 3 * m], refs[3 * m : 4 * m]
        send, recv, local, lsem, csend, crecv, ysend, yrecv, xsend, xrecv = refs[4 * m :]
        x, y, core = dp_place()
        to_core, to_x = dp_index(x, y, core + 1), dp_index(x + 1, y, core)
        to_y = [dp_index(x, y + r, core) for r in (1, 2, 3)]
        _, peers = expert_peers()
        signal_all(peers, [to_core, to_x] + to_y)
        modes = ["exchange"] * n
        order = [(r, s) for r in (1, 0) for s in (2, 1, 3, 0)]
        started, loads, shares = [], {}, {}

        def remote(src, dst, s, r, target):
            c = pltpu.make_async_remote_copy(
                src_ref=src,
                dst_ref=dst,
                send_sem=s,
                recv_sem=r,
                device_id={"dp": target},
                device_id_type=MESH,
            )
            c.start()
            started.append(c)
            return c

        for i in range(m):
            for r, s in order:
                k = 4 * r + s
                shares[i, k] = remote(
                    dins[i].at[dp_index(x + r, y + s, core + 1)],
                    theirs[i].at[k],
                    csend.at[i, k],
                    crecv.at[i, k],
                    to_core,
                )
                loads[i, k] = pltpu.make_async_copy(
                    dins[i].at[dp_index(x + r, y + s, core)], mine[i].at[k], lsem.at[i, k]
                )
                loads[i, k].start()
        copies = expert_copies(ins, outs, modes, send, recv) + own_copies(ins, outs, modes, local)
        for c in copies:
            c.start()
        moves = {}
        for r, s in order:
            k = 4 * r + s
            for i in range(m):
                loads[i, k].wait()
                shares[i, k].wait_recv()
                mine[i][k] = (mine[i][k].astype(F32) + theirs[i][k].astype(F32)).astype(BF)
                if s > 0:
                    moves[i, r, s] = remote(
                        mine[i].at[k],
                        along[i].at[3 * r + s - 1],
                        ysend.at[i, 3 * r + s - 1],
                        yrecv.at[i, 3 * r + s - 1],
                        to_y[s - 1],
                    )
        crossings = []
        for i in range(m):
            acc = mine[i][4].astype(F32)
            for s in (2, 1, 3):
                moves[i, 1, s].wait_recv()
                acc = acc + along[i][3 + s - 1].astype(F32)
            mine[i][4] = acc.astype(BF)
            crossings.append(remote(mine[i].at[4], last[i], xsend.at[i], xrecv.at[i], to_x))
        for i in range(m):
            acc = mine[i][0].astype(F32)
            for s in (2, 1, 3):
                moves[i, 0, s].wait_recv()
                acc = acc + along[i][s - 1].astype(F32)
            crossings[i].wait_recv()
            totals[i][...] = acc + last[i][...].astype(F32)
        for c in started:
            c.wait_send()
        for c in copies:
            c.wait()

    vmem = pl.BlockSpec(memory_space=pltpu.VMEM)
    return pl.pallas_call(
        kernel,
        out_shape=[jax.ShapeDtypeStruct(a.shape, a.dtype) for a in arrays]
        + [jax.ShapeDtypeStruct(d, F32) for d in shapes],
        in_specs=any_specs(n + m),
        out_specs=any_specs(n) + [vmem] * m,
        scratch_shapes=[pltpu.VMEM((8,) + d, BF) for d in shapes]
        + [pltpu.VMEM((8,) + d, BF) for d in shapes]
        + [pltpu.VMEM((6,) + d, BF) for d in shapes]
        + [pltpu.VMEM(d, BF) for d in shapes]
        + [
            pltpu.SemaphoreType.DMA((n, 7)),
            pltpu.SemaphoreType.DMA((n, 7)),
            pltpu.SemaphoreType.DMA((n,)),
            pltpu.SemaphoreType.DMA((m, 8)),
            pltpu.SemaphoreType.DMA((m, 8)),
            pltpu.SemaphoreType.DMA((m, 8)),
            pltpu.SemaphoreType.DMA((m, 6)),
            pltpu.SemaphoreType.DMA((m, 6)),
            pltpu.SemaphoreType.DMA((m,)),
            pltpu.SemaphoreType.DMA((m,)),
        ],
        compiler_params=pltpu.CompilerParams(
            collective_id=cid, has_side_effects=True, vmem_limit_bytes=40 << 20
        ),
        cost_estimate=lasting(45),
    )(*arrays, *dense)


def dot(a, b, contract):
    return lax.dot_general(a, b, ((contract[0], contract[1]), ((), ())), preferred_element_type=F32)


def experts_kernel(*refs):
    (rows_ref, cot_ref, slot_ref, gate_ref), refs = refs[:4], refs[4:]
    pieces, shared, late, refs = refs[:8], refs[8], refs[9:11], refs[11:]
    (out_ref, back_ref, inner_ref, keep_ref, given_ref), refs = refs[:5], refs[5:]
    xg, cg, weights, grads, gates, inners, wsem, gsem, rsem = refs
    x, y, core = dp_place()
    other = dp_index(x, y, core + 1)
    signal_all([], [other])

    def loads(e, b):
        copies = []
        for k, (rx, ry) in enumerate(SLOTS):
            for c in range(2):
                src = pieces[k].at[e] if c == 0 else shared.at[k, e] if k < 6 else late[k - 6].at[e]
                copies.append(
                    pltpu.make_async_copy(
                        src,
                        weights.at[b, dp_index(x + rx, y + ry, core + c)],
                        wsem.at[b, 2 * k + c],
                    )
                )
        return copies

    def kept(e, b):
        return [
            pltpu.make_async_copy(
                grads.at[b, dp_index(x + rx, y + ry, core)], keep_ref.at[k, e], gsem.at[b, k]
            )
            for k, (rx, ry) in enumerate(SLOTS)
        ]

    def given(e, b):
        return [
            pltpu.make_async_remote_copy(
                src_ref=grads.at[b, dp_index(x + rx, y + ry, core + 1)],
                dst_ref=given_ref.at[k, e],
                send_sem=gsem.at[b, 8 + k],
                recv_sem=rsem.at[e, k],
                device_id={"dp": other},
                device_id_type=MESH,
            )
            for k, (rx, ry) in enumerate(SLOTS)
        ]

    def stored(e, b):
        for c in kept(e, b):
            c.wait()
        for c in given(e, b):
            c.wait_send()

    for c in loads(0, 0):
        c.start()

    def onehot(b):
        places = lax.broadcasted_iota(jnp.int32, (CAP, TOK), 0).astype(F32)
        return [(places == slot_ref[b, e : e + 1, :]) for e in range(LOCAL)]

    def collect(b, _):
        hot = onehot(b)
        pick = jnp.concatenate([h.astype(F32) for h in hot], axis=0).astype(BF)
        xg[b] = dot(pick, rows_ref[b], ((1,), (0,))).astype(BF)
        cg[b] = dot(pick, cot_ref[b], ((1,), (0,))).astype(BF)
        for e in range(LOCAL):
            g = jnp.sum(jnp.where(hot[e], gate_ref[b, e : e + 1, :], 0.0), axis=1, keepdims=True)
            gates[e, pl.ds(b * CAP, CAP), :] = jnp.broadcast_to(g, (CAP, 128))
        return _

    lax.fori_loop(0, PEERS, collect, 0)

    def expert(e, _):
        b = lax.rem(e, 2)
        for c in loads(e, b):
            c.wait()

        @pl.when(e + 1 < LOCAL)
        def _next():
            for c in loads(e + 1, 1 - b):
                c.start()

        @pl.when(e >= 2)
        def _free():
            stored(e - 2, b)

        span = pl.ds(pl.multiple_of(e * CAP, CAP), CAP)
        rows = xg[:, span, :].reshape(PEERS * CAP, DIM)
        cot = cg[:, span, :].reshape(PEERS * CAP, DIM)
        gate = gates[e][:, :1]
        w_gate = weights[b, :, 0:96, :].reshape(DIM, FFE)
        gate_act = dot(rows, w_gate, ((1,), (0,)))
        w_up = weights[b, :, 96:192, :].reshape(DIM, FFE)
        up_act = dot(rows, w_up, ((1,), (0,)))
        sig = 1.0 / (1.0 + jnp.exp(-gate_act))
        silu = gate_act * sig
        hidden = (silu * up_act).astype(BF)
        grad_out = (cot.astype(F32) * gate).astype(BF)
        inner = jnp.zeros((PEERS * CAP, 1), F32)
        grad_hidden = jnp.zeros((PEERS * CAP, FFE), F32)
        gated = []
        for k in range(3):
            lanes = slice(k * FFE, (k + 1) * FFE)
            w_down = weights[b, :, 192 + 32 * k : 224 + 32 * k, :].reshape(FFE, FFE)
            part = dot(hidden, w_down, ((1,), (0,))).astype(BF).astype(F32)
            inner = inner + jnp.sum(part * cot[:, lanes].astype(F32), axis=1, keepdims=True)
            gated.append((part * gate).astype(BF))
            grad_hidden = grad_hidden + dot(grad_out[:, lanes], w_down, ((1,), (1,)))
            grads[b, :, 192 + 32 * k : 224 + 32 * k, :] = (
                dot(hidden, grad_out[:, lanes], ((0,), (0,))).astype(BF).reshape(DP, 32, FFE)
            )
        inners[e] = jnp.broadcast_to(inner, (PEERS * CAP, 128))
        grad_gate = (grad_hidden * up_act * sig * (1.0 + gate_act * (1.0 - sig))).astype(BF)
        grad_up = (grad_hidden * silu).astype(BF)
        grads[b, :, 0:96, :] = (
            dot(rows, grad_gate, ((0,), (0,))).astype(BF).reshape(DP, ROWS, FFE)
        )
        grads[b, :, 96:192, :] = (
            dot(rows, grad_up, ((0,), (0,))).astype(BF).reshape(DP, ROWS, FFE)
        )
        for c in kept(e, b) + given(e, b):
            c.start()
        back = dot(grad_gate, w_gate, ((1,), (1,))) + dot(grad_up, w_up, ((1,), (1,)))
        xg[:, span, :] = back.astype(BF).reshape(PEERS, CAP, DIM)
        for k in range(3):
            cg[:, span, k * FFE : (k + 1) * FFE] = gated[k].reshape(PEERS, CAP, FFE)
        return _

    lax.fori_loop(0, LOCAL, expert, 0)

    def combine(b, _):
        hot = onehot(b)
        pick = jnp.concatenate([h.astype(F32) for h in hot], axis=0).astype(BF)
        out_ref[b] = dot(pick, cg[b], ((0,), (0,))).astype(BF)
        back_ref[b] = dot(pick, xg[b], ((0,), (0,))).astype(BF)
        lines = []
        for e in range(LOCAL):
            value = inners[e, pl.ds(b * CAP, CAP), :][:, :1]
            lines.append(jnp.sum(jnp.where(hot[e], value, 0.0), axis=0, keepdims=True))
        inner_ref[b] = jnp.concatenate(lines + [jnp.zeros((8 - LOCAL, TOK), F32)], axis=0)
        return _

    lax.fori_loop(0, PEERS, combine, 0)
    for e in (LOCAL - 2, LOCAL - 1):
        stored(e, e % 2)
    for e in range(LOCAL):
        for c in given(e, e % 2):
            c.wait_recv()


def run_experts(rows, cot, slots, gates, pieces, shared, late):
    vmem = pl.BlockSpec(memory_space=pltpu.VMEM)
    piece = (LOCAL, 3 * ROWS, FFE)
    return pl.pallas_call(
        experts_kernel,
        out_shape=[
            jax.ShapeDtypeStruct((PEERS, TOK, DIM), BF),
            jax.ShapeDtypeStruct((PEERS, TOK, DIM), BF),
            jax.ShapeDtypeStruct((PEERS, 8, TOK), F32),
            jax.ShapeDtypeStruct((8,) + piece, BF),
            jax.ShapeDtypeStruct((8,) + piece, BF),
        ],
        in_specs=[vmem] * 4 + any_specs(11),
        out_specs=[vmem] * 3 + any_specs(2),
        scratch_shapes=[
            pltpu.VMEM((PEERS, LOCAL * CAP, DIM), BF),
            pltpu.VMEM((PEERS, LOCAL * CAP, DIM), BF),
            pltpu.VMEM((2, DP, 3 * ROWS, FFE), BF),
            pltpu.VMEM((2, DP, 3 * ROWS, FFE), BF),
            pltpu.VMEM((LOCAL, PEERS * CAP, 128), F32),
            pltpu.VMEM((LOCAL, PEERS * CAP, 128), F32),
            pltpu.SemaphoreType.DMA((2, 16)),
            pltpu.SemaphoreType.DMA((2, 16)),
            pltpu.SemaphoreType.DMA((LOCAL, 8)),
        ],
        compiler_params=pltpu.CompilerParams(
            collective_id=2, has_side_effects=True, vmem_limit_bytes=60 << 20
        ),
        cost_estimate=pl.CostEstimate(
            flops=20_000_000_000, bytes_accessed=60_000_000, transcendentals=700_000
        ),
    )(rows, cot, slots, gates, *pieces, shared, *late)


def shift(value, move):
    pairs = []
    for d in range(DP):
        x, y, core = move(d // 8, d // 2 % 4, d % 2)
        pairs.append((d, (x % 2 * 4 + y % 4) * 2 + core % 2))
    return lax.ppermute(value, "dp", pairs)


def up(value):
    return shift(value, lambda x, y, c: (x, y + 1, c))


def down(value):
    return shift(value, lambda x, y, c: (x, y + 3, c))


def across(value):
    return shift(value, lambda x, y, c: (x + 1, y, c))


def other_core(value):
    return shift(value, lambda x, y, c: (x, y, c + 1))


def to_peers(blocks):
    return lax.all_to_all(blocks, "expert", split_axis=0, concat_axis=0, tiled=True)


def add(a, b):
    return (a.astype(F32) + b.astype(F32)).astype(BF)


def rms_scale(values):
    return lax.rsqrt(jnp.mean(values * values, axis=-1, keepdims=True) + epsilon)


def rope_tables(offsets, head_width):
    exponent = jnp.arange(head_width // 2, dtype=jnp.float32) * (2.0 / head_width)
    frequency = jnp.exp(-exponent * math.log(rope_base))
    phase_angles = offsets.astype(jnp.float32)[:, None] * frequency[None, :]
    return (jnp.cos(phase_angles)[:, None, :], jnp.sin(phase_angles)[:, None, :])


def rotate(values, cosine, sine_table):
    half = values.shape[-1] // 2
    first, second = values[..., :half], values[..., half:]
    return jnp.concatenate(
        [first * cosine - second * sine_table, second * cosine + first * sine_table], axis=-1
    )


def layout(lengths, group_count):
    seq_ends = jnp.cumsum(lengths)
    starts = seq_ends - lengths
    places = jnp.arange(group_count, dtype=jnp.int32)
    member = ((places[:, None] >= starts[None, :]) & (places[:, None] < seq_ends[None, :])).astype(
        jnp.int32
    )
    numbers = jnp.arange(lengths.shape[0], dtype=jnp.int32)
    segment = jnp.sum(member * numbers[None, :], axis=1)
    offsets = places - jnp.sum(member * starts[None, :], axis=1)
    return (segment, offsets)


def norm_back(values, row_scale, gain_vector, grad_normed):
    weighted = grad_normed * gain_vector
    return row_scale * weighted - values * row_scale**3 * jnp.mean(
        weighted * values, axis=-1, keepdims=True
    )


def by_peer(table):
    return jnp.pad(table.reshape(PEERS, LOCAL, TOK), ((0, 0), (0, 8 - LOCAL), (0, 0)))


def local(
    tokens,
    cotangent,
    seq_lengths,
    expert_ids,
    w_query,
    w_key,
    w_value,
    w_output,
    norm_one,
    norm_two,
    w_router,
    w_gate,
    w_up,
    w_down,
):
    score_scale = HEAD ** (-0.5)
    down_piece = w_down.reshape(LOCAL, 32, 3, FFE).transpose(0, 2, 1, 3).reshape(LOCAL, ROWS, FFE)
    piece = jnp.concatenate([w_gate, w_up, down_piece], axis=1)

    slices = jnp.concatenate(
        [
            w_query.reshape(12, PEERS, QS).transpose(1, 0, 2),
            w_key.reshape(12, PEERS, HEAD).transpose(1, 0, 2),
            w_value.reshape(12, PEERS, HEAD).transpose(1, 0, 2),
            jnp.broadcast_to(
                jnp.concatenate(
                    [
                        norm_one[:, None],
                        norm_two[:, None],
                        w_router,
                        jnp.zeros((12, SLICE - QS - 2 * HEAD - 2 - EXPERTS), BF),
                    ],
                    axis=1,
                )[None],
                (PEERS, 12, SLICE - QS - 2 * HEAD),
            ),
        ],
        axis=2,
    )
    member = jnp.any(
        expert_ids[None, :, :] == jnp.arange(EXPERTS, dtype=jnp.int32)[:, None, None], axis=-1
    )
    before = jnp.arange(TOK)[:, None] < jnp.arange(TOK)[None, :]
    places = jnp.dot(member.astype(BF), before.astype(BF), preferred_element_type=F32)
    slot_table = by_peer(jnp.where(member, places, -1.0))

    slices_all, output_all, tokens_all, slots_all = gather_start(
        slices, w_output, [tokens, slot_table], ["gather", "exchange"], 1
    )
    piece, cot, _ = lax.optimization_barrier((piece, cotangent, slots_all))
    cot_all = to_peers(jnp.broadcast_to(cot[None], (PEERS, TOK, DIM)))
    x1 = across(piece)
    y3, y1 = up(piece), down(piece)
    x1y3, x1y1 = up(x1), down(x1)
    y2, x1y2 = up(y3), down(x1y1)
    pieces = [piece, x1, y1, y3, x1y1, x1y3, y2, x1y2]

    slices_all = slices_all.reshape(DIM, SLICE)
    output_all = output_all.reshape(DIM, DIM)
    qkv_all = slices_all[:, : QS + 2 * HEAD]
    gains = slices_all[:, QS + 2 * HEAD : QS + 2 * HEAD + 2].astype(F32).T
    gain_one, gain_two = gains[0], gains[1]
    router_all = slices_all[:, QS + 2 * HEAD + 2 : QS + 2 * HEAD + 2 + EXPERTS]

    segment, offsets = layout(seq_lengths[0], GROUP)
    cosine, sine_table = rope_tables(offsets, HEAD)
    places = jnp.arange(GROUP, dtype=jnp.int32)
    allowed = (segment[:, None] == segment[None, :]) & (places[None, :] <= places[:, None])

    inputs_all = tokens_all.reshape(GROUP, DIM).astype(F32)
    scale_all = rms_scale(inputs_all)
    normed_all = (inputs_all * scale_all * gain_one).astype(BF)
    qkv = jnp.dot(normed_all, qkv_all, preferred_element_type=F32)
    heads = rotate(
        qkv[:, : QS + HEAD].reshape(GROUP, REP + 1, HEAD), cosine, sine_table
    ).astype(BF)
    query, key = heads[:, :REP], heads[:, REP]
    value = qkv[:, QS + HEAD :].astype(BF)
    scores = jnp.einsum("qrh,kh->rqk", query, key, preferred_element_type=F32) * score_scale
    scores = jnp.where(allowed, scores, masked_score)
    highest = jnp.max(scores, axis=-1, keepdims=True)
    terms = jnp.exp(scores - highest)
    probs = terms / jnp.sum(terms, axis=-1, keepdims=True)
    probs_low = probs.astype(BF)
    attended = jnp.einsum("rqk,kh->qrh", probs_low, value, preferred_element_type=F32).astype(BF)
    (attended,) = exchange([attended.reshape(PEERS, TOK, QS)], ["exchange"], 3)
    attended = attended.transpose(1, 0, 2).reshape(TOK, DIM)

    inputs = tokens.astype(F32)
    middle = inputs + jnp.dot(attended, output_all, preferred_element_type=F32)
    scale_two = rms_scale(middle)
    normed_two = (middle * scale_two * gain_two).astype(BF)
    logits = lax.dot_general(
        router_all, normed_two, (((0,), (1,)), ((), ())), preferred_element_type=F32
    )
    chosen = jnp.where(member, logits, masked_score)
    weight = jnp.where(member, jnp.exp(chosen - jnp.max(chosen, axis=0, keepdims=True)), 0.0)
    gate_values = weight / jnp.sum(weight, axis=0, keepdims=True)

    late = [other_core(y2), other_core(x1y2)]
    rows_all, gates_all, shared = exchange_and_share(
        [normed_two, by_peer(gate_values)], ["gather", "exchange"], pieces[:6], 4
    )
    out_part, back_part, inner_part, keep, given = run_experts(
        rows_all, cot_all, slots_all, gates_all, pieces, shared, late
    )
    back_all, inner_all = exchange([back_part, inner_part], ["exchange", "exchange"], 5, 38)

    sums = {s: add(keep[k], given[k]) for k, s in enumerate(SLOTS)}
    up_two, down_two = up(sums[(0, 2)]), down(sums[(1, 2)])
    far = (
        sums[(1, 0)].astype(F32)
        + up(sums[(1, 1)]).astype(F32)
        + down(add(sums[(1, 3)], down_two)).astype(F32)
    ).astype(BF)
    near = (
        sums[(0, 0)].astype(F32)
        + up(add(sums[(0, 1)], up_two)).astype(F32)
        + down(sums[(0, 3)]).astype(F32)
    )
    expert_grads = near + across(far).astype(F32)

    grad_normed_two = jnp.sum(back_all.astype(F32), axis=0)
    grad_gates = inner_all[:, :LOCAL, :].reshape(EXPERTS, TOK)
    grad_chosen = gate_values * (
        grad_gates - jnp.sum(gate_values * grad_gates, axis=0, keepdims=True)
    )
    grad_logits = grad_chosen.astype(BF)
    grad_out = cotangent.astype(F32)
    grad_router = lax.dot_general(
        normed_two, grad_logits, (((0,), (1,)), ((), ())), preferred_element_type=F32
    )
    grad_normed_two = grad_normed_two + lax.dot_general(
        grad_logits, router_all, (((0,), (1,)), ((), ())), preferred_element_type=F32
    )
    grad_gain_two = jnp.sum(grad_normed_two * middle * scale_two, axis=0)
    grad_middle = grad_out + norm_back(middle, scale_two, gain_two, grad_normed_two)
    grad_branch = grad_middle.astype(BF)
    grad_attended = lax.dot_general(
        grad_branch, output_all, (((1,), (1,)), ((), ())), preferred_element_type=F32
    ).astype(BF)
    grad_attended = grad_attended.reshape(TOK, PEERS, QS).transpose(1, 0, 2)
    (grad_attended,) = exchange([grad_attended], ["exchange"], 6)
    out_part, _ = lax.optimization_barrier((out_part, grad_attended))
    out_all = to_peers(out_part)
    grad_attended = grad_attended.reshape(GROUP, REP, HEAD)
    grad_output = lax.dot_general(
        attended, grad_branch, (((0,), (0,)), ((), ())), preferred_element_type=F32
    )

    grad_probs = jnp.einsum("qrh,kh->rqk", grad_attended, value, preferred_element_type=F32)
    grad_scores = (
        probs * (grad_probs - jnp.sum(probs * grad_probs, axis=-1, keepdims=True))
    ).astype(BF)
    grad_query = (
        jnp.einsum("rqk,kh->qrh", grad_scores, key, preferred_element_type=F32) * score_scale
    )
    grad_key = (
        jnp.einsum("rqk,qrh->kh", grad_scores, query, preferred_element_type=F32) * score_scale
    )
    grad_value = jnp.einsum("rqk,qrh->kh", probs_low, grad_attended, preferred_element_type=F32)
    grad_heads = rotate(
        jnp.concatenate([grad_query, grad_key[:, None, :]], axis=1), cosine, -sine_table
    ).reshape(GROUP, QS + HEAD)
    grad_qkv = jnp.concatenate([grad_heads, grad_value], axis=1).astype(BF)
    grad_slices = lax.dot_general(
        normed_all, grad_qkv, (((0,), (0,)), ((), ())), preferred_element_type=F32
    )
    grad_normed = lax.dot_general(
        grad_qkv, qkv_all, (((1,), (1,)), ((), ())), preferred_element_type=F32
    )
    grad_gain_one = jnp.sum(grad_normed * inputs_all * scale_all, axis=0)
    small = jnp.concatenate(
        [
            grad_slices.astype(BF),
            grad_gain_one[:, None].astype(BF),
            grad_gain_two[:, None].astype(BF),
            grad_router.astype(BF),
            jnp.zeros((DIM, SLICE - QS - 2 * HEAD - 2 - EXPERTS), BF),
        ],
        axis=1,
    )
    normed_back, small_rows, output_rows = scatter_sum(
        [grad_normed.astype(BF).reshape(PEERS, TOK, DIM)],
        [small.reshape(DP, ROWS, SLICE), grad_output.astype(BF).reshape(DP, ROWS, DIM)],
        7,
    )
    mixed = middle + jnp.sum(out_all.astype(F32), axis=0)
    grad_tokens = grad_middle + norm_back(
        inputs, scale_all_own(scale_all), gain_one, jnp.sum(normed_back.astype(F32), axis=0)
    )
    small_own, output_own = exchange(
        [small_rows.reshape(PEERS, 12, SLICE), output_rows.reshape(PEERS, 12, DIM)],
        ["exchange", "exchange"],
        8,
    )
    own_sum = jnp.sum(small_own[:, :, QS + 2 * HEAD :], axis=0)
    last = QS + 2 * HEAD
    return (
        mixed.astype(BF),
        grad_tokens,
        small_own[:, :, :QS].transpose(1, 0, 2).reshape(12, DIM),
        small_own[:, :, QS : QS + HEAD].transpose(1, 0, 2).reshape(12, KV_HEADS * HEAD),
        small_own[:, :, QS + HEAD : last].transpose(1, 0, 2).reshape(12, KV_HEADS * HEAD),
        jnp.sum(output_own, axis=0),
        own_sum[:, 0],
        own_sum[:, 1],
        own_sum[:, 2 : 2 + EXPERTS],
        expert_grads[:, :ROWS],
        expert_grads[:, ROWS : 2 * ROWS],
        expert_grads[:, 2 * ROWS :]
        .reshape(LOCAL, 3, 32, FFE)
        .transpose(0, 2, 1, 3)
        .reshape(LOCAL, 32, DIM),
    )


def scale_all_own(scale_all):
    return lax.dynamic_slice_in_dim(scale_all, lax.axis_index("expert") * TOK, TOK)


def solution(mesh):
    both = P(("dp", "expert"), None)
    line = P(("dp", "expert"))
    cube = P("expert", "dp", None)
    in_specs = (both, both, P("dp", None), both, both, both, both, both)
    in_specs = in_specs + (line, line, both, cube, cube, cube)
    out_specs = (both,) * 6 + (line, line, both, cube, cube, cube)
    return jax.shard_map(local, mesh=mesh, in_specs=in_specs, out_specs=out_specs, check_vma=False)
```

```python
import functools
import math

import jax
import jax.numpy as jnp
from jax import lax
from jax.experimental import pallas as pl
from jax.experimental.pallas import tpu as pltpu
from jax.sharding import PartitionSpec as P

HEADS = 24
KV_HEADS = 8
HEAD = 64
DIM = 1536
FFE = 512
EXPERTS = 40
LOCAL = 5
CAP = 32
TOK = 128
PEERS = 8
DP = 16
GROUP = TOK * PEERS
REP = HEADS // KV_HEADS
SLICE = 384
QS = REP * HEAD
ROWS = 96
ROUTER = QS + 2 * HEAD
GAINS = ROUTER + EXPERTS

epsilon = 1e-06
rope_base = 10000.0
masked_score = -1e30
MESH = pl.DeviceIdType.MESH
BF = jnp.bfloat16
F32 = jnp.float32

RELATIVE = ((2, 1), (2, 0), (1, 1), (3, 1), (0, 1), (1, 0), (3, 0))
SLOTS = ((0, 0), (1, 0), (0, 1), (0, 3), (1, 1), (1, 3), (0, 2), (1, 2))


def expert_peers():
    me = lax.axis_index("expert")
    z, x = me // 2, me % 2
    return me, [(z + rz) % 4 * 2 + (x + rx) % 2 for rz, rx in RELATIVE]


def dp_place():
    d = lax.axis_index("dp")
    return d // 8, (d // 2) % 4, d % 2


def dp_index(x, y, core):
    return (x % 2 * 4 + y % 4) * 2 + core % 2


def signal_all(expert_ids, dp_ids):
    barrier = pltpu.get_barrier_semaphore()
    for p in expert_ids:
        pl.semaphore_signal(barrier, inc=1, device_id={"expert": p}, device_id_type=MESH)
    for p in dp_ids:
        pl.semaphore_signal(barrier, inc=1, device_id={"dp": p}, device_id_type=MESH)
    pl.semaphore_wait(barrier, len(expert_ids) + len(dp_ids))


def any_specs(count):
    return [pl.BlockSpec(memory_space=pl.ANY)] * count


def expert_copies(ins, outs, modes, send, recv):
    me, peers = expert_peers()
    copies = []
    for r, p in enumerate(peers):
        for i, mode in enumerate(modes):
            copies.append(
                pltpu.make_async_remote_copy(
                    src_ref=ins[i] if mode == "gather" else ins[i].at[p],
                    dst_ref=outs[i].at[me],
                    send_sem=send.at[i, r],
                    recv_sem=recv.at[i, r],
                    device_id={"expert": p},
                    device_id_type=MESH,
                )
            )
    return copies


def own_copies(ins, outs, modes, sems):
    me = lax.axis_index("expert")
    return [
        pltpu.make_async_copy(
            ins[i] if mode == "gather" else ins[i].at[me], outs[i].at[me], sems.at[i]
        )
        for i, mode in enumerate(modes)
    ]


def lasting(us):
    return pl.CostEstimate(flops=us * 1_000_000_000, bytes_accessed=0, transcendentals=0)


def exchange(arrays, modes, cid, us=10):
    n = len(arrays)

    def kernel(*refs):
        ins, outs = refs[:n], refs[n : 2 * n]
        send, recv, local = refs[2 * n :]
        _, peers = expert_peers()
        signal_all(peers, [])
        copies = expert_copies(ins, outs, modes, send, recv) + own_copies(ins, outs, modes, local)
        for c in copies:
            c.start()
        for c in copies:
            c.wait()

    shapes = [
        jax.ShapeDtypeStruct(((PEERS,) + a.shape) if m == "gather" else a.shape, a.dtype)
        for a, m in zip(arrays, modes)
    ]
    return pl.pallas_call(
        kernel,
        out_shape=shapes,
        in_specs=any_specs(n),
        out_specs=any_specs(n),
        scratch_shapes=[
            pltpu.SemaphoreType.DMA((n, 7)),
            pltpu.SemaphoreType.DMA((n, 7)),
            pltpu.SemaphoreType.DMA((n,)),
        ],
        compiler_params=pltpu.CompilerParams(collective_id=cid, has_side_effects=True),
        cost_estimate=lasting(us),
    )(*arrays)


class Gather:
    def __init__(self, src, out, send, recv, local):
        self.src, self.out, self.send, self.recv, self.local = src, out, send, recv, local
        me = lax.axis_index("expert")
        z, x = me // 2, me % 2

        def place(dz, dx):
            return (z + dz) % 4 * 2 + (x + dx) % 2

        self.me, self.across, self.up, self.down = me, place(0, 1), place(1, 0), place(3, 0)
        self.slots = [
            place(0, 1),
            place(3, 0),
            place(1, 0),
            place(3, 1),
            place(1, 1),
            place(2, 0),
            place(2, 1),
        ]
        self.started = []

    def copy(self, k, src, slot, target):
        c = pltpu.make_async_remote_copy(
            src_ref=src,
            dst_ref=self.out.at[slot],
            send_sem=self.send.at[k],
            recv_sem=self.recv.at[k],
            device_id={"expert": target},
            device_id_type=MESH,
        )
        c.start()
        self.started.append(c)

    def arrive(self, k):
        pltpu.make_async_remote_copy(
            src_ref=self.src,
            dst_ref=self.out.at[self.slots[k]],
            send_sem=self.send.at[k],
            recv_sem=self.recv.at[k],
            device_id={"expert": self.up},
            device_id_type=MESH,
        ).wait_recv()

    def begin(self):
        self.copy(0, self.src, self.me, self.across)
        self.copy(1, self.src, self.me, self.up)
        self.copy(2, self.src, self.me, self.down)
        self.own = pltpu.make_async_copy(self.src, self.out.at[self.me], self.local)
        self.own.start()

    def first(self):
        self.arrive(0)
        self.copy(3, self.out.at[self.slots[0]], self.slots[0], self.up)
        self.copy(4, self.out.at[self.slots[0]], self.slots[0], self.down)

    def second(self):
        self.arrive(1)
        self.copy(5, self.out.at[self.slots[1]], self.slots[1], self.up)

    def third(self):
        self.arrive(4)
        self.copy(6, self.out.at[self.slots[4]], self.slots[4], self.down)

    def finish(self):
        for k in (2, 3, 5, 6):
            self.arrive(k)
        for c in self.started:
            c.wait_send()
        self.own.wait()


class Dense:
    def __init__(self, rows, out, send, recv, local):
        self.rows, self.out, self.send, self.recv, self.local = rows, out, send, recv, local
        x, y, core = dp_place()
        self.x, self.y, self.core = x, y, core
        self.mine = dp_index(x, y, core)
        self.to_x, self.to_up = dp_index(x + 1, y, core), dp_index(x, y + 1, core)
        self.to_down, self.to_core = dp_index(x, y + 3, core), dp_index(x, y, core + 1)
        self.slots = [dp_index(x + rx, y + ry, core) for rx, ry in SLOTS]
        self.started = []

    def descriptor(self, k, src, slot, target):
        return pltpu.make_async_remote_copy(
            src_ref=src,
            dst_ref=self.out.at[slot],
            send_sem=self.send.at[k],
            recv_sem=self.recv.at[k],
            device_id={"dp": target},
            device_id_type=MESH,
        )

    def copy(self, k, slot, target, src=None):
        c = self.descriptor(k, self.out.at[slot] if src is None else src, slot, target)
        c.start()
        self.started.append(c)

    def arrive(self, k, slot):
        self.descriptor(k, self.out.at[slot], slot, self.to_x).wait_recv()

    def share(self, k):
        self.copy(8 + k, self.slots[k], self.to_core)

    def begin(self):
        self.copy(1, self.mine, self.to_x, self.rows)
        self.copy(3, self.mine, self.to_up, self.rows)
        self.copy(2, self.mine, self.to_down, self.rows)
        self.copy(8, self.mine, self.to_core, self.rows)
        self.own = pltpu.make_async_copy(self.rows, self.out.at[self.mine], self.local)
        self.own.start()

    def first(self):
        self.arrive(1, self.slots[1])
        self.copy(5, self.slots[1], self.to_up)
        self.copy(4, self.slots[1], self.to_down)
        self.share(1)
        self.arrive(3, self.slots[3])
        self.copy(6, self.slots[3], self.to_up)
        self.share(3)
        self.arrive(2, self.slots[2])
        self.share(2)

    def second(self):
        self.arrive(4, self.slots[4])
        self.copy(7, self.slots[4], self.to_down)
        self.share(4)
        self.arrive(5, self.slots[5])
        self.share(5)

    def third(self):
        for k in (6, 7):
            self.arrive(k, self.slots[k])
            self.share(k)

    def finish(self):
        for k, (rx, ry) in enumerate(SLOTS):
            self.arrive(8 + k, dp_index(self.x + rx, self.y + ry, self.core + 1))
        for c in self.started:
            c.wait_send()
        self.own.wait()


class Pieces:
    parts = ((0, 3), (3, 1), (4, 1))

    def __init__(self, piece, out, send, recv, local):
        self.piece, self.out, self.send, self.recv, self.local = piece, out, send, recv, local
        x, y, core = dp_place()
        self.x, self.y, self.core = x, y, core
        self.mine = dp_index(x, y, core)
        self.targets = {
            "x": dp_index(x + 1, y, core),
            "up": dp_index(x, y + 1, core),
            "down": dp_index(x, y + 3, core),
            "core": dp_index(x, y, core + 1),
        }
        self.slots = [dp_index(x + rx, y + ry, core) for rx, ry in SLOTS]
        self.started = []

    def descriptor(self, g, k, src, slot, target):
        first, count = self.parts[g]
        return pltpu.make_async_remote_copy(
            src_ref=src.at[pl.ds(first, count)],
            dst_ref=self.out.at[slot, pl.ds(first, count)],
            send_sem=self.send.at[g, k],
            recv_sem=self.recv.at[g, k],
            device_id={"dp": target},
            device_id_type=MESH,
        )

    def move(self, g, k, where, source=0):
        src = self.piece if source == 0 else self.out.at[self.slots[source]]
        c = self.descriptor(g, k, src, self.slots[source], self.targets[where])
        c.start()
        self.started.append(c)

    def arrive(self, g, k, share=True):
        slot = self.slots[k]
        self.descriptor(g, k, self.out.at[slot], slot, self.targets["x"]).wait_recv()
        if share:
            self.move(g, 8 + k, "core", k)

    def begin(self):
        for g in range(3):
            self.move(g, 8, "core")
        self.own = pltpu.make_async_copy(self.piece, self.out.at[self.mine], self.local)
        self.own.start()

    def finish(self):
        for g in range(3):
            for k, (rx, ry) in enumerate(SLOTS):
                slot = dp_index(self.x + rx, self.y + ry, self.core + 1)
                self.descriptor(
                    g, 8 + k, self.out.at[slot], slot, self.targets["x"]
                ).wait_recv()
        for c in self.started:
            c.wait_send()
        self.own.wait()


def first_kernel(*refs):
    (slices, output, tokens, cot, member_ref, slot_send, piece, cos_ref, sin_ref, start_ref) = refs[
        :10
    ]
    (
        pieces_out,
        cot_all,
        slots_all,
        rows_all,
        gates_all,
        tokens_out,
        normed_out,
        small_out,
        output_out,
        query_ref,
        key_ref,
        value_ref,
        log_ref,
        attended_ref,
        middle_ref,
        normed_two_ref,
        gates_ref,
    ) = refs[10:27]
    (
        small_in,
        output_in,
        small_rows,
        output_rows,
        small,
        dense,
        tokens_in,
        normed,
        att_send,
        gate_send,
        s_small,
        s_dense,
        s_piece,
        r_small,
        r_dense,
        r_piece,
        s_gather,
        r_gather,
        s_direct,
        r_direct,
        l_sem,
    ) = refs[27:]
    _, peers = expert_peers()
    x, y, core = dp_place()
    signal_all(
        peers,
        [
            dp_index(x + 1, y, core),
            dp_index(x, y + 1, core),
            dp_index(x, y + 3, core),
            dp_index(x, y, core + 1),
        ],
    )

    def direct(i, src, out, mode):
        part = expert_copies(
            [src], [out], [mode], s_direct.at[pl.ds(i, 1)], r_direct.at[pl.ds(i, 1)]
        ) + own_copies([src], [out], [mode], l_sem.at[pl.ds(i, 1)])
        for c in part:
            c.start()
        return part

    def settle(part):
        for c in part:
            c.wait()

    saved = []

    def save(src, dst, i):
        c = pltpu.make_async_copy(src, dst, l_sem.at[i])
        c.start()
        saved.append(c)

    parts = [
        direct(0, slices, small_in, "exchange"),
        direct(1, output, output_in, "gather"),
        direct(2, slot_send, slots_all, "exchange"),
    ]
    tokens_gather = Gather(tokens, tokens_in, s_gather.at[0], r_gather.at[0], l_sem.at[5])
    tokens_gather.begin()
    experts = Pieces(piece, pieces_out, s_piece, r_piece, l_sem.at[6])
    experts.begin()
    for g in (1, 2):
        experts.move(g, 3, "up")
        experts.move(g, 2, "down")

    weights = []
    for i, (landed, rows, out) in enumerate(
        ((small_in, small_rows, small), (output_in, output_rows, dense))
    ):
        settle(parts[i])
        rows[...] = jnp.concatenate([landed[j] for j in range(PEERS)], axis=0)
        weights.append(Dense(rows, out, s_dense.at[i], r_dense.at[i], l_sem.at[7 + i]))
        weights[i].begin()
    experts.move(0, 1, "x")
    for g in (1, 2):
        experts.move(g, 1, "x")
    tokens_gather.first()
    for w in weights:
        w.first()
    tokens_gather.second()
    for w in weights:
        w.second()
    tokens_gather.third()
    experts.move(0, 3, "up")
    experts.move(0, 2, "down")
    cot_gather = Gather(cot, cot_all, s_gather.at[1], r_gather.at[1], l_sem.at[9])
    cot_gather.begin()
    for w in weights:
        w.third()
    weights[0].finish()
    tokens_gather.finish()

    for g in (1, 2):
        experts.arrive(g, 3)
        experts.arrive(g, 2)
    experts.move(1, 6, "up", 3)
    experts.move(2, 6, "down", 2)
    for g in (1, 2):
        experts.move(g, 5, "x", 3)
        experts.move(g, 4, "x", 2)

    w_small = small[...].reshape(DIM, SLICE)
    pick = (
        lax.broadcasted_iota(jnp.int32, (8, SLICE), 1)
        == lax.broadcasted_iota(jnp.int32, (8, SLICE), 0) + GAINS
    )
    gains = dot(pick.astype(F32).astype(BF), w_small, ((1,), (1,)))
    gain_one, gain_two = gains[0:1], gains[1:2]

    def project(i, _):
        values = tokens_in[pl.ds(2 * i, 2)].reshape(2 * TOK, DIM).astype(F32)
        scale = lax.rsqrt(jnp.mean(values * values, axis=-1, keepdims=True) + epsilon)
        low = (values * scale * gain_one).astype(BF)
        normed[pl.ds(2 * i, 2)] = low.reshape(2, TOK, DIM)
        qkv = dot(low, small[...].reshape(DIM, SLICE), ((1,), (0,)))
        span = pl.ds(pl.multiple_of(i * 2 * TOK, 2 * TOK), 2 * TOK)
        cosine, sine = cos_ref[span, :], sin_ref[span, :]
        lane = lax.broadcasted_iota(jnp.int32, (2 * TOK, 128), 1)
        turned = []
        for h in range(2):
            v = qkv[:, 128 * h : 128 * h + 128]
            other = jnp.where(lane % HEAD < HEAD // 2, pltpu.roll(v, 96, 1), pltpu.roll(v, 32, 1))
            turned.append((v * cosine + other * sine).astype(BF))
        heads = (turned[0][:, :HEAD], turned[0][:, HEAD:], turned[1][:, :HEAD])
        for b in range(2):
            for h in range(REP):
                query_ref[2 * i + b, h * TOK : (h + 1) * TOK, :] = heads[h][
                    b * TOK : (b + 1) * TOK
                ]
        key_ref[span, :] = turned[1][:, HEAD:]
        value_ref[span, :] = qkv[:, QS + HEAD : ROUTER].astype(BF)
        return _

    lax.fori_loop(0, 4, project, 0)
    save(tokens_in, tokens_out, 10)
    save(normed, normed_out, 11)
    save(small, small_out, 12)

    def attend(width, i, _):
        scores = dot(query_ref[i], key_ref[0:width, :], ((1,), (1,))) * HEAD ** (-0.5)
        keys = lax.broadcasted_iota(jnp.int32, (TOK, width), 1)
        rows = lax.broadcasted_iota(jnp.int32, (TOK, width), 0) + i * TOK
        begins = start_ref[pl.ds(pl.multiple_of(i * TOK, TOK), TOK), :][:, :1]
        allowed = (keys <= rows) & (keys >= begins)
        scores = jnp.where(allowed[None], scores.reshape(REP, TOK, width), masked_score)
        top = jnp.max(scores, axis=-1, keepdims=True)
        terms = jnp.exp(scores - top)
        total = jnp.sum(terms, axis=-1, keepdims=True)
        probs = (terms / total).astype(BF).reshape(REP * TOK, width)
        out = dot(probs, value_ref[0:width, :], ((1,), (0,))).astype(BF)
        att_send[i] = jnp.concatenate([out[h * TOK : (h + 1) * TOK] for h in range(REP)], axis=1)
        log_ref[i] = jnp.broadcast_to(
            (top + jnp.log(total)).reshape(REP * TOK, 1), (REP * TOK, 128)
        )
        return _

    experts.arrive(0, 1)
    experts.move(0, 5, "up", 1)
    experts.move(0, 4, "down", 1)
    cot_gather.first()
    cot_gather.second()
    lax.fori_loop(0, 4, functools.partial(attend, GROUP // 2), 0)
    for g in (1, 2):
        experts.arrive(g, 1)
    cot_gather.third()
    lax.fori_loop(4, 8, functools.partial(attend, GROUP), 0)
    parts.append(direct(3, att_send, attended_ref, "exchange"))
    experts.arrive(0, 3)
    experts.move(0, 6, "up", 3)
    experts.arrive(0, 2)
    for g in (1, 2):
        experts.arrive(g, 4)
        experts.arrive(g, 5)
    settle(parts[3])
    weights[1].finish()
    save(dense, output_out, 13)

    me = lax.axis_index("expert")
    middle = tokens_in[me].astype(F32)
    for j in range(PEERS):
        middle = middle + dot(
            attended_ref[j], dense[2 * j : 2 * j + 2].reshape(QS, DIM), ((1,), (0,))
        )
    middle_ref[...] = middle
    scale_two = lax.rsqrt(jnp.mean(middle * middle, axis=-1, keepdims=True) + epsilon)
    normed_two = (middle * scale_two * gain_two).astype(BF)
    normed_two_ref[...] = normed_two
    rows_gather = Gather(normed_two_ref, rows_all, s_gather.at[2], r_gather.at[2], l_sem.at[14])
    rows_gather.begin()
    logits = dot(small[:, :, 256:SLICE].reshape(DIM, SLICE - 256), normed_two, ((0,), (1,)))
    logits = logits[ROUTER - 256 : GAINS - 256]
    member = member_ref[...] >= 0.0
    chosen = jnp.where(member, logits, masked_score)
    weight = jnp.where(member, jnp.exp(chosen - jnp.max(chosen, axis=0, keepdims=True)), 0.0)
    gates_ref[...] = weight / jnp.sum(weight, axis=0, keepdims=True)
    gate_send[...] = jnp.zeros_like(gate_send)
    for j in range(PEERS):
        gate_send[j, 0:LOCAL, :] = gates_ref[LOCAL * j : LOCAL * (j + 1), :]
    parts.append(direct(4, gate_send, gates_all, "exchange"))

    rows_gather.first()
    rows_gather.second()
    experts.arrive(0, 4)
    experts.move(0, 7, "down", 4)
    experts.arrive(0, 5)
    rows_gather.third()
    for g in (1, 2):
        experts.arrive(g, 6)
        experts.move(g, 7, "x", 6)
    cot_gather.finish()
    rows_gather.finish()
    settle(parts[2])
    settle(parts[4])
    experts.arrive(0, 6)
    for g in (0, 1, 2):
        experts.arrive(g, 7)
    experts.finish()
    for c in saved:
        c.wait()


def first_phase(slices, output, tokens, cot, member, slot_send, piece, cosine, sine, start):
    hbm, vmem = pl.BlockSpec(memory_space=pl.ANY), pl.BlockSpec(memory_space=pltpu.VMEM)
    shape = jax.ShapeDtypeStruct
    blocks = (PEERS, TOK, DIM)
    outs = [
        (shape((DP,) + piece.shape, BF), hbm),
        (shape(blocks, BF), hbm),
        (shape((PEERS, 8, TOK), F32), hbm),
        (shape(blocks, BF), hbm),
        (shape((PEERS, 8, TOK), F32), hbm),
        (shape(blocks, BF), hbm),
        (shape(blocks, BF), hbm),
        (shape((DP, ROWS, SLICE), BF), hbm),
        (shape((DP, ROWS, DIM), BF), hbm),
        (shape((PEERS, REP * TOK, HEAD), BF), vmem),
        (shape((GROUP, HEAD), BF), vmem),
        (shape((GROUP, HEAD), BF), vmem),
        (shape((PEERS, REP * TOK, 128), F32), vmem),
        (shape((PEERS, TOK, QS), BF), vmem),
        (shape((TOK, DIM), F32), vmem),
        (shape((TOK, DIM), BF), vmem),
        (shape((EXPERTS, TOK), F32), vmem),
    ]
    dma = pltpu.SemaphoreType.DMA
    return pl.pallas_call(
        first_kernel,
        out_shape=[o[0] for o in outs],
        in_specs=[hbm] * 4 + [vmem] + [hbm] * 2 + [vmem] * 3,
        out_specs=[o[1] for o in outs],
        scratch_shapes=[
            pltpu.VMEM((PEERS, 12, SLICE), BF),
            pltpu.VMEM((PEERS, 12, DIM), BF),
            pltpu.VMEM((ROWS, SLICE), BF),
            pltpu.VMEM((ROWS, DIM), BF),
            pltpu.VMEM((DP, ROWS, SLICE), BF),
            pltpu.VMEM((DP, ROWS, DIM), BF),
            pltpu.VMEM(blocks, BF),
            pltpu.VMEM(blocks, BF),
            pltpu.VMEM((PEERS, TOK, QS), BF),
            pltpu.VMEM((PEERS, 8, TOK), F32),
            dma((1,)),
            dma((2, 16)),
            dma((3, 16)),
            dma((1,)),
            dma((2, 16)),
            dma((3, 16)),
            dma((3, 7)),
            dma((3, 7)),
            dma((5, 7)),
            dma((5, 7)),
            dma((15,)),
        ],
        compiler_params=pltpu.CompilerParams(
            collective_id=1, has_side_effects=True, vmem_limit_bytes=50 << 20
        ),
        cost_estimate=lasting(120),
    )(slices, output, tokens, cot, member, slot_send, piece, cosine, sine, start)


def scatter_sum(arrays, dense, cid):
    n, m = len(arrays), len(dense)
    shapes = [(d.shape[1], d.shape[2]) for d in dense]

    def kernel(*refs):
        ins, dins = refs[:n], refs[n : n + m]
        outs, totals = refs[n + m : 2 * n + m], refs[2 * n + m : 2 * (n + m)]
        refs = refs[2 * (n + m) :]
        mine, theirs, along, last = refs[:m], refs[m : 2 * m], refs[2 * m : 3 * m], refs[3 * m : 4 * m]
        send, recv, local, lsem, csend, crecv, ysend, yrecv, xsend, xrecv = refs[4 * m :]
        x, y, core = dp_place()
        to_core, to_x = dp_index(x, y, core + 1), dp_index(x + 1, y, core)
        to_y = [dp_index(x, y + r, core) for r in (1, 2, 3)]
        _, peers = expert_peers()
        signal_all(peers, [to_core, to_x] + to_y)
        modes = ["exchange"] * n
        order = [(r, s) for r in (1, 0) for s in (2, 1, 3, 0)]
        started, loads, shares = [], {}, {}

        def remote(src, dst, s, r, target):
            c = pltpu.make_async_remote_copy(
                src_ref=src,
                dst_ref=dst,
                send_sem=s,
                recv_sem=r,
                device_id={"dp": target},
                device_id_type=MESH,
            )
            c.start()
            started.append(c)
            return c

        for i in range(m):
            for r, s in order:
                k = 4 * r + s
                shares[i, k] = remote(
                    dins[i].at[dp_index(x + r, y + s, core + 1)],
                    theirs[i].at[k],
                    csend.at[i, k],
                    crecv.at[i, k],
                    to_core,
                )
                loads[i, k] = pltpu.make_async_copy(
                    dins[i].at[dp_index(x + r, y + s, core)], mine[i].at[k], lsem.at[i, k]
                )
                loads[i, k].start()
        copies = expert_copies(ins, outs, modes, send, recv) + own_copies(ins, outs, modes, local)
        for c in copies:
            c.start()
        moves = {}
        for r, s in order:
            k = 4 * r + s
            for i in range(m):
                loads[i, k].wait()
                shares[i, k].wait_recv()
                mine[i][k] = (mine[i][k].astype(F32) + theirs[i][k].astype(F32)).astype(BF)
                if s > 0:
                    moves[i, r, s] = remote(
                        mine[i].at[k],
                        along[i].at[3 * r + s - 1],
                        ysend.at[i, 3 * r + s - 1],
                        yrecv.at[i, 3 * r + s - 1],
                        to_y[s - 1],
                    )
        crossings = []
        for i in range(m):
            acc = mine[i][4].astype(F32)
            for s in (2, 1, 3):
                moves[i, 1, s].wait_recv()
                acc = acc + along[i][3 + s - 1].astype(F32)
            mine[i][4] = acc.astype(BF)
            crossings.append(remote(mine[i].at[4], last[i], xsend.at[i], xrecv.at[i], to_x))
        for i in range(m):
            acc = mine[i][0].astype(F32)
            for s in (2, 1, 3):
                moves[i, 0, s].wait_recv()
                acc = acc + along[i][s - 1].astype(F32)
            crossings[i].wait_recv()
            totals[i][...] = acc + last[i][...].astype(F32)
        for c in started:
            c.wait_send()
        for c in copies:
            c.wait()

    vmem = pl.BlockSpec(memory_space=pltpu.VMEM)
    return pl.pallas_call(
        kernel,
        out_shape=[jax.ShapeDtypeStruct(a.shape, a.dtype) for a in arrays]
        + [jax.ShapeDtypeStruct(d, F32) for d in shapes],
        in_specs=any_specs(n + m),
        out_specs=any_specs(n) + [vmem] * m,
        scratch_shapes=[pltpu.VMEM((8,) + d, BF) for d in shapes]
        + [pltpu.VMEM((8,) + d, BF) for d in shapes]
        + [pltpu.VMEM((6,) + d, BF) for d in shapes]
        + [pltpu.VMEM(d, BF) for d in shapes]
        + [
            pltpu.SemaphoreType.DMA((n, 7)),
            pltpu.SemaphoreType.DMA((n, 7)),
            pltpu.SemaphoreType.DMA((n,)),
            pltpu.SemaphoreType.DMA((m, 8)),
            pltpu.SemaphoreType.DMA((m, 8)),
            pltpu.SemaphoreType.DMA((m, 8)),
            pltpu.SemaphoreType.DMA((m, 6)),
            pltpu.SemaphoreType.DMA((m, 6)),
            pltpu.SemaphoreType.DMA((m,)),
            pltpu.SemaphoreType.DMA((m,)),
        ],
        compiler_params=pltpu.CompilerParams(
            collective_id=cid, has_side_effects=True, vmem_limit_bytes=40 << 20
        ),
        cost_estimate=lasting(45),
    )(*arrays, *dense)


def dot(a, b, contract):
    return lax.dot_general(a, b, ((contract[0], contract[1]), ((), ())), preferred_element_type=F32)


def experts_kernel(*refs):
    (rows_ref, cot_ref, slot_ref, gate_ref), refs = refs[:4], refs[4:]
    pieces, refs = refs[0], refs[1:]
    (out_ref, back_ref, inner_ref, keep_ref, given_ref), refs = refs[:5], refs[5:]
    xg, cg, weights, grads, gates, inners, wsem, gsem, rsem = refs
    x, y, core = dp_place()
    other = dp_index(x, y, core + 1)
    signal_all([], [other])

    def load(e, b):
        return pltpu.make_async_copy(pieces.at[:, e], weights.at[b], wsem.at[b])

    def kept(e, b):
        return [
            pltpu.make_async_copy(
                grads.at[b, dp_index(x + rx, y + ry, core)], keep_ref.at[k, e], gsem.at[b, k]
            )
            for k, (rx, ry) in enumerate(SLOTS)
        ]

    def given(e, b):
        return [
            pltpu.make_async_remote_copy(
                src_ref=grads.at[b, dp_index(x + rx, y + ry, core + 1)],
                dst_ref=given_ref.at[k, e],
                send_sem=gsem.at[b, 8 + k],
                recv_sem=rsem.at[e, k],
                device_id={"dp": other},
                device_id_type=MESH,
            )
            for k, (rx, ry) in enumerate(SLOTS)
        ]

    def stored(e, b):
        for c in kept(e, b):
            c.wait()
        for c in given(e, b):
            c.wait_send()

    load(0, 0).start()

    def onehot(b):
        places = lax.broadcasted_iota(jnp.int32, (CAP, TOK), 0).astype(F32)
        return [(places == slot_ref[b, e : e + 1, :]) for e in range(LOCAL)]

    def collect(b, _):
        hot = onehot(b)
        pick = jnp.concatenate([h.astype(F32) for h in hot], axis=0).astype(BF)
        xg[b] = dot(pick, rows_ref[b], ((1,), (0,))).astype(BF)
        cg[b] = dot(pick, cot_ref[b], ((1,), (0,))).astype(BF)
        for e in range(LOCAL):
            g = jnp.sum(jnp.where(hot[e], gate_ref[b, e : e + 1, :], 0.0), axis=1, keepdims=True)
            gates[e, pl.ds(b * CAP, CAP), :] = jnp.broadcast_to(g, (CAP, 128))
        return _

    lax.fori_loop(0, PEERS, collect, 0)

    def expert(e, _):
        b = lax.rem(e, 2)
        load(e, b).wait()

        @pl.when(e + 1 < LOCAL)
        def _next():
            load(e + 1, 1 - b).start()

        @pl.when(e >= 2)
        def _free():
            stored(e - 2, b)

        span = pl.ds(pl.multiple_of(e * CAP, CAP), CAP)
        rows = xg[:, span, :].reshape(PEERS * CAP, DIM)
        cot = cg[:, span, :].reshape(PEERS * CAP, DIM)
        gate = gates[e][:, :1]
        w_gate = weights[b, :, 0:96, :].reshape(DIM, FFE)
        gate_act = dot(rows, w_gate, ((1,), (0,)))
        w_up = weights[b, :, 96:192, :].reshape(DIM, FFE)
        up_act = dot(rows, w_up, ((1,), (0,)))
        sig = 1.0 / (1.0 + jnp.exp(-gate_act))
        silu = gate_act * sig
        hidden = (silu * up_act).astype(BF)
        grad_out = (cot.astype(F32) * gate).astype(BF)
        inner = jnp.zeros((PEERS * CAP, 1), F32)
        grad_hidden = jnp.zeros((PEERS * CAP, FFE), F32)
        gated = []
        for k in range(3):
            lanes = slice(k * FFE, (k + 1) * FFE)
            w_down = weights[b, :, 192 + 32 * k : 224 + 32 * k, :].reshape(FFE, FFE)
            part = dot(hidden, w_down, ((1,), (0,))).astype(BF).astype(F32)
            inner = inner + jnp.sum(part * cot[:, lanes].astype(F32), axis=1, keepdims=True)
            gated.append((part * gate).astype(BF))
            grad_hidden = grad_hidden + dot(grad_out[:, lanes], w_down, ((1,), (1,)))
            grads[b, :, 192 + 32 * k : 224 + 32 * k, :] = (
                dot(hidden, grad_out[:, lanes], ((0,), (0,))).astype(BF).reshape(DP, 32, FFE)
            )
        inners[e] = jnp.broadcast_to(inner, (PEERS * CAP, 128))
        grad_gate = (grad_hidden * up_act * sig * (1.0 + gate_act * (1.0 - sig))).astype(BF)
        grad_up = (grad_hidden * silu).astype(BF)
        grads[b, :, 0:96, :] = (
            dot(rows, grad_gate, ((0,), (0,))).astype(BF).reshape(DP, ROWS, FFE)
        )
        grads[b, :, 96:192, :] = (
            dot(rows, grad_up, ((0,), (0,))).astype(BF).reshape(DP, ROWS, FFE)
        )
        for c in kept(e, b) + given(e, b):
            c.start()
        back = dot(grad_gate, w_gate, ((1,), (1,))) + dot(grad_up, w_up, ((1,), (1,)))
        xg[:, span, :] = back.astype(BF).reshape(PEERS, CAP, DIM)
        for k in range(3):
            cg[:, span, k * FFE : (k + 1) * FFE] = gated[k].reshape(PEERS, CAP, FFE)
        return _

    lax.fori_loop(0, LOCAL, expert, 0)

    def combine(b, _):
        hot = onehot(b)
        pick = jnp.concatenate([h.astype(F32) for h in hot], axis=0).astype(BF)
        out_ref[b] = dot(pick, cg[b], ((0,), (0,))).astype(BF)
        back_ref[b] = dot(pick, xg[b], ((0,), (0,))).astype(BF)
        lines = []
        for e in range(LOCAL):
            value = inners[e, pl.ds(b * CAP, CAP), :][:, :1]
            lines.append(jnp.sum(jnp.where(hot[e], value, 0.0), axis=0, keepdims=True))
        inner_ref[b] = jnp.concatenate(lines + [jnp.zeros((8 - LOCAL, TOK), F32)], axis=0)
        return _

    lax.fori_loop(0, PEERS, combine, 0)
    for e in (LOCAL - 2, LOCAL - 1):
        stored(e, e % 2)
    for e in range(LOCAL):
        for c in given(e, e % 2):
            c.wait_recv()


def run_experts(rows, cot, slots, gates, pieces):
    vmem = pl.BlockSpec(memory_space=pltpu.VMEM)
    piece = (LOCAL, 3 * ROWS, FFE)
    return pl.pallas_call(
        experts_kernel,
        out_shape=[
            jax.ShapeDtypeStruct((PEERS, TOK, DIM), BF),
            jax.ShapeDtypeStruct((PEERS, TOK, DIM), BF),
            jax.ShapeDtypeStruct((PEERS, 8, TOK), F32),
            jax.ShapeDtypeStruct((8,) + piece, BF),
            jax.ShapeDtypeStruct((8,) + piece, BF),
        ],
        in_specs=[vmem] * 4 + any_specs(1),
        out_specs=[vmem] * 3 + any_specs(2),
        scratch_shapes=[
            pltpu.VMEM((PEERS, LOCAL * CAP, DIM), BF),
            pltpu.VMEM((PEERS, LOCAL * CAP, DIM), BF),
            pltpu.VMEM((2, DP, 3 * ROWS, FFE), BF),
            pltpu.VMEM((2, DP, 3 * ROWS, FFE), BF),
            pltpu.VMEM((LOCAL, PEERS * CAP, 128), F32),
            pltpu.VMEM((LOCAL, PEERS * CAP, 128), F32),
            pltpu.SemaphoreType.DMA((2,)),
            pltpu.SemaphoreType.DMA((2, 16)),
            pltpu.SemaphoreType.DMA((LOCAL, 8)),
        ],
        compiler_params=pltpu.CompilerParams(
            collective_id=2, has_side_effects=True, vmem_limit_bytes=60 << 20
        ),
        cost_estimate=pl.CostEstimate(
            flops=20_000_000_000, bytes_accessed=60_000_000, transcendentals=700_000
        ),
    )(rows, cot, slots, gates, pieces)


def shift(value, move):
    pairs = []
    for d in range(DP):
        x, y, core = move(d // 8, d // 2 % 4, d % 2)
        pairs.append((d, (x % 2 * 4 + y % 4) * 2 + core % 2))
    return lax.ppermute(value, "dp", pairs)


def up(value):
    return shift(value, lambda x, y, c: (x, y + 1, c))


def down(value):
    return shift(value, lambda x, y, c: (x, y + 3, c))


def across(value):
    return shift(value, lambda x, y, c: (x + 1, y, c))


def other_core(value):
    return shift(value, lambda x, y, c: (x, y, c + 1))


def to_peers(blocks):
    return lax.all_to_all(blocks, "expert", split_axis=0, concat_axis=0, tiled=True)


def add(a, b):
    return (a.astype(F32) + b.astype(F32)).astype(BF)


def rms_scale(values):
    return lax.rsqrt(jnp.mean(values * values, axis=-1, keepdims=True) + epsilon)


def rope_tables(offsets, head_width):
    exponent = jnp.arange(head_width // 2, dtype=jnp.float32) * (2.0 / head_width)
    frequency = jnp.exp(-exponent * math.log(rope_base))
    phase_angles = offsets.astype(jnp.float32)[:, None] * frequency[None, :]
    return (jnp.cos(phase_angles)[:, None, :], jnp.sin(phase_angles)[:, None, :])


def rotate(values, cosine, sine_table):
    half = values.shape[-1] // 2
    first, second = values[..., :half], values[..., half:]
    return jnp.concatenate(
        [first * cosine - second * sine_table, second * cosine + first * sine_table], axis=-1
    )


def layout(lengths, group_count):
    seq_ends = jnp.cumsum(lengths)
    starts = seq_ends - lengths
    places = jnp.arange(group_count, dtype=jnp.int32)
    member = ((places[:, None] >= starts[None, :]) & (places[:, None] < seq_ends[None, :])).astype(
        jnp.int32
    )
    numbers = jnp.arange(lengths.shape[0], dtype=jnp.int32)
    segment = jnp.sum(member * numbers[None, :], axis=1)
    offsets = places - jnp.sum(member * starts[None, :], axis=1)
    return (segment, offsets)


def norm_back(values, row_scale, gain_vector, grad_normed):
    weighted = grad_normed * gain_vector
    return row_scale * weighted - values * row_scale**3 * jnp.mean(
        weighted * values, axis=-1, keepdims=True
    )


def by_peer(table):
    return jnp.pad(table.reshape(PEERS, LOCAL, TOK), ((0, 0), (0, 8 - LOCAL), (0, 0)))


def local(
    tokens,
    cotangent,
    seq_lengths,
    expert_ids,
    w_query,
    w_key,
    w_value,
    w_output,
    norm_one,
    norm_two,
    w_router,
    w_gate,
    w_up,
    w_down,
):
    score_scale = HEAD ** (-0.5)
    down_piece = w_down.reshape(LOCAL, 32, 3, FFE).transpose(0, 2, 1, 3).reshape(LOCAL, ROWS, FFE)
    piece = jnp.concatenate([w_gate, w_up, down_piece], axis=1)

    slices = jnp.concatenate(
        [
            w_query.reshape(12, PEERS, QS).transpose(1, 0, 2),
            w_key.reshape(12, PEERS, HEAD).transpose(1, 0, 2),
            w_value.reshape(12, PEERS, HEAD).transpose(1, 0, 2),
            jnp.broadcast_to(
                jnp.concatenate(
                    [
                        w_router,
                        norm_one[:, None],
                        norm_two[:, None],
                        jnp.zeros((12, SLICE - GAINS - 2), BF),
                    ],
                    axis=1,
                )[None],
                (PEERS, 12, SLICE - ROUTER),
            ),
        ],
        axis=2,
    )
    member = jnp.any(
        expert_ids[None, :, :] == jnp.arange(EXPERTS, dtype=jnp.int32)[:, None, None], axis=-1
    )
    before = jnp.arange(TOK)[:, None] < jnp.arange(TOK)[None, :]
    places = jnp.dot(member.astype(BF), before.astype(BF), preferred_element_type=F32)
    slot_table = jnp.where(member, places, -1.0)

    segment, offsets = layout(seq_lengths[0], GROUP)
    cosine, sine_table = rope_tables(offsets, HEAD)
    wide_cosine = jnp.tile(cosine[:, 0, :], (1, 4))
    wide_sine = jnp.tile(jnp.concatenate([-sine_table[:, 0, :], sine_table[:, 0, :]], axis=1), (1, 2))
    start = jnp.broadcast_to((jnp.arange(GROUP, dtype=jnp.int32) - offsets)[:, None], (GROUP, 128))
    (
        pieces,
        cot_all,
        slots_all,
        rows_all,
        gates_all,
        tokens_all,
        normed_all,
        slices_all,
        output_all,
        query,
        key,
        value,
        log_total,
        attended,
        middle,
        normed_two,
        gate_values,
    ) = first_phase(
        slices,
        w_output,
        tokens,
        cotangent,
        slot_table,
        by_peer(slot_table),
        piece,
        wide_cosine,
        wide_sine,
        start,
    )
    slices_all = slices_all.reshape(DIM, SLICE)
    output_all = output_all.reshape(DIM, DIM)
    qkv_all = slices_all[:, :ROUTER]
    gains = slices_all[:, GAINS : GAINS + 2].astype(F32).T
    gain_one, gain_two = gains[0], gains[1]
    router_all = slices_all[:, ROUTER:GAINS]
    inputs = tokens.astype(F32)
    inputs_all = tokens_all.reshape(GROUP, DIM).astype(F32)
    normed_all = normed_all.reshape(GROUP, DIM)
    scale_all = rms_scale(inputs_all)
    scale_two = rms_scale(middle)
    attended = attended.transpose(1, 0, 2).reshape(TOK, DIM)
    query = query.reshape(PEERS, REP, TOK, HEAD).transpose(0, 2, 1, 3).reshape(GROUP, REP, HEAD)
    log_total = log_total[:, :, 0].reshape(PEERS, REP, TOK).transpose(1, 0, 2).reshape(REP, GROUP, 1)
    places = jnp.arange(GROUP, dtype=jnp.int32)
    allowed = (segment[:, None] == segment[None, :]) & (places[None, :] <= places[:, None])
    scores = jnp.einsum("qrh,kh->rqk", query, key, preferred_element_type=F32) * score_scale
    probs = jnp.exp(jnp.where(allowed, scores, masked_score) - log_total)
    probs_low = probs.astype(BF)

    out_part, back_part, inner_part, keep, given = run_experts(
        rows_all, cot_all, slots_all, gates_all, pieces
    )
    back_all, inner_all = exchange([back_part, inner_part], ["exchange", "exchange"], 5, 38)

    sums = {s: add(keep[k], given[k]) for k, s in enumerate(SLOTS)}
    up_two, down_two = up(sums[(0, 2)]), down(sums[(1, 2)])
    far = (
        sums[(1, 0)].astype(F32)
        + up(sums[(1, 1)]).astype(F32)
        + down(add(sums[(1, 3)], down_two)).astype(F32)
    ).astype(BF)
    near = (
        sums[(0, 0)].astype(F32)
        + up(add(sums[(0, 1)], up_two)).astype(F32)
        + down(sums[(0, 3)]).astype(F32)
    )
    expert_grads = near + across(far).astype(F32)

    grad_normed_two = jnp.sum(back_all.astype(F32), axis=0)
    grad_gates = inner_all[:, :LOCAL, :].reshape(EXPERTS, TOK)
    grad_chosen = gate_values * (
        grad_gates - jnp.sum(gate_values * grad_gates, axis=0, keepdims=True)
    )
    grad_logits = grad_chosen.astype(BF)
    grad_out = cotangent.astype(F32)
    grad_router = lax.dot_general(
        normed_two, grad_logits, (((0,), (1,)), ((), ())), preferred_element_type=F32
    )
    grad_normed_two = grad_normed_two + lax.dot_general(
        grad_logits, router_all, (((0,), (1,)), ((), ())), preferred_element_type=F32
    )
    grad_gain_two = jnp.sum(grad_normed_two * middle * scale_two, axis=0)
    grad_middle = grad_out + norm_back(middle, scale_two, gain_two, grad_normed_two)
    grad_branch = grad_middle.astype(BF)
    grad_attended = lax.dot_general(
        grad_branch, output_all, (((1,), (1,)), ((), ())), preferred_element_type=F32
    ).astype(BF)
    grad_attended = grad_attended.reshape(TOK, PEERS, QS).transpose(1, 0, 2)
    (grad_attended,) = exchange([grad_attended], ["exchange"], 6)
    out_part, _ = lax.optimization_barrier((out_part, grad_attended))
    out_all = to_peers(out_part)
    grad_attended = grad_attended.reshape(GROUP, REP, HEAD)
    grad_output = lax.dot_general(
        attended, grad_branch, (((0,), (0,)), ((), ())), preferred_element_type=F32
    )

    grad_probs = jnp.einsum("qrh,kh->rqk", grad_attended, value, preferred_element_type=F32)
    grad_scores = (
        probs * (grad_probs - jnp.sum(probs * grad_probs, axis=-1, keepdims=True))
    ).astype(BF)
    grad_query = (
        jnp.einsum("rqk,kh->qrh", grad_scores, key, preferred_element_type=F32) * score_scale
    )
    grad_key = (
        jnp.einsum("rqk,qrh->kh", grad_scores, query, preferred_element_type=F32) * score_scale
    )
    grad_value = jnp.einsum("rqk,qrh->kh", probs_low, grad_attended, preferred_element_type=F32)
    grad_heads = rotate(
        jnp.concatenate([grad_query, grad_key[:, None, :]], axis=1), cosine, -sine_table
    ).reshape(GROUP, QS + HEAD)
    grad_qkv = jnp.concatenate([grad_heads, grad_value], axis=1).astype(BF)
    grad_slices = lax.dot_general(
        normed_all, grad_qkv, (((0,), (0,)), ((), ())), preferred_element_type=F32
    )
    grad_normed = lax.dot_general(
        grad_qkv, qkv_all, (((1,), (1,)), ((), ())), preferred_element_type=F32
    )
    grad_gain_one = jnp.sum(grad_normed * inputs_all * scale_all, axis=0)
    small = jnp.concatenate(
        [
            grad_slices.astype(BF),
            grad_router.astype(BF),
            grad_gain_one[:, None].astype(BF),
            grad_gain_two[:, None].astype(BF),
            jnp.zeros((DIM, SLICE - GAINS - 2), BF),
        ],
        axis=1,
    )
    normed_back, small_rows, output_rows = scatter_sum(
        [grad_normed.astype(BF).reshape(PEERS, TOK, DIM)],
        [small.reshape(DP, ROWS, SLICE), grad_output.astype(BF).reshape(DP, ROWS, DIM)],
        7,
    )
    mixed = middle + jnp.sum(out_all.astype(F32), axis=0)
    grad_tokens = grad_middle + norm_back(
        inputs, scale_all_own(scale_all), gain_one, jnp.sum(normed_back.astype(F32), axis=0)
    )
    small_own, output_own = exchange(
        [small_rows.reshape(PEERS, 12, SLICE), output_rows.reshape(PEERS, 12, DIM)],
        ["exchange", "exchange"],
        8,
    )
    own_sum = jnp.sum(small_own[:, :, ROUTER:], axis=0)
    return (
        mixed.astype(BF),
        grad_tokens,
        small_own[:, :, :QS].transpose(1, 0, 2).reshape(12, DIM),
        small_own[:, :, QS : QS + HEAD].transpose(1, 0, 2).reshape(12, KV_HEADS * HEAD),
        small_own[:, :, QS + HEAD : ROUTER].transpose(1, 0, 2).reshape(12, KV_HEADS * HEAD),
        jnp.sum(output_own, axis=0),
        own_sum[:, EXPERTS],
        own_sum[:, EXPERTS + 1],
        own_sum[:, :EXPERTS],
        expert_grads[:, :ROWS],
        expert_grads[:, ROWS : 2 * ROWS],
        expert_grads[:, 2 * ROWS :]
        .reshape(LOCAL, 3, 32, FFE)
        .transpose(0, 2, 1, 3)
        .reshape(LOCAL, 32, DIM),
    )


def scale_all_own(scale_all):
    return lax.dynamic_slice_in_dim(scale_all, lax.axis_index("expert") * TOK, TOK)


def solution(mesh):
    both = P(("dp", "expert"), None)
    line = P(("dp", "expert"))
    cube = P("expert", "dp", None)
    in_specs = (both, both, P("dp", None), both, both, both, both, both)
    in_specs = in_specs + (line, line, both, cube, cube, cube)
    out_specs = (both,) * 6 + (line, line, both, cube, cube, cube)
    return jax.shard_map(local, mesh=mesh, in_specs=in_specs, out_specs=out_specs, check_vma=False)
```

```python
import functools
import math

import jax
import jax.numpy as jnp
from jax import lax
from jax.experimental import pallas as pl
from jax.experimental.pallas import tpu as pltpu
from jax.sharding import PartitionSpec as P

HEADS = 24
KV_HEADS = 8
HEAD = 64
DIM = 1536
FFE = 512
EXPERTS = 40
LOCAL = 5
CAP = 32
TOK = 128
PEERS = 8
DP = 16
GROUP = TOK * PEERS
REP = HEADS // KV_HEADS
SLICE = 384
QS = REP * HEAD
ROWS = 96
ROUTER = QS + 2 * HEAD
GAINS = ROUTER + EXPERTS

epsilon = 1e-06
rope_base = 10000.0
masked_score = -1e30
MESH = pl.DeviceIdType.MESH
BF = jnp.bfloat16
F32 = jnp.float32

RELATIVE = ((2, 1), (2, 0), (1, 1), (3, 1), (0, 1), (1, 0), (3, 0))
SLOTS = ((0, 0), (1, 0), (0, 1), (0, 3), (1, 1), (1, 3), (0, 2), (1, 2))


def expert_peers():
    me = lax.axis_index("expert")
    z, x = me // 2, me % 2
    return me, [(z + rz) % 4 * 2 + (x + rx) % 2 for rz, rx in RELATIVE]


def dp_place():
    d = lax.axis_index("dp")
    return d // 8, (d // 2) % 4, d % 2


def dp_index(x, y, core):
    return (x % 2 * 4 + y % 4) * 2 + core % 2


def signal_all(expert_ids, dp_ids):
    barrier = pltpu.get_barrier_semaphore()
    for p in expert_ids:
        pl.semaphore_signal(barrier, inc=1, device_id={"expert": p}, device_id_type=MESH)
    for p in dp_ids:
        pl.semaphore_signal(barrier, inc=1, device_id={"dp": p}, device_id_type=MESH)
    pl.semaphore_wait(barrier, len(expert_ids) + len(dp_ids))


def any_specs(count):
    return [pl.BlockSpec(memory_space=pl.ANY)] * count


def expert_copies(ins, outs, modes, send, recv):
    me, peers = expert_peers()
    copies = []
    for r, p in enumerate(peers):
        for i, mode in enumerate(modes):
            copies.append(
                pltpu.make_async_remote_copy(
                    src_ref=ins[i] if mode == "gather" else ins[i].at[p],
                    dst_ref=outs[i].at[me],
                    send_sem=send.at[i, r],
                    recv_sem=recv.at[i, r],
                    device_id={"expert": p},
                    device_id_type=MESH,
                )
            )
    return copies


def own_copies(ins, outs, modes, sems):
    me = lax.axis_index("expert")
    return [
        pltpu.make_async_copy(
            ins[i] if mode == "gather" else ins[i].at[me], outs[i].at[me], sems.at[i]
        )
        for i, mode in enumerate(modes)
    ]


def lasting(us):
    return pl.CostEstimate(flops=us * 1_000_000_000, bytes_accessed=0, transcendentals=0)


class Gather:
    def __init__(self, src, out, send, recv, local):
        self.src, self.out, self.send, self.recv, self.local = src, out, send, recv, local
        me = lax.axis_index("expert")
        z, x = me // 2, me % 2

        def place(dz, dx):
            return (z + dz) % 4 * 2 + (x + dx) % 2

        self.me, self.across, self.up, self.down = me, place(0, 1), place(1, 0), place(3, 0)
        self.slots = [
            place(0, 1),
            place(3, 0),
            place(1, 0),
            place(3, 1),
            place(1, 1),
            place(2, 0),
            place(2, 1),
        ]
        self.started = []

    def copy(self, k, src, slot, target):
        c = pltpu.make_async_remote_copy(
            src_ref=src,
            dst_ref=self.out.at[slot],
            send_sem=self.send.at[k],
            recv_sem=self.recv.at[k],
            device_id={"expert": target},
            device_id_type=MESH,
        )
        c.start()
        self.started.append(c)

    def arrive(self, k):
        pltpu.make_async_remote_copy(
            src_ref=self.src,
            dst_ref=self.out.at[self.slots[k]],
            send_sem=self.send.at[k],
            recv_sem=self.recv.at[k],
            device_id={"expert": self.up},
            device_id_type=MESH,
        ).wait_recv()

    def begin(self):
        self.copy(0, self.src, self.me, self.across)
        self.copy(1, self.src, self.me, self.up)
        self.copy(2, self.src, self.me, self.down)
        self.own = pltpu.make_async_copy(self.src, self.out.at[self.me], self.local)
        self.own.start()

    def first(self):
        self.arrive(0)
        self.copy(3, self.out.at[self.slots[0]], self.slots[0], self.up)
        self.copy(4, self.out.at[self.slots[0]], self.slots[0], self.down)

    def second(self):
        self.arrive(1)
        self.copy(5, self.out.at[self.slots[1]], self.slots[1], self.up)

    def third(self):
        self.arrive(4)
        self.copy(6, self.out.at[self.slots[4]], self.slots[4], self.down)

    def finish(self):
        for k in (2, 3, 5, 6):
            self.arrive(k)
        for c in self.started:
            c.wait_send()
        self.own.wait()


class Dense:
    def __init__(self, rows, out, send, recv, local):
        self.rows, self.out, self.send, self.recv, self.local = rows, out, send, recv, local
        x, y, core = dp_place()
        self.x, self.y, self.core = x, y, core
        self.mine = dp_index(x, y, core)
        self.to_x, self.to_up = dp_index(x + 1, y, core), dp_index(x, y + 1, core)
        self.to_down, self.to_core = dp_index(x, y + 3, core), dp_index(x, y, core + 1)
        self.slots = [dp_index(x + rx, y + ry, core) for rx, ry in SLOTS]
        self.started = []

    def descriptor(self, k, src, slot, target):
        return pltpu.make_async_remote_copy(
            src_ref=src,
            dst_ref=self.out.at[slot],
            send_sem=self.send.at[k],
            recv_sem=self.recv.at[k],
            device_id={"dp": target},
            device_id_type=MESH,
        )

    def copy(self, k, slot, target, src=None):
        c = self.descriptor(k, self.out.at[slot] if src is None else src, slot, target)
        c.start()
        self.started.append(c)

    def arrive(self, k, slot):
        self.descriptor(k, self.out.at[slot], slot, self.to_x).wait_recv()

    def share(self, k):
        self.copy(8 + k, self.slots[k], self.to_core)

    def begin(self):
        self.copy(1, self.mine, self.to_x, self.rows)
        self.copy(3, self.mine, self.to_up, self.rows)
        self.copy(2, self.mine, self.to_down, self.rows)
        self.copy(8, self.mine, self.to_core, self.rows)
        self.own = pltpu.make_async_copy(self.rows, self.out.at[self.mine], self.local)
        self.own.start()

    def first(self):
        self.arrive(1, self.slots[1])
        self.copy(5, self.slots[1], self.to_up)
        self.copy(4, self.slots[1], self.to_down)
        self.share(1)
        self.arrive(3, self.slots[3])
        self.copy(6, self.slots[3], self.to_up)
        self.share(3)
        self.arrive(2, self.slots[2])
        self.share(2)

    def second(self):
        self.arrive(4, self.slots[4])
        self.copy(7, self.slots[4], self.to_down)
        self.share(4)
        self.arrive(5, self.slots[5])
        self.share(5)

    def third(self):
        for k in (6, 7):
            self.arrive(k, self.slots[k])
            self.share(k)

    def finish(self):
        for k, (rx, ry) in enumerate(SLOTS):
            self.arrive(8 + k, dp_index(self.x + rx, self.y + ry, self.core + 1))
        for c in self.started:
            c.wait_send()
        self.own.wait()


class Pieces:
    parts = ((0, 3), (3, 1), (4, 1))

    def __init__(self, piece, out, send, recv, local):
        self.piece, self.out, self.send, self.recv, self.local = piece, out, send, recv, local
        x, y, core = dp_place()
        self.x, self.y, self.core = x, y, core
        self.mine = dp_index(x, y, core)
        self.targets = {
            "x": dp_index(x + 1, y, core),
            "up": dp_index(x, y + 1, core),
            "down": dp_index(x, y + 3, core),
            "core": dp_index(x, y, core + 1),
        }
        self.slots = [dp_index(x + rx, y + ry, core) for rx, ry in SLOTS]
        self.started = []

    def descriptor(self, g, k, src, slot, target):
        first, count = self.parts[g]
        return pltpu.make_async_remote_copy(
            src_ref=src.at[pl.ds(first, count)],
            dst_ref=self.out.at[slot, pl.ds(first, count)],
            send_sem=self.send.at[g, k],
            recv_sem=self.recv.at[g, k],
            device_id={"dp": target},
            device_id_type=MESH,
        )

    def move(self, g, k, where, source=0):
        src = self.piece if source == 0 else self.out.at[self.slots[source]]
        c = self.descriptor(g, k, src, self.slots[source], self.targets[where])
        c.start()
        self.started.append(c)

    def arrive(self, g, k, share=True):
        slot = self.slots[k]
        self.descriptor(g, k, self.out.at[slot], slot, self.targets["x"]).wait_recv()
        if share:
            self.move(g, 8 + k, "core", k)

    def begin(self):
        for g in range(3):
            self.move(g, 8, "core")
        self.own = pltpu.make_async_copy(self.piece, self.out.at[self.mine], self.local)
        self.own.start()

    def finish(self):
        for g in range(3):
            for k, (rx, ry) in enumerate(SLOTS):
                slot = dp_index(self.x + rx, self.y + ry, self.core + 1)
                self.descriptor(
                    g, 8 + k, self.out.at[slot], slot, self.targets["x"]
                ).wait_recv()
        for c in self.started:
            c.wait_send()
        self.own.wait()


def first_kernel(*refs):
    (slices, output, tokens, cot, member_ref, slot_send, piece, cos_ref, sin_ref, start_ref) = refs[
        :10
    ]
    (
        pieces_out,
        cot_all,
        slots_all,
        rows_all,
        gates_all,
        tokens_out,
        normed_out,
        small_out,
        output_out,
        query_ref,
        key_ref,
        value_ref,
        log_ref,
        attended_ref,
        middle_ref,
        normed_two_ref,
        gates_ref,
    ) = refs[10:27]
    (
        small_in,
        output_in,
        small_rows,
        output_rows,
        small,
        dense,
        tokens_in,
        normed,
        att_send,
        gate_send,
        s_small,
        s_dense,
        s_piece,
        r_small,
        r_dense,
        r_piece,
        s_gather,
        r_gather,
        s_direct,
        r_direct,
        l_sem,
    ) = refs[27:]
    _, peers = expert_peers()
    x, y, core = dp_place()
    signal_all(
        peers,
        [
            dp_index(x + 1, y, core),
            dp_index(x, y + 1, core),
            dp_index(x, y + 3, core),
            dp_index(x, y, core + 1),
        ],
    )

    def direct(i, src, out, mode):
        part = expert_copies(
            [src], [out], [mode], s_direct.at[pl.ds(i, 1)], r_direct.at[pl.ds(i, 1)]
        ) + own_copies([src], [out], [mode], l_sem.at[pl.ds(i, 1)])
        for c in part:
            c.start()
        return part

    def settle(part):
        for c in part:
            c.wait()

    saved = []

    def save(src, dst, i):
        c = pltpu.make_async_copy(src, dst, l_sem.at[i])
        c.start()
        saved.append(c)

    parts = [
        direct(0, slices, small_in, "exchange"),
        direct(1, output, output_in, "gather"),
        direct(2, slot_send, slots_all, "exchange"),
    ]
    tokens_gather = Gather(tokens, tokens_in, s_gather.at[0], r_gather.at[0], l_sem.at[5])
    tokens_gather.begin()
    experts = Pieces(piece, pieces_out, s_piece, r_piece, l_sem.at[6])
    experts.begin()
    for g in (1, 2):
        experts.move(g, 3, "up")
        experts.move(g, 2, "down")

    weights = []
    for i, (landed, rows, out) in enumerate(
        ((small_in, small_rows, small), (output_in, output_rows, dense))
    ):
        settle(parts[i])
        rows[...] = jnp.concatenate([landed[j] for j in range(PEERS)], axis=0)
        weights.append(Dense(rows, out, s_dense.at[i], r_dense.at[i], l_sem.at[7 + i]))
        weights[i].begin()
    experts.move(0, 1, "x")
    for g in (1, 2):
        experts.move(g, 1, "x")
    tokens_gather.first()
    for w in weights:
        w.first()
    tokens_gather.second()
    for w in weights:
        w.second()
    tokens_gather.third()
    experts.move(0, 3, "up")
    experts.move(0, 2, "down")
    cot_gather = Gather(cot, cot_all, s_gather.at[1], r_gather.at[1], l_sem.at[9])
    cot_gather.begin()
    for w in weights:
        w.third()
    weights[0].finish()
    tokens_gather.finish()

    for g in (1, 2):
        experts.arrive(g, 3)
        experts.arrive(g, 2)
    experts.move(1, 6, "up", 3)
    experts.move(2, 6, "down", 2)
    for g in (1, 2):
        experts.move(g, 5, "x", 3)
        experts.move(g, 4, "x", 2)

    w_small = small[...].reshape(DIM, SLICE)
    pick = (
        lax.broadcasted_iota(jnp.int32, (8, SLICE), 1)
        == lax.broadcasted_iota(jnp.int32, (8, SLICE), 0) + GAINS
    )
    gains = dot(pick.astype(F32).astype(BF), w_small, ((1,), (1,)))
    gain_one, gain_two = gains[0:1], gains[1:2]

    def project(i, _):
        values = tokens_in[pl.ds(2 * i, 2)].reshape(2 * TOK, DIM).astype(F32)
        scale = lax.rsqrt(jnp.mean(values * values, axis=-1, keepdims=True) + epsilon)
        low = (values * scale * gain_one).astype(BF)
        normed[pl.ds(2 * i, 2)] = low.reshape(2, TOK, DIM)
        qkv = dot(low, small[...].reshape(DIM, SLICE), ((1,), (0,)))
        span = pl.ds(pl.multiple_of(i * 2 * TOK, 2 * TOK), 2 * TOK)
        cosine, sine = cos_ref[span, :], sin_ref[span, :]
        lane = lax.broadcasted_iota(jnp.int32, (2 * TOK, 128), 1)
        turned = []
        for h in range(2):
            v = qkv[:, 128 * h : 128 * h + 128]
            other = jnp.where(lane % HEAD < HEAD // 2, pltpu.roll(v, 96, 1), pltpu.roll(v, 32, 1))
            turned.append((v * cosine + other * sine).astype(BF))
        heads = (turned[0][:, :HEAD], turned[0][:, HEAD:], turned[1][:, :HEAD])
        for b in range(2):
            for h in range(REP):
                query_ref[2 * i + b, h * TOK : (h + 1) * TOK, :] = heads[h][
                    b * TOK : (b + 1) * TOK
                ]
        key_ref[span, :] = turned[1][:, HEAD:]
        value_ref[span, :] = qkv[:, QS + HEAD : ROUTER].astype(BF)
        return _

    lax.fori_loop(0, 4, project, 0)
    save(tokens_in, tokens_out, 10)
    save(normed, normed_out, 11)
    save(small, small_out, 12)

    def attend(width, i, _):
        scores = dot(query_ref[i], key_ref[0:width, :], ((1,), (1,))) * HEAD ** (-0.5)
        keys = lax.broadcasted_iota(jnp.int32, (TOK, width), 1)
        rows = lax.broadcasted_iota(jnp.int32, (TOK, width), 0) + i * TOK
        begins = start_ref[pl.ds(pl.multiple_of(i * TOK, TOK), TOK), :][:, :1]
        allowed = (keys <= rows) & (keys >= begins)
        scores = jnp.where(allowed[None], scores.reshape(REP, TOK, width), masked_score)
        top = jnp.max(scores, axis=-1, keepdims=True)
        terms = jnp.exp(scores - top)
        total = jnp.sum(terms, axis=-1, keepdims=True)
        probs = (terms / total).astype(BF).reshape(REP * TOK, width)
        out = dot(probs, value_ref[0:width, :], ((1,), (0,))).astype(BF)
        att_send[i] = jnp.concatenate([out[h * TOK : (h + 1) * TOK] for h in range(REP)], axis=1)
        log_ref[i] = jnp.broadcast_to(
            (top + jnp.log(total)).reshape(REP * TOK, 1), (REP * TOK, 128)
        )
        return _

    experts.arrive(0, 1)
    experts.move(0, 5, "up", 1)
    experts.move(0, 4, "down", 1)
    cot_gather.first()
    cot_gather.second()
    lax.fori_loop(0, 4, functools.partial(attend, GROUP // 2), 0)
    for g in (1, 2):
        experts.arrive(g, 1)
    cot_gather.third()
    lax.fori_loop(4, 8, functools.partial(attend, GROUP), 0)
    parts.append(direct(3, att_send, attended_ref, "exchange"))
    experts.arrive(0, 3)
    experts.move(0, 6, "up", 3)
    experts.arrive(0, 2)
    for g in (1, 2):
        experts.arrive(g, 4)
        experts.arrive(g, 5)
    settle(parts[3])
    weights[1].finish()
    save(dense, output_out, 13)

    me = lax.axis_index("expert")
    middle = tokens_in[me].astype(F32)
    for j in range(PEERS):
        middle = middle + dot(
            attended_ref[j], dense[2 * j : 2 * j + 2].reshape(QS, DIM), ((1,), (0,))
        )
    middle_ref[...] = middle
    scale_two = lax.rsqrt(jnp.mean(middle * middle, axis=-1, keepdims=True) + epsilon)
    normed_two = (middle * scale_two * gain_two).astype(BF)
    normed_two_ref[...] = normed_two
    rows_gather = Gather(normed_two_ref, rows_all, s_gather.at[2], r_gather.at[2], l_sem.at[14])
    rows_gather.begin()
    logits = dot(small[:, :, 256:SLICE].reshape(DIM, SLICE - 256), normed_two, ((0,), (1,)))
    logits = logits[ROUTER - 256 : GAINS - 256]
    member = member_ref[...] >= 0.0
    chosen = jnp.where(member, logits, masked_score)
    weight = jnp.where(member, jnp.exp(chosen - jnp.max(chosen, axis=0, keepdims=True)), 0.0)
    gates_ref[...] = weight / jnp.sum(weight, axis=0, keepdims=True)
    gate_send[...] = jnp.zeros_like(gate_send)
    for j in range(PEERS):
        gate_send[j, 0:LOCAL, :] = gates_ref[LOCAL * j : LOCAL * (j + 1), :]
    parts.append(direct(4, gate_send, gates_all, "exchange"))

    rows_gather.first()
    rows_gather.second()
    experts.arrive(0, 4)
    experts.move(0, 7, "down", 4)
    experts.arrive(0, 5)
    rows_gather.third()
    for g in (1, 2):
        experts.arrive(g, 6)
        experts.move(g, 7, "x", 6)
    cot_gather.finish()
    rows_gather.finish()
    settle(parts[2])
    settle(parts[4])
    experts.arrive(0, 6)
    for g in (0, 1, 2):
        experts.arrive(g, 7)
    experts.finish()
    for c in saved:
        c.wait()


def first_phase(slices, output, tokens, cot, member, slot_send, piece, cosine, sine, start):
    hbm, vmem = pl.BlockSpec(memory_space=pl.ANY), pl.BlockSpec(memory_space=pltpu.VMEM)
    shape = jax.ShapeDtypeStruct
    blocks = (PEERS, TOK, DIM)
    outs = [
        (shape((DP,) + piece.shape, BF), hbm),
        (shape(blocks, BF), hbm),
        (shape((PEERS, 8, TOK), F32), hbm),
        (shape(blocks, BF), hbm),
        (shape((PEERS, 8, TOK), F32), hbm),
        (shape(blocks, BF), hbm),
        (shape(blocks, BF), hbm),
        (shape((DP, ROWS, SLICE), BF), hbm),
        (shape((DP, ROWS, DIM), BF), hbm),
        (shape((PEERS, REP * TOK, HEAD), BF), vmem),
        (shape((GROUP, HEAD), BF), vmem),
        (shape((GROUP, HEAD), BF), vmem),
        (shape((PEERS, REP * TOK, 128), F32), vmem),
        (shape((PEERS, TOK, QS), BF), vmem),
        (shape((TOK, DIM), F32), vmem),
        (shape((TOK, DIM), BF), vmem),
        (shape((EXPERTS, TOK), F32), vmem),
    ]
    dma = pltpu.SemaphoreType.DMA
    return pl.pallas_call(
        first_kernel,
        out_shape=[o[0] for o in outs],
        in_specs=[hbm] * 4 + [vmem] + [hbm] * 2 + [vmem] * 3,
        out_specs=[o[1] for o in outs],
        scratch_shapes=[
            pltpu.VMEM((PEERS, 12, SLICE), BF),
            pltpu.VMEM((PEERS, 12, DIM), BF),
            pltpu.VMEM((ROWS, SLICE), BF),
            pltpu.VMEM((ROWS, DIM), BF),
            pltpu.VMEM((DP, ROWS, SLICE), BF),
            pltpu.VMEM((DP, ROWS, DIM), BF),
            pltpu.VMEM(blocks, BF),
            pltpu.VMEM(blocks, BF),
            pltpu.VMEM((PEERS, TOK, QS), BF),
            pltpu.VMEM((PEERS, 8, TOK), F32),
            dma((1,)),
            dma((2, 16)),
            dma((3, 16)),
            dma((1,)),
            dma((2, 16)),
            dma((3, 16)),
            dma((3, 7)),
            dma((3, 7)),
            dma((5, 7)),
            dma((5, 7)),
            dma((15,)),
        ],
        compiler_params=pltpu.CompilerParams(
            collective_id=1, has_side_effects=True, vmem_limit_bytes=50 << 20
        ),
        cost_estimate=lasting(120),
    )(slices, output, tokens, cot, member, slot_send, piece, cosine, sine, start)


def dot(a, b, contract):
    return lax.dot_general(a, b, ((contract[0], contract[1]), ((), ())), preferred_element_type=F32)


class Reduce:
    def __init__(self, src, own, landed, send, recv):
        self.src, self.own, self.landed = src, own, landed
        self.send, self.recv = send, recv
        me = lax.axis_index("expert")
        z, x = me // 2, me % 2
        self.place = lambda dz, dx: (z + dz) % 4 * 2 + (x + dx) % 2
        self.targets = {"up": self.place(1, 0), "down": self.place(3, 0), "x": self.place(0, 1)}
        self.started = []

    def copy(self, k, src, where):
        c = pltpu.make_async_remote_copy(
            src_ref=src,
            dst_ref=self.landed.at[k],
            send_sem=self.send.at[k],
            recv_sem=self.recv.at[k],
            device_id={"expert": self.targets[where]},
            device_id_type=MESH,
        )
        c.start()
        self.started.append(c)

    def got(self, k):
        pltpu.make_async_remote_copy(
            src_ref=self.landed.at[k],
            dst_ref=self.landed.at[k],
            send_sem=self.send.at[k],
            recv_sem=self.recv.at[k],
            device_id={"expert": self.targets["x"]},
            device_id_type=MESH,
        ).wait_recv()
        return self.landed[k].astype(F32)

    def begin(self):
        self.copy(0, self.src.at[self.place(2, 1)], "up")
        self.copy(1, self.src.at[self.place(2, 0)], "down")
        self.copy(3, self.src.at[self.place(3, 1)], "down")

    def relay(self):
        self.landed[0] = (self.own(1, 1) + self.got(0)).astype(BF)
        self.copy(2, self.landed.at[0], "up")
        self.copy(4, self.src.at[self.place(1, 0)], "up")
        self.landed[1] = (self.own(3, 0) + self.got(1)).astype(BF)
        self.copy(5, self.landed.at[1], "down")

    def cross(self):
        self.landed[2] = (self.own(0, 1) + self.got(2) + self.got(3)).astype(BF)
        self.copy(6, self.landed.at[2], "x")

    def total(self):
        return self.own(0, 0) + self.got(4) + self.got(5) + self.got(6)

    def finish(self):
        for c in self.started:
            c.wait_send()


class DenseSum:
    def __init__(self, grads, theirs, landed, send, recv):
        self.grads, self.theirs, self.landed, self.send, self.recv = grads, theirs, landed, send, recv
        x, y, core = dp_place()
        self.targets = {
            "x": dp_index(x + 1, y, core),
            "up": dp_index(x, y + 1, core),
            "down": dp_index(x, y + 3, core),
            "core": dp_index(x, y, core + 1),
        }
        self.slots = [dp_index(x + rx, y + ry, core) for rx, ry in SLOTS]
        self.others = [dp_index(x + rx, y + ry, core + 1) for rx, ry in SLOTS]
        self.started = []

    def descriptor(self, k, src, dst, where):
        return pltpu.make_async_remote_copy(
            src_ref=src,
            dst_ref=dst,
            send_sem=self.send.at[k],
            recv_sem=self.recv.at[k],
            device_id={"dp": self.targets[where]},
            device_id_type=MESH,
        )

    def copy(self, k, src, dst, where):
        c = self.descriptor(k, src, dst, where)
        c.start()
        self.started.append(c)

    def begin(self):
        for k in (6, 7, 4, 5, 2, 3, 1, 0):
            self.copy(8 + k, self.grads.at[self.others[k]], self.theirs.at[k], "core")

    def got(self, k):
        self.descriptor(k, self.landed.at[k], self.landed.at[k], "x").wait_recv()
        return self.landed[k].astype(F32)

    def both(self, k):
        self.descriptor(8 + k, self.theirs.at[k], self.theirs.at[k], "core").wait_recv()
        return self.grads[self.slots[k]].astype(F32) + self.theirs[k].astype(F32)

    def put(self, k, value, j, where):
        self.grads[self.slots[k]] = value.astype(BF)
        self.copy(j, self.grads.at[self.slots[k]], self.landed.at[j], where)

    def first(self):
        self.put(6, self.both(6), 0, "up")
        self.put(7, self.both(7), 1, "down")
        self.put(4, self.both(4), 2, "up")

    def second(self):
        self.put(5, self.both(5) + self.got(1), 3, "down")
        self.put(2, self.both(2) + self.got(0), 4, "up")
        self.put(3, self.both(3), 5, "down")

    def third(self):
        self.put(1, self.both(1) + self.got(2) + self.got(3), 6, "x")

    def total(self):
        return self.both(0) + self.got(4) + self.got(5) + self.got(6)

    def finish(self):
        for c in self.started:
            c.wait_send()


class ExpertSum:
    def __init__(self, keep, given, near, far, stage, sends, far_sends, ends, s_near, r_near, s_far, r_far, l_sem):
        self.keep, self.given, self.near, self.far, self.stage = keep, given, near, far, stage
        self.sends, self.far_sends, self.ends = sends, far_sends, ends
        self.s_near, self.r_near, self.s_far, self.r_far, self.l_sem = s_near, r_near, s_far, r_far, l_sem
        x, y, core = dp_place()
        self.targets = {
            "x": dp_index(x + 1, y, core),
            "up": dp_index(x, y + 1, core),
            "down": dp_index(x, y + 3, core),
        }
        self.started = []

    def descriptor(self, src, dst, send, recv, where):
        return pltpu.make_async_remote_copy(
            src_ref=src,
            dst_ref=dst,
            send_sem=send,
            recv_sem=recv,
            device_id={"dp": self.targets[where]},
            device_id_type=MESH,
        )

    def add(self, refs, out, count):
        def load(e):
            return [
                pltpu.make_async_copy(r.at[e], self.stage.at[e % 2, i], self.l_sem.at[e % 2, i])
                for i, r in enumerate(refs)
            ]

        for c in load(0):
            c.start()
        for e in range(count):
            if e + 1 < count:
                for c in load(e + 1):
                    c.start()
            for c in load(e):
                c.wait()
            acc = self.stage[e % 2, 0].astype(F32)
            for i in range(1, len(refs)):
                acc = acc + self.stage[e % 2, i].astype(F32)
            out[e] = acc.astype(out.dtype)

    def parts(self, k, first, count):
        span = pl.ds(first, count)
        return [self.keep.at[k, span], self.given.at[k, span]]

    def near_send(self, k, j, where, more=()):
        for i in more:
            self.near_got(i)
        out = self.sends.at[j]
        self.add(self.parts(k, 0, 3) + [self.near.at[i] for i in more], out, 3)
        c = self.descriptor(out, self.near.at[j], self.s_near.at[j], self.r_near.at[j], where)
        c.start()
        self.started.append(c)

    def near_got(self, j):
        self.descriptor(
            self.near.at[j], self.near.at[j], self.s_near.at[j], self.r_near.at[j], "x"
        ).wait_recv()

    def far_send(self, k, j, where, which=(0, 1), more=()):
        for i in which:
            for m in more:
                if m < 4 or m == 4 + i:
                    self.far_got(m, i)
            out = self.far_sends.at[j, pl.ds(i, 1)]
            self.add(
                self.parts(k, 3 + i, 1)
                + [self.far.at[m, pl.ds(i, 1)] for m in more if m < 4 or m == 4 + i],
                out,
                1,
            )
            c = self.descriptor(
                out,
                self.far.at[j, pl.ds(i, 1)],
                self.s_far.at[j, i],
                self.r_far.at[j, i],
                where,
            )
            c.start()
            self.started.append(c)

    def far_got(self, j, i):
        ref = self.far.at[j, pl.ds(i, 1)]
        self.descriptor(ref, ref, self.s_far.at[j, i], self.r_far.at[j, i], "x").wait_recv()

    def near_end(self):
        for j in (4, 5, 6):
            self.near_got(j)
        self.add(
            self.parts(0, 0, 3) + [self.near.at[j] for j in (4, 5, 6)],
            self.ends,
            3,
        )

    def far_end(self):
        for j in (0, 6, 7):
            for i in range(2):
                self.far_got(j, i)
        self.add(
            self.parts(0, 3, 2) + [self.far.at[j] for j in (0, 6, 7)], self.ends, 2
        )

    def finish(self):
        for c in self.started:
            c.wait_send()


def last_kernel(*refs):
    (
        back_part,
        inner_part,
        out_part,
        keep,
        given,
        tokens_all,
        normed_all,
        small_hbm,
        dense_hbm,
        tokens,
        cot,
        gates_ref,
        middle_ref,
        normed_two_ref,
        attended_ref,
        query_ref,
        key_ref,
        value_ref,
        log_ref,
        cos_ref,
        sin_ref,
        start_ref,
    ) = refs[:22]
    mixed_ref, grad_tokens_ref, expert_ref, small_own, output_own, near, far = refs[22:29]
    (
        inner_in,
        gates_grad,
        logits_grad,
        small,
        dense,
        grad_small,
        normed,
        token_rows,
        grad_normed,
        att_send,
        att_in,
        grad_query,
        grad_key,
        grad_value,
        grad_qkv,
        gain_sum,
        grad_middle_ref,
        z_own,
        z_landed,
        y_landed,
        stage,
        sends,
        far_sends,
        ends,
        small_theirs,
        small_landed,
        dense_theirs,
        dense_landed,
        small_cut,
        dense_cut,
        dense_in,
        s_direct,
        r_direct,
        s_reduce,
        r_reduce,
        s_dense,
        r_dense,
        s_near,
        r_near,
        s_far,
        r_far,
        l_sem,
        l_add,
    ) = refs[29:]
    _, peers = expert_peers()
    x, y, core = dp_place()
    me = lax.axis_index("expert")
    signal_all(
        peers,
        [
            dp_index(x + 1, y, core),
            dp_index(x, y + 1, core),
            dp_index(x, y + 3, core),
            dp_index(x, y, core + 1),
        ],
    )

    def direct(i, src, out, mode):
        part = expert_copies(
            [src], [out], [mode], s_direct.at[pl.ds(i, 1)], r_direct.at[pl.ds(i, 1)]
        ) + own_copies([src], [out], [mode], l_sem.at[pl.ds(i, 1)])
        for c in part:
            c.start()
        return part

    def settle(part):
        for c in part:
            c.wait()

    def load(src, dst, i):
        c = pltpu.make_async_copy(src, dst, l_sem.at[i])
        c.start()
        return c

    OWN = ((1, 1), (3, 0), (0, 1), (0, 0))

    def own_blocks(reduce, src, base):
        return [
            load(src.at[reduce.place(*d)], z_own.at[i], base + i) for i, d in enumerate(OWN)
        ]

    def from_own(dz, dx):
        return z_own[OWN.index((dz, dx))].astype(F32)

    back = Reduce(back_part, from_own, z_landed, s_reduce.at[0], r_reduce.at[0])
    back.begin()
    loads = own_blocks(back, back_part, 8)
    inner = direct(0, inner_part, inner_in, "exchange")
    loads_small = load(small_hbm, small, 4)
    loads_dense = load(dense_hbm, dense, 5)
    loads_normed = load(normed_all, normed, 6)
    experts = ExpertSum(
        keep, given, near, far, stage, sends, far_sends, ends, s_near, r_near, s_far, r_far, l_add
    )
    experts.near_send(6, 0, "up")
    experts.near_send(7, 1, "down")
    settle(loads)
    back.relay()
    experts.far_send(7, 3, "x")
    experts.far_send(4, 1, "x")
    experts.near_send(4, 2, "up")
    back.cross()
    experts.far_send(6, 4, "up", (0,), (3,))
    experts.far_send(6, 5, "down", (1,), (3,))
    experts.near_send(5, 3, "down", (1,))
    experts.near_send(2, 4, "up", (0,))
    settle(inner)
    settle([loads_small, loads_dense])

    for j in range(PEERS):
        gates_grad[LOCAL * j : LOCAL * (j + 1), :] = inner_in[j, 0:LOCAL, :]
    gates = gates_ref[...]
    grad_gates = gates_grad[...]
    logits_grad[...] = jnp.zeros_like(logits_grad)
    logits_grad[ROUTER - 256 : GAINS - 256, :] = gates * (
        grad_gates - jnp.sum(gates * grad_gates, axis=0, keepdims=True)
    )
    pick = (
        lax.broadcasted_iota(jnp.int32, (8, SLICE), 1)
        == lax.broadcasted_iota(jnp.int32, (8, SLICE), 0) + GAINS
    )
    gains = dot(pick.astype(F32).astype(BF), small[...].reshape(DIM, SLICE), ((1,), (1,)))
    gain_one, gain_two = gains[0:1], gains[1:2]
    grad_logits = logits_grad[...].astype(BF)
    router = small[:, :, 256:SLICE].reshape(DIM, SLICE - 256)
    grad = back.total() + dot(grad_logits, router, ((0,), (1,)))
    middle = middle_ref[...]
    scale_two = lax.rsqrt(jnp.mean(middle * middle, axis=-1, keepdims=True) + epsilon)
    gain_sum[0] = jnp.sum((grad * middle * scale_two).reshape(TOK // 8, 8, DIM), axis=0)
    grad_middle = cot[...].astype(F32) + norm_back(middle, scale_two, gain_two, grad)
    grad_middle_ref[...] = grad_middle
    grad_branch = grad_middle.astype(BF)
    for j in range(PEERS):
        att_send[j] = dot(
            grad_branch, dense[2 * j : 2 * j + 2].reshape(QS, DIM), ((1,), (1,))
        ).astype(BF)
    back.finish()
    exchanged = direct(1, att_send, att_in, "exchange")
    experts.far_send(5, 2, "x")
    for j in range(PEERS):
        dense[2 * j : 2 * j + 2] = (
            dot(attended_ref[j], grad_branch, ((0,), (0,))).astype(BF).reshape(2, ROWS, DIM)
        )
    experts.near_send(3, 5, "down")
    settle(exchanged)
    out = Reduce(out_part, from_own, y_landed, s_reduce.at[1], r_reduce.at[1])
    out.begin()
    loads = own_blocks(out, out_part, 8)
    sums = [
        DenseSum(dense, dense_theirs, dense_landed, s_dense.at[0], r_dense.at[0]),
        DenseSum(grad_small, small_theirs, small_landed, s_dense.at[1], r_dense.at[1]),
    ]
    sums[0].begin()
    experts.far_send(1, 0, "x")

    grad_key[...] = jnp.zeros_like(grad_key)
    grad_value[...] = jnp.zeros_like(grad_value)

    def attend(width, i, _):
        queries = query_ref[i]
        incoming = att_in[i]
        incoming = jnp.concatenate(
            [incoming[:, h * HEAD : (h + 1) * HEAD] for h in range(REP)], axis=0
        )
        scores = dot(queries, key_ref[0:width, :], ((1,), (1,))) * HEAD ** (-0.5)
        keys = lax.broadcasted_iota(jnp.int32, (TOK, width), 1)
        rows = lax.broadcasted_iota(jnp.int32, (TOK, width), 0) + i * TOK
        begins = start_ref[pl.ds(pl.multiple_of(i * TOK, TOK), TOK), :][:, :1]
        allowed = (keys <= rows) & (keys >= begins)
        scores = jnp.where(allowed[None], scores.reshape(REP, TOK, width), masked_score)
        probs = jnp.exp(scores.reshape(REP * TOK, width) - log_ref[i][:, :1])
        grad_probs = dot(incoming, value_ref[0:width, :], ((1,), (1,)))
        inner_sum = jnp.sum(probs * grad_probs, axis=-1, keepdims=True)
        grad_scores = (probs * (grad_probs - inner_sum)).astype(BF)
        grad_query[i] = dot(grad_scores, key_ref[0:width, :], ((1,), (0,))) * HEAD ** (-0.5)
        grad_key[0:width, :] += dot(grad_scores, queries, ((0,), (0,))) * HEAD ** (-0.5)
        grad_value[0:width, :] += dot(probs.astype(BF), incoming, ((0,), (0,)))
        return _

    lax.fori_loop(0, 4, functools.partial(attend, GROUP // 2), 0)
    settle(loads)
    out.relay()
    experts.far_send(2, 6, "up", (0, 1), (1, 4))
    experts.far_send(3, 7, "down", (0, 1), (2, 5))
    experts.near_send(1, 6, "x", (2, 3))
    lax.fori_loop(4, 8, functools.partial(attend, GROUP), 0)
    out.cross()

    settle([loads_normed])
    gain_sum[1] = jnp.zeros((8, DIM), F32)

    def project(i, _):
        span = pl.ds(pl.multiple_of(i * 2 * TOK, 2 * TOK), 2 * TOK)
        rows = load(tokens_all.at[pl.ds(2 * i, 2)], token_rows, 7)
        cosine, sine = cos_ref[span, :], sin_ref[span, :]
        lane = lax.broadcasted_iota(jnp.int32, (2 * TOK, 128), 1)
        heads = [
            jnp.concatenate(
                [grad_query[2 * i + b, h * TOK : (h + 1) * TOK, :] for b in range(2)], axis=0
            )
            for h in range(REP)
        ]
        turned = []
        for pair in ((heads[0], heads[1]), (heads[2], grad_key[span, :])):
            v = jnp.concatenate(pair, axis=1)
            other = jnp.where(lane % HEAD < HEAD // 2, pltpu.roll(v, 96, 1), pltpu.roll(v, 32, 1))
            turned.append((v * cosine - other * sine).astype(BF))
        tail = jnp.concatenate(
            [grad_value[span, :], jnp.zeros((2 * TOK, SLICE - ROUTER), F32)], axis=1
        ).astype(BF)
        low = jnp.concatenate(turned + [tail], axis=1)
        grad_qkv[span, :] = low
        grad = dot(low, small[...].reshape(DIM, SLICE), ((1,), (1,)))
        grad_normed[pl.ds(2 * i, 2)] = grad.astype(BF).reshape(2, TOK, DIM)
        rows.wait()
        values = token_rows[...].reshape(2 * TOK, DIM).astype(F32)
        scale = lax.rsqrt(jnp.mean(values * values, axis=-1, keepdims=True) + epsilon)
        gain_sum[1] += jnp.sum((grad * values * scale).reshape(2 * TOK // 8, 8, DIM), axis=0)
        return _

    lax.fori_loop(0, 4, project, 0)

    def from_grad(dz, dx):
        return grad_normed[first.place(dz, dx)].astype(F32)

    first = Reduce(grad_normed, from_grad, z_landed, s_reduce.at[2], r_reduce.at[2])
    first.begin()
    sums[0].first()

    lanes = lax.broadcasted_iota(jnp.int32, (8, 128), 1)
    marks = [(lanes == GAINS - 256 + i).astype(F32).astype(BF) for i in range(2)]
    first.relay()
    for c in range(4):
        span = slice(c * 384, (c + 1) * 384)
        part = dot(normed[:, :, span].reshape(GROUP, 384), grad_qkv[...], ((0,), (0,)))
        extra = dot(normed_two_ref[:, span], grad_logits, ((0,), (1,)))
        for i in range(2):
            value = gain_sum[1 - i, :, span]
            high = value.astype(BF)
            rest = (value - high.astype(F32)).astype(BF)
            extra = extra + dot(high, marks[i], ((0,), (0,))) + dot(rest, marks[i], ((0,), (0,)))
        grad_small[4 * c : 4 * c + 4, :, 0:256] = (
            part[:, 0:256].astype(BF).reshape(4, ROWS, 256)
        )
        grad_small[4 * c : 4 * c + 4, :, 256:SLICE] = (
            (part[:, 256:SLICE] + extra).astype(BF).reshape(4, ROWS, SLICE - 256)
        )
    sums[1].begin()
    sums[0].second()
    mixed_ref[...] = (middle_ref[...] + out.total()).astype(BF)
    sums[1].first()
    first.cross()
    sums[1].second()
    experts.far_end()
    saved = load(ends.at[pl.ds(0, 2)], expert_ref.at[pl.ds(3, 2)], 4)
    sums[0].third()
    sums[1].third()
    values = tokens[...].astype(F32)
    scale = lax.rsqrt(jnp.mean(values * values, axis=-1, keepdims=True) + epsilon)
    grad_tokens_ref[...] = grad_middle_ref[...] + norm_back(values, scale, gain_one, first.total())
    total = sums[0].total()
    for j in range(PEERS):
        dense_cut[j] = total[12 * j : 12 * (j + 1)]
    total = sums[1].total()
    for j in range(PEERS):
        small_cut[j] = total[12 * j : 12 * (j + 1)]
    cuts = direct(2, dense_cut, dense_in, "exchange") + direct(3, small_cut, small_own, "exchange")
    saved.wait()
    experts.near_end()
    saved = load(ends, expert_ref.at[pl.ds(0, 3)], 4)
    settle(cuts)
    acc = dense_in[0]
    for j in range(1, PEERS):
        acc = acc + dense_in[j]
    output_own[...] = acc
    for part in (out, first, sums[0], sums[1], experts):
        part.finish()
    saved.wait()


def last_phase(*args):
    hbm, vmem = pl.BlockSpec(memory_space=pl.ANY), pl.BlockSpec(memory_space=pltpu.VMEM)
    shape, dma = jax.ShapeDtypeStruct, pltpu.SemaphoreType.DMA
    blocks = (PEERS, TOK, DIM)
    piece = (3 * ROWS, FFE)
    outs = [
        (shape((TOK, DIM), BF), vmem),
        (shape((TOK, DIM), F32), vmem),
        (shape((LOCAL,) + piece, F32), hbm),
        (shape((PEERS, 12, SLICE), F32), hbm),
        (shape((12, DIM), F32), vmem),
        (shape((7, 3) + piece, BF), hbm),
        (shape((8, 2) + piece, BF), hbm),
    ]
    return pl.pallas_call(
        last_kernel,
        out_shape=[o[0] for o in outs],
        in_specs=[hbm] * 9 + [vmem] * 13,
        out_specs=[o[1] for o in outs],
        scratch_shapes=[
            pltpu.VMEM((PEERS, 8, TOK), F32),
            pltpu.VMEM((EXPERTS, TOK), F32),
            pltpu.VMEM((SLICE - 256, TOK), F32),
            pltpu.VMEM((DP, ROWS, SLICE), BF),
            pltpu.VMEM((DP, ROWS, DIM), BF),
            pltpu.VMEM((DP, ROWS, SLICE), BF),
            pltpu.VMEM(blocks, BF),
            pltpu.VMEM((2, TOK, DIM), BF),
            pltpu.VMEM(blocks, BF),
            pltpu.VMEM((PEERS, TOK, QS), BF),
            pltpu.VMEM((PEERS, TOK, QS), BF),
            pltpu.VMEM((PEERS, REP * TOK, HEAD), F32),
            pltpu.VMEM((GROUP, HEAD), F32),
            pltpu.VMEM((GROUP, HEAD), F32),
            pltpu.VMEM((GROUP, SLICE), BF),
            pltpu.VMEM((2, 8, DIM), F32),
            pltpu.VMEM((TOK, DIM), F32),
            pltpu.VMEM((4, TOK, DIM), BF),
            pltpu.VMEM((7, TOK, DIM), BF),
            pltpu.VMEM((7, TOK, DIM), BF),
            pltpu.VMEM((2, 5) + piece, BF),
            pltpu.VMEM((7, 3) + piece, BF),
            pltpu.VMEM((8, 2) + piece, BF),
            pltpu.VMEM((3,) + piece, F32),
            pltpu.VMEM((8, ROWS, SLICE), BF),
            pltpu.VMEM((7, ROWS, SLICE), BF),
            pltpu.VMEM((8, ROWS, DIM), BF),
            pltpu.VMEM((7, ROWS, DIM), BF),
            pltpu.VMEM((PEERS, 12, SLICE), F32),
            pltpu.VMEM((PEERS, 12, DIM), F32),
            pltpu.VMEM((PEERS, 12, DIM), F32),
            dma((4, 7)),
            dma((4, 7)),
            dma((3, 7)),
            dma((3, 7)),
            dma((2, 16)),
            dma((2, 16)),
            dma((7,)),
            dma((7,)),
            dma((8, 2)),
            dma((8, 2)),
            dma((12,)),
            dma((2, 5)),
        ],
        compiler_params=pltpu.CompilerParams(
            collective_id=3, has_side_effects=True, vmem_limit_bytes=62 << 20
        ),
        cost_estimate=lasting(120),
    )(*args)


def experts_kernel(*refs):
    (rows_ref, cot_ref, slot_ref, gate_ref), refs = refs[:4], refs[4:]
    pieces, refs = refs[0], refs[1:]
    (out_ref, back_ref, inner_ref, keep_ref, given_ref), refs = refs[:5], refs[5:]
    xg, cg, weights, grads, gates, inners, wsem, gsem, rsem = refs
    x, y, core = dp_place()
    other = dp_index(x, y, core + 1)
    signal_all([], [other])

    def load(e, b):
        return pltpu.make_async_copy(pieces.at[:, e], weights.at[b], wsem.at[b])

    def kept(e, b):
        return [
            pltpu.make_async_copy(
                grads.at[b, dp_index(x + rx, y + ry, core)], keep_ref.at[k, e], gsem.at[b, k]
            )
            for k, (rx, ry) in enumerate(SLOTS)
        ]

    def given(e, b):
        return [
            pltpu.make_async_remote_copy(
                src_ref=grads.at[b, dp_index(x + rx, y + ry, core + 1)],
                dst_ref=given_ref.at[k, e],
                send_sem=gsem.at[b, 8 + k],
                recv_sem=rsem.at[e, k],
                device_id={"dp": other},
                device_id_type=MESH,
            )
            for k, (rx, ry) in enumerate(SLOTS)
        ]

    def stored(e, b):
        for c in kept(e, b):
            c.wait()
        for c in given(e, b):
            c.wait_send()

    load(0, 0).start()

    def onehot(b):
        places = lax.broadcasted_iota(jnp.int32, (CAP, TOK), 0).astype(F32)
        return [(places == slot_ref[b, e : e + 1, :]) for e in range(LOCAL)]

    def collect(b, _):
        hot = onehot(b)
        pick = jnp.concatenate([h.astype(F32) for h in hot], axis=0).astype(BF)
        xg[b] = dot(pick, rows_ref[b], ((1,), (0,))).astype(BF)
        cg[b] = dot(pick, cot_ref[b], ((1,), (0,))).astype(BF)
        for e in range(LOCAL):
            g = jnp.sum(jnp.where(hot[e], gate_ref[b, e : e + 1, :], 0.0), axis=1, keepdims=True)
            gates[e, pl.ds(b * CAP, CAP), :] = jnp.broadcast_to(g, (CAP, 128))
        return _

    lax.fori_loop(0, PEERS, collect, 0)

    def expert(e, _):
        b = lax.rem(e, 2)
        load(e, b).wait()

        @pl.when(e + 1 < LOCAL)
        def _next():
            load(e + 1, 1 - b).start()

        @pl.when(e >= 2)
        def _free():
            stored(e - 2, b)

        span = pl.ds(pl.multiple_of(e * CAP, CAP), CAP)
        rows = xg[:, span, :].reshape(PEERS * CAP, DIM)
        cot = cg[:, span, :].reshape(PEERS * CAP, DIM)
        gate = gates[e][:, :1]
        w_gate = weights[b, :, 0:96, :].reshape(DIM, FFE)
        gate_act = dot(rows, w_gate, ((1,), (0,)))
        w_up = weights[b, :, 96:192, :].reshape(DIM, FFE)
        up_act = dot(rows, w_up, ((1,), (0,)))
        sig = 1.0 / (1.0 + jnp.exp(-gate_act))
        silu = gate_act * sig
        hidden = (silu * up_act).astype(BF)
        grad_out = (cot.astype(F32) * gate).astype(BF)
        inner = jnp.zeros((PEERS * CAP, 1), F32)
        grad_hidden = jnp.zeros((PEERS * CAP, FFE), F32)
        gated = []
        for k in range(3):
            lanes = slice(k * FFE, (k + 1) * FFE)
            w_down = weights[b, :, 192 + 32 * k : 224 + 32 * k, :].reshape(FFE, FFE)
            part = dot(hidden, w_down, ((1,), (0,))).astype(BF).astype(F32)
            inner = inner + jnp.sum(part * cot[:, lanes].astype(F32), axis=1, keepdims=True)
            gated.append((part * gate).astype(BF))
            grad_hidden = grad_hidden + dot(grad_out[:, lanes], w_down, ((1,), (1,)))
            grads[b, :, 192 + 32 * k : 224 + 32 * k, :] = (
                dot(hidden, grad_out[:, lanes], ((0,), (0,))).astype(BF).reshape(DP, 32, FFE)
            )
        inners[e] = jnp.broadcast_to(inner, (PEERS * CAP, 128))
        grad_gate = (grad_hidden * up_act * sig * (1.0 + gate_act * (1.0 - sig))).astype(BF)
        grad_up = (grad_hidden * silu).astype(BF)
        grads[b, :, 0:96, :] = (
            dot(rows, grad_gate, ((0,), (0,))).astype(BF).reshape(DP, ROWS, FFE)
        )
        grads[b, :, 96:192, :] = (
            dot(rows, grad_up, ((0,), (0,))).astype(BF).reshape(DP, ROWS, FFE)
        )
        for c in kept(e, b) + given(e, b):
            c.start()
        back = dot(grad_gate, w_gate, ((1,), (1,))) + dot(grad_up, w_up, ((1,), (1,)))
        xg[:, span, :] = back.astype(BF).reshape(PEERS, CAP, DIM)
        for k in range(3):
            cg[:, span, k * FFE : (k + 1) * FFE] = gated[k].reshape(PEERS, CAP, FFE)
        return _

    lax.fori_loop(0, LOCAL, expert, 0)

    def combine(b, _):
        hot = onehot(b)
        pick = jnp.concatenate([h.astype(F32) for h in hot], axis=0).astype(BF)
        out_ref[b] = dot(pick, cg[b], ((0,), (0,))).astype(BF)
        back_ref[b] = dot(pick, xg[b], ((0,), (0,))).astype(BF)
        lines = []
        for e in range(LOCAL):
            value = inners[e, pl.ds(b * CAP, CAP), :][:, :1]
            lines.append(jnp.sum(jnp.where(hot[e], value, 0.0), axis=0, keepdims=True))
        inner_ref[b] = jnp.concatenate(lines + [jnp.zeros((8 - LOCAL, TOK), F32)], axis=0)
        return _

    lax.fori_loop(0, PEERS, combine, 0)
    for e in (LOCAL - 2, LOCAL - 1):
        stored(e, e % 2)
    for e in range(LOCAL):
        for c in given(e, e % 2):
            c.wait_recv()


def run_experts(rows, cot, slots, gates, pieces):
    vmem = pl.BlockSpec(memory_space=pltpu.VMEM)
    piece = (LOCAL, 3 * ROWS, FFE)
    return pl.pallas_call(
        experts_kernel,
        out_shape=[
            jax.ShapeDtypeStruct((PEERS, TOK, DIM), BF),
            jax.ShapeDtypeStruct((PEERS, TOK, DIM), BF),
            jax.ShapeDtypeStruct((PEERS, 8, TOK), F32),
            jax.ShapeDtypeStruct((8,) + piece, BF),
            jax.ShapeDtypeStruct((8,) + piece, BF),
        ],
        in_specs=[vmem] * 4 + any_specs(1),
        out_specs=[vmem] * 3 + any_specs(2),
        scratch_shapes=[
            pltpu.VMEM((PEERS, LOCAL * CAP, DIM), BF),
            pltpu.VMEM((PEERS, LOCAL * CAP, DIM), BF),
            pltpu.VMEM((2, DP, 3 * ROWS, FFE), BF),
            pltpu.VMEM((2, DP, 3 * ROWS, FFE), BF),
            pltpu.VMEM((LOCAL, PEERS * CAP, 128), F32),
            pltpu.VMEM((LOCAL, PEERS * CAP, 128), F32),
            pltpu.SemaphoreType.DMA((2,)),
            pltpu.SemaphoreType.DMA((2, 16)),
            pltpu.SemaphoreType.DMA((LOCAL, 8)),
        ],
        compiler_params=pltpu.CompilerParams(
            collective_id=2, has_side_effects=True, vmem_limit_bytes=60 << 20
        ),
        cost_estimate=pl.CostEstimate(
            flops=20_000_000_000, bytes_accessed=60_000_000, transcendentals=700_000
        ),
    )(rows, cot, slots, gates, pieces)


def rope_tables(offsets, head_width):
    exponent = jnp.arange(head_width // 2, dtype=jnp.float32) * (2.0 / head_width)
    frequency = jnp.exp(-exponent * math.log(rope_base))
    phase_angles = offsets.astype(jnp.float32)[:, None] * frequency[None, :]
    return (jnp.cos(phase_angles)[:, None, :], jnp.sin(phase_angles)[:, None, :])


def layout(lengths, group_count):
    seq_ends = jnp.cumsum(lengths)
    starts = seq_ends - lengths
    places = jnp.arange(group_count, dtype=jnp.int32)
    member = ((places[:, None] >= starts[None, :]) & (places[:, None] < seq_ends[None, :])).astype(
        jnp.int32
    )
    numbers = jnp.arange(lengths.shape[0], dtype=jnp.int32)
    segment = jnp.sum(member * numbers[None, :], axis=1)
    offsets = places - jnp.sum(member * starts[None, :], axis=1)
    return (segment, offsets)


def norm_back(values, row_scale, gain_vector, grad_normed):
    weighted = grad_normed * gain_vector
    return row_scale * weighted - values * row_scale**3 * jnp.mean(
        weighted * values, axis=-1, keepdims=True
    )


def by_peer(table):
    return jnp.pad(table.reshape(PEERS, LOCAL, TOK), ((0, 0), (0, 8 - LOCAL), (0, 0)))


def local(
    tokens,
    cotangent,
    seq_lengths,
    expert_ids,
    w_query,
    w_key,
    w_value,
    w_output,
    norm_one,
    norm_two,
    w_router,
    w_gate,
    w_up,
    w_down,
):
    down_piece = w_down.reshape(LOCAL, 32, 3, FFE).transpose(0, 2, 1, 3).reshape(LOCAL, ROWS, FFE)
    piece = jnp.concatenate([w_gate, w_up, down_piece], axis=1)

    slices = jnp.concatenate(
        [
            w_query.reshape(12, PEERS, QS).transpose(1, 0, 2),
            w_key.reshape(12, PEERS, HEAD).transpose(1, 0, 2),
            w_value.reshape(12, PEERS, HEAD).transpose(1, 0, 2),
            jnp.broadcast_to(
                jnp.concatenate(
                    [
                        w_router,
                        norm_one[:, None],
                        norm_two[:, None],
                        jnp.zeros((12, SLICE - GAINS - 2), BF),
                    ],
                    axis=1,
                )[None],
                (PEERS, 12, SLICE - ROUTER),
            ),
        ],
        axis=2,
    )
    member = jnp.any(
        expert_ids[None, :, :] == jnp.arange(EXPERTS, dtype=jnp.int32)[:, None, None], axis=-1
    )
    before = jnp.arange(TOK)[:, None] < jnp.arange(TOK)[None, :]
    places = jnp.dot(member.astype(BF), before.astype(BF), preferred_element_type=F32)
    slot_table = jnp.where(member, places, -1.0)

    segment, offsets = layout(seq_lengths[0], GROUP)
    cosine, sine_table = rope_tables(offsets, HEAD)
    wide_cosine = jnp.tile(cosine[:, 0, :], (1, 4))
    wide_sine = jnp.tile(jnp.concatenate([-sine_table[:, 0, :], sine_table[:, 0, :]], axis=1), (1, 2))
    start = jnp.broadcast_to((jnp.arange(GROUP, dtype=jnp.int32) - offsets)[:, None], (GROUP, 128))
    (
        pieces,
        cot_all,
        slots_all,
        rows_all,
        gates_all,
        tokens_all,
        normed_all,
        slices_all,
        output_all,
        query,
        key,
        value,
        log_total,
        attended,
        middle,
        normed_two,
        gate_values,
    ) = first_phase(
        slices,
        w_output,
        tokens,
        cotangent,
        slot_table,
        by_peer(slot_table),
        piece,
        wide_cosine,
        wide_sine,
        start,
    )
    out_part, back_part, inner_part, keep, given = run_experts(
        rows_all, cot_all, slots_all, gates_all, pieces
    )
    mixed, grad_tokens, expert_grads, small_own, output_own, _, _ = last_phase(
        back_part,
        inner_part,
        out_part,
        keep,
        given,
        tokens_all,
        normed_all,
        slices_all,
        output_all,
        tokens,
        cotangent,
        gate_values,
        middle,
        normed_two,
        attended,
        query,
        key,
        value,
        log_total,
        wide_cosine,
        wide_sine,
        start,
    )
    own_sum = jnp.sum(small_own[:, :, ROUTER:], axis=0)
    return (
        mixed,
        grad_tokens,
        small_own[:, :, :QS].transpose(1, 0, 2).reshape(12, DIM),
        small_own[:, :, QS : QS + HEAD].transpose(1, 0, 2).reshape(12, KV_HEADS * HEAD),
        small_own[:, :, QS + HEAD : ROUTER].transpose(1, 0, 2).reshape(12, KV_HEADS * HEAD),
        output_own,
        own_sum[:, EXPERTS],
        own_sum[:, EXPERTS + 1],
        own_sum[:, :EXPERTS],
        expert_grads[:, :ROWS],
        expert_grads[:, ROWS : 2 * ROWS],
        expert_grads[:, 2 * ROWS :]
        .reshape(LOCAL, 3, 32, FFE)
        .transpose(0, 2, 1, 3)
        .reshape(LOCAL, 32, DIM),
    )


def solution(mesh):
    both = P(("dp", "expert"), None)
    line = P(("dp", "expert"))
    cube = P("expert", "dp", None)
    in_specs = (both, both, P("dp", None), both, both, both, both, both)
    in_specs = in_specs + (line, line, both, cube, cube, cube)
    out_specs = (both,) * 6 + (line, line, both, cube, cube, cube)
    return jax.shard_map(local, mesh=mesh, in_specs=in_specs, out_specs=out_specs, check_vma=False)
```

```python
import functools
import math

import jax
import jax.numpy as jnp
from jax import lax
from jax.experimental import pallas as pl
from jax.experimental.pallas import tpu as pltpu
from jax.sharding import PartitionSpec as P

HEADS = 24
KV_HEADS = 8
HEAD = 64
DIM = 1536
FFE = 512
EXPERTS = 40
LOCAL = 5
CAP = 32
TOK = 128
PEERS = 8
DP = 16
GROUP = TOK * PEERS
REP = HEADS // KV_HEADS
SLICE = 384
QS = REP * HEAD
ROWS = 96
ROUTER = QS + 2 * HEAD
GAINS = ROUTER + EXPERTS

epsilon = 1e-06
rope_base = 10000.0
masked_score = -1e30
MESH = pl.DeviceIdType.MESH
BF = jnp.bfloat16
F32 = jnp.float32

RELATIVE = ((2, 1), (2, 0), (1, 1), (3, 1), (0, 1), (1, 0), (3, 0))
SLOTS = ((0, 0), (1, 0), (0, 1), (0, 3), (1, 1), (1, 3), (0, 2), (1, 2))


def expert_peers():
    me = lax.axis_index("expert")
    z, x = me // 2, me % 2
    return me, [(z + rz) % 4 * 2 + (x + rx) % 2 for rz, rx in RELATIVE]


def dp_place():
    d = lax.axis_index("dp")
    return d // 8, (d // 2) % 4, d % 2


def dp_index(x, y, core):
    return (x % 2 * 4 + y % 4) * 2 + core % 2


def signal_all(expert_ids, dp_ids):
    barrier = pltpu.get_barrier_semaphore()
    for p in expert_ids:
        pl.semaphore_signal(barrier, inc=1, device_id={"expert": p}, device_id_type=MESH)
    for p in dp_ids:
        pl.semaphore_signal(barrier, inc=1, device_id={"dp": p}, device_id_type=MESH)
    pl.semaphore_wait(barrier, len(expert_ids) + len(dp_ids))


def any_specs(count):
    return [pl.BlockSpec(memory_space=pltpu.HBM)] * count


def expert_copies(ins, outs, modes, send, recv):
    me, peers = expert_peers()
    copies = []
    for r, p in enumerate(peers):
        for i, mode in enumerate(modes):
            copies.append(
                pltpu.make_async_remote_copy(
                    src_ref=ins[i] if mode == "gather" else ins[i].at[p],
                    dst_ref=outs[i].at[me],
                    send_sem=send.at[i, r],
                    recv_sem=recv.at[i, r],
                    device_id={"expert": p},
                    device_id_type=MESH,
                )
            )
    return copies


def own_copies(ins, outs, modes, sems):
    me = lax.axis_index("expert")
    return [
        pltpu.make_async_copy(
            ins[i] if mode == "gather" else ins[i].at[me], outs[i].at[me], sems.at[i]
        )
        for i, mode in enumerate(modes)
    ]


def lasting(us):
    return pl.CostEstimate(flops=us * 1_000_000_000, bytes_accessed=0, transcendentals=0)


class Gather:
    def __init__(self, src, out, send, recv, local):
        self.src, self.out, self.send, self.recv, self.local = src, out, send, recv, local
        me = lax.axis_index("expert")
        z, x = me // 2, me % 2

        def place(dz, dx):
            return (z + dz) % 4 * 2 + (x + dx) % 2

        self.slots = [
            place(0, 1),
            place(3, 0),
            place(1, 0),
            place(3, 1),
            place(1, 1),
            place(2, 0),
            place(2, 1),
        ]
        self.me = me
        x, up, down = place(0, 1), place(1, 0), place(3, 0)
        self.moves = ((None, x), (None, up), (None, down), (0, up), (0, down), (1, up), (4, down))
        self.started = []

    def descriptor(self, k, src, slot, target):
        return pltpu.make_async_remote_copy(
            src_ref=src,
            dst_ref=self.out.at[slot],
            send_sem=self.send.at[k],
            recv_sem=self.recv.at[k],
            device_id={"expert": target},
            device_id_type=MESH,
        )

    def begin(self):
        self.own = pltpu.make_async_copy(self.src, self.out.at[self.me], self.local)
        self.own.start()

    def issue(self, k):
        source, target = self.moves[k]
        slot = self.me if source is None else self.slots[source]
        src = self.src if source is None else self.out.at[slot]
        c = self.descriptor(k, src, slot, target)
        c.start()
        self.started.append(c)

    def arrive(self, k):
        self.descriptor(k, self.src, self.slots[k], self.moves[0][1]).wait_recv()


class Line:
    def __init__(self, src, view, moves, send, recv):
        self.src, self.view, self.send, self.recv = src, view, send, recv
        x, y, core = dp_place()
        self.targets = {
            "x": dp_index(x + 1, y, core),
            "up": dp_index(x, y + 1, core),
            "down": dp_index(x, y + 3, core),
            "core": dp_index(x, y, core + 1),
        }
        self.moves = dict(moves)
        for k in range(8):
            self.moves[8 + k] = (k, "core")
        self.slots = [dp_index(x + rx, y + ry, core + c) for c in range(2) for rx, ry in SLOTS]
        self.started = []

    def descriptor(self, k, src, slot, where):
        return pltpu.make_async_remote_copy(
            src_ref=src,
            dst_ref=self.view(slot),
            send_sem=self.send.at[k],
            recv_sem=self.recv.at[k],
            device_id={"dp": self.targets[where]},
            device_id_type=MESH,
        )

    def issue(self, k):
        source, where = self.moves[k]
        slot = self.slots[source]
        src = self.src if source == 0 else self.view(slot)
        c = self.descriptor(k, src, slot, where)
        c.start()
        self.started.append(c)

    def arrive(self, k):
        slot = self.slots[k]
        self.descriptor(k, self.view(slot), slot, "x").wait_recv()


X_FIRST = {
    1: (0, "x"),
    2: (0, "down"),
    3: (0, "up"),
    4: (1, "down"),
    5: (1, "up"),
    6: (3, "up"),
    7: (4, "down"),
}
Y_FIRST = {
    1: (0, "x"),
    2: (0, "down"),
    3: (0, "up"),
    4: (2, "x"),
    5: (3, "x"),
    6: (3, "up"),
    7: (6, "x"),
}
Y_FIRST_DOWN = {**Y_FIRST, 6: (2, "down")}
PARTS = (
    ((0, 1), (0, 288), X_FIRST),
    ((1, 1), (0, 288), X_FIRST),
    ((2, 1), (0, 288), X_FIRST),
    ((3, 1), (0, 288), Y_FIRST),
    ((4, 1), (0, 192), Y_FIRST_DOWN),
    ((4, 1), (192, 96), X_FIRST),
)
KEPT = tuple(
    jax.ShapeDtypeStruct(shape, kind)
    for shape, kind in (
        ((PEERS, REP * TOK, HEAD), BF),
        ((GROUP, HEAD), BF),
        ((GROUP, HEAD), BF),
        ((PEERS, REP * TOK, 128), F32),
        ((PEERS, TOK, QS), BF),
        ((TOK, DIM), F32),
        ((TOK, DIM), BF),
        ((EXPERTS, TOK), F32),
        ((GROUP, 128), F32),
        ((GROUP, 128), F32),
        ((GROUP, 128), jnp.int32),
    )
)
FIRST_STEPS = ("ss", "so", "sl", "a", "g", "ls", "lo", "P0", "P1", "A0", "A1", "A2", "C2", "gt", "tb")
FIRST_STEPS = FIRST_STEPS + tuple("tr%d" % i for i in range(4))
FIRST_LINES = ("t", "c", "r", "s", "o") + tuple("p%d." % i for i in range(len(PARTS)))
FIRST_STEPS = FIRST_STEPS + tuple(n + str(k) for n in FIRST_LINES for k in range(16))
FIRST_ORDER = (
    1, -1, 2, 6, 76, 69, 70, 71, -2, 135, 166, 20, 108, 188, 38, 156, 124, 15, 3, -69, 77, -71, 79,
    172, 21, -70, 78, 140, 7, 102, 92, -166, 174, 74, 73, -135, 143, 101, 22, 119, 16, -74, 82, 37,
    150, 17, -73, 81, -102, 110, 149, 103, 72, -101, 109, 18, -20, 24, -119, 127, 170, -150, 158,
    23, 19, -72, 80, 152, 105, 134, -149, 157, -103, 111, -170, 178, -21, 25, 85, -24, 26, 183, 75,
    -152, 160, -105, 113, 87, 118, -134, 142, -183, 191, -75, 83, 181, -37, 41, -85, 93, 36, 89,
    88, -22, -23, -25, -26, -76, -77, -78, -79, -80, -81, -82, -83, 8, -87, 90, 95, -118, 126,
    -181, 184, 133, 189, 9, 185, 86, 10, -184, 187, -36, 40, -89, 97, 138, 39, 192, -88, 96, 91,
    117, 11, -185, 193, -86, 94, -133, 141, 137, -187, 195, 136, 168, -90, 98, 12, 4, -138, 146,
    -117, 125, -40, 42, -91, 99, -168, 176, 165, 151, 122, 120, 171, 104, -4, -92, -93, -94, -95,
    -96, -97, -98, -99, 13, -151, 159, -165, 173, 53, 54, 52, -136, 144, -137, 145, 14, 5, -171,
    179, -120, 128, 154, -122, 130, 139, -104, 112, 153, -53, 57, 106, -52, 56, -154, 162, 107,
    -139, 147, 155, 167, -153, 161, 55, -106, 114, 123, -56, 58, -107, 115, 121, -167, 175, 169,
    -155, 163, 182, -123, 131, 186, -169, 177, -121, 129, -182, 190, -186, 194, -108, -188, -156,
    -124, -172, -140, -174, -143, -38, -3, -110, -109, -127, -158, -157, -111, -178, -160, -113,
    -142, -191, -126, -189, -41, -192, -193, -141, -195, -39, -146, -125, -176, -42, -159, -173,
    -144, -145, -179, -128, -130, -54, -112, -5, -162, -147, -161, -57, -114, -115, -175, -163,
    -55, -131, -58, -177, -129, -190, -194,
)


def first_kernel(*refs):
    w_dense, (output, tokens, cot, ids, lengths, w_gate, w_up, w_down) = refs[:4], refs[4:12]
    (
        pieces_out,
        cot_all,
        slots_all,
        rows_all,
        gates_all,
        tokens_out,
        normed_out,
        small_out,
        output_out,
    ) = refs[12:21]
    kept_out = refs[21:32]
    kept_refs = refs[32:43]
    (
        query_ref,
        key_ref,
        value_ref,
        log_ref,
        attended_ref,
        middle_ref,
        normed_two_ref,
        gates_ref,
        cos_ref,
        sin_ref,
        start_ref,
    ) = kept_refs
    w_query, w_key, w_value, tail = refs[43:47]
    (
        piece,
        ids_ref,
        member_ref,
        slot_send,
        slices,
        small_in,
        output_in,
        small_rows,
        output_rows,
        small,
        dense,
        tokens_in,
        normed,
        att_send,
        gate_send,
        s_small,
        s_dense,
        s_piece,
        r_small,
        r_dense,
        r_piece,
        s_gather,
        r_gather,
        s_direct,
        r_direct,
        l_sem,
    ) = refs[47:]
    x, y, core = dp_place()
    me = lax.axis_index("expert")
    mine = dp_index(x, y, core)
    loads = [
        pltpu.make_async_copy(src, dst, l_sem.at[20 + i])
        for i, (src, dst) in enumerate(
            zip(w_dense + (ids,), (w_query, w_key, w_value, tail, ids_ref))
        )
    ]
    own = [
        pltpu.make_async_copy(w_gate, piece.at[:, pl.ds(0, ROWS)], l_sem.at[15]),
        pltpu.make_async_copy(w_up, piece.at[:, pl.ds(ROWS, ROWS)], l_sem.at[16]),
    ] + [
        pltpu.make_async_copy(
            w_down.at[:, :, pl.ds(k * FFE, FFE)],
            piece.at[:, pl.ds(2 * ROWS + 32 * k, 32)],
            l_sem.at[17 + k],
        )
        for k in range(3)
    ]
    for c in loads + own:
        c.start()
    _, peers = expert_peers()
    signal_all(
        peers,
        [
            dp_index(x + 1, y, core),
            dp_index(x, y + 1, core),
            dp_index(x, y + 3, core),
            dp_index(x, y, core + 1),
        ],
    )
    for c in loads + own:
        c.wait()
    for j in range(PEERS):
        slices[j] = jnp.concatenate(
            [
                w_query[:, QS * j : QS * (j + 1)],
                w_key[:, HEAD * j : HEAD * (j + 1)],
                w_value[:, HEAD * j : HEAD * (j + 1)],
                tail[...],
            ],
            axis=1,
        )

    def direct(i, src, out, mode):
        part = expert_copies(
            [src], [out], [mode], s_direct.at[pl.ds(i, 1)], r_direct.at[pl.ds(i, 1)]
        ) + own_copies([src], [out], [mode], l_sem.at[pl.ds(i, 1)])

        def start():
            for c in part:
                c.start()

        def wait():
            for c in part:
                c.wait()

        return start, wait

    saved = []

    def save(src, dst, i):
        c = pltpu.make_async_copy(src, dst, l_sem.at[i])
        c.start()
        saved.append(c)

    issue, arrive = {}, {}
    for i, (name, src, out, mode) in enumerate(
        (
            ("ss", slices, small_in, "exchange"),
            ("so", output, output_in, "gather"),
            ("sl", slot_send, slots_all, "exchange"),
            ("a", att_send, attended_ref, "exchange"),
            ("g", gate_send, gates_all, "exchange"),
        )
    ):
        issue[name], arrive[name] = direct(i, src, out, mode)
    lines = {}
    for i, (name, src, out) in enumerate(
        (("t", tokens, tokens_in), ("c", cot, cot_all), ("r", normed_two_ref, rows_all))
    ):
        lines[name] = Gather(src, out, s_gather.at[i], r_gather.at[i], l_sem.at[5 + i])
    for i, (name, src, out) in enumerate((("s", small_rows, small), ("o", output_rows, dense))):
        lines[name] = Line(src, lambda k, out=out: out.at[k], X_FIRST, s_dense.at[i], r_dense.at[i])
    for i, ((expert, count), (row, rows), moves) in enumerate(PARTS):
        def view(k, span=pl.ds(expert, count), part=pl.ds(row, rows)):
            return pieces_out.at[k, span, part]

        own_part = piece.at[pl.ds(expert, count), pl.ds(row, rows)]
        lines["p%d." % i] = Line(own_part, view, moves, s_piece.at[i], r_piece.at[i])
    for name, line in lines.items():
        for k in range(16):
            issue[name + str(k)] = functools.partial(line.issue, k)
            arrive[name + str(k)] = functools.partial(line.arrive, k)

    kept = {}

    def lay_out(name, landed, rows, out, i):
        rows[...] = jnp.concatenate([landed[j] for j in range(PEERS)], axis=0)
        kept[name] = pltpu.make_async_copy(rows, out.at[mine], l_sem.at[8 + i])
        kept[name].start()

    def tables():
        named = jnp.zeros((TOK, 128), F32)
        experts = lax.broadcasted_iota(jnp.int32, (TOK, 128), 1)
        for k in range(ids_ref.shape[1]):
            named = named + (ids_ref[:, k : k + 1] == experts).astype(F32)
        before = (lax.broadcasted_iota(jnp.int32, (TOK, 128), 0) > experts).astype(F32)
        places = dot(before.astype(BF), named.astype(BF), ((1,), (0,)))
        member_ref[...] = jnp.transpose(jnp.where(named > 0.0, places, -1.0))[:EXPERTS]
        slot_send[...] = jnp.full_like(slot_send, -1.0)
        for j in range(PEERS):
            slot_send[j, 0:LOCAL, :] = member_ref[LOCAL * j : LOCAL * (j + 1), :]

    def turns(first, last):
        second = lengths[0, 0]
        third = second + lengths[0, 1]
        fourth = third + lengths[0, 2]

        def block(i, _):
            span = pl.ds(pl.multiple_of(i * TOK, TOK), TOK)
            place = lax.broadcasted_iota(jnp.int32, (TOK, 128), 0) + i * TOK
            begins = jnp.where(
                place >= fourth,
                fourth,
                jnp.where(place >= third, third, jnp.where(place >= second, second, 0)),
            )
            start_ref[span, :] = begins
            lane = lax.broadcasted_iota(jnp.int32, (TOK, 128), 1)
            step = (lane % (HEAD // 2)).astype(F32) * (2.0 / HEAD)
            angle = (place - begins).astype(F32) * jnp.exp(-step * math.log(rope_base))
            cos_ref[span, :] = jnp.cos(angle)
            sin_ref[span, :] = jnp.where(lane % HEAD < HEAD // 2, -1.0, 1.0) * jnp.sin(angle)
            return _

        lax.fori_loop(first, last, block, 0)

    issue["ls"] = functools.partial(lay_out, "s", small_in, small_rows, small, 0)
    issue["lo"] = functools.partial(lay_out, "o", output_in, output_rows, dense, 1)

    def project(i, _):
        values = tokens_in[pl.ds(2 * i, 2)].reshape(2 * TOK, DIM).astype(F32)
        scale = lax.rsqrt(jnp.mean(values * values, axis=-1, keepdims=True) + epsilon)
        low = (values * scale * kept["gains"][0:1]).astype(BF)
        normed[pl.ds(2 * i, 2)] = low.reshape(2, TOK, DIM)
        qkv = dot(low, small[...].reshape(DIM, SLICE), ((1,), (0,)))
        span = pl.ds(pl.multiple_of(i * 2 * TOK, 2 * TOK), 2 * TOK)
        cosine, sine = cos_ref[span, :], sin_ref[span, :]
        lane = lax.broadcasted_iota(jnp.int32, (2 * TOK, 128), 1)
        turned = []
        for h in range(2):
            v = qkv[:, 128 * h : 128 * h + 128]
            other = jnp.where(lane % HEAD < HEAD // 2, pltpu.roll(v, 96, 1), pltpu.roll(v, 32, 1))
            turned.append((v * cosine + other * sine).astype(BF))
        heads = (turned[0][:, :HEAD], turned[0][:, HEAD:], turned[1][:, :HEAD])
        for b in range(2):
            for h in range(REP):
                query_ref[2 * i + b, h * TOK : (h + 1) * TOK, :] = heads[h][
                    b * TOK : (b + 1) * TOK
                ]
        key_ref[span, :] = turned[1][:, HEAD:]
        value_ref[span, :] = qkv[:, QS + HEAD : ROUTER].astype(BF)
        return _

    def project_first():
        lines["t"].own.wait()
        kept["s"].wait()
        pick = (
            lax.broadcasted_iota(jnp.int32, (8, SLICE), 1)
            == lax.broadcasted_iota(jnp.int32, (8, SLICE), 0) + GAINS
        )
        kept["gains"] = dot(
            pick.astype(F32).astype(BF), small[...].reshape(DIM, SLICE), ((1,), (1,))
        )
        lax.fori_loop(0, 2, project, 0)

    def project_rest():
        lax.fori_loop(2, 4, project, 0)
        save(tokens_in, tokens_out, 10)
        save(normed, normed_out, 11)
        save(small, small_out, 12)

    def attend(width, i, _):
        scores = dot(query_ref[i], key_ref[0:width, :], ((1,), (1,))) * HEAD ** (-0.5)
        keys = lax.broadcasted_iota(jnp.int32, (TOK, width), 1)
        rows = lax.broadcasted_iota(jnp.int32, (TOK, width), 0) + i * TOK
        begins = start_ref[pl.ds(pl.multiple_of(i * TOK, TOK), TOK), :][:, :1]
        allowed = (keys <= rows) & (keys >= begins)
        scores = jnp.where(allowed[None], scores.reshape(REP, TOK, width), masked_score)
        top = jnp.max(scores, axis=-1, keepdims=True)
        terms = jnp.exp(scores - top)
        total = jnp.sum(terms, axis=-1, keepdims=True)
        probs = (terms / total).astype(BF).reshape(REP * TOK, width)
        out = dot(probs, value_ref[0:width, :], ((1,), (0,))).astype(BF)
        att_send[i] = jnp.concatenate([out[h * TOK : (h + 1) * TOK] for h in range(REP)], axis=1)
        log_ref[i] = jnp.broadcast_to(
            (top + jnp.log(total)).reshape(REP * TOK, 1), (REP * TOK, 128)
        )
        return _

    issue["P0"], issue["P1"] = project_first, project_rest
    for name, first, last, width in (("A0", 0, 4, 512), ("A1", 4, 6, 1024), ("A2", 6, 8, 1024)):
        issue[name] = functools.partial(
            lax.fori_loop, first, last, functools.partial(attend, width), 0
        )

    def out_project():
        kept["o"].wait()
        save(dense, output_out, 13)
        middle = tokens_in[me].astype(F32)
        for j in range(PEERS):
            middle = middle + dot(
                attended_ref[j], dense[2 * j : 2 * j + 2].reshape(QS, DIM), ((1,), (0,))
            )
        middle_ref[...] = middle
        scale_two = lax.rsqrt(jnp.mean(middle * middle, axis=-1, keepdims=True) + epsilon)
        normed_two_ref[...] = (middle * scale_two * kept["gains"][1:2]).astype(BF)
        lines["r"].begin()

    def choose():
        router = small[:, :, 256:SLICE].reshape(DIM, SLICE - 256)
        logits = dot(router, normed_two_ref[...], ((0,), (1,)))[ROUTER - 256 : GAINS - 256]
        member = member_ref[...] >= 0.0
        chosen = jnp.where(member, logits, masked_score)
        weight = jnp.where(member, jnp.exp(chosen - jnp.max(chosen, axis=0, keepdims=True)), 0.0)
        gates_ref[...] = weight / jnp.sum(weight, axis=0, keepdims=True)
        gate_send[...] = jnp.zeros_like(gate_send)
        for j in range(PEERS):
            gate_send[j, 0:LOCAL, :] = gates_ref[LOCAL * j : LOCAL * (j + 1), :]

    issue["C2"], issue["gt"] = out_project, choose
    save(piece, pieces_out.at[mine], 14)
    lines["t"].begin()
    lines["c"].begin()
    issue["tb"] = tables
    for i in range(4):
        issue["tr%d" % i] = functools.partial(turns, 2 * i, 2 * i + 2)
    for step in FIRST_ORDER:
        (issue if step > 0 else arrive)[FIRST_STEPS[abs(step) - 1]]()
    lines["c"].own.wait()
    lines["r"].own.wait()
    for line in lines.values():
        for c in line.started:
            c.wait_send()
    for i, (src, dst) in enumerate(zip(kept_refs, kept_out)):
        save(src, dst, 25 + i)
    for c in saved:
        c.wait()


def first_phase(*args):
    hbm, smem = pl.BlockSpec(memory_space=pltpu.HBM), pl.BlockSpec(memory_space=pltpu.SMEM)
    shape = jax.ShapeDtypeStruct
    blocks = (PEERS, TOK, DIM)
    outs = [
        (shape((DP, LOCAL, 3 * ROWS, FFE), BF), hbm),
        (shape(blocks, BF), hbm),
        (shape((PEERS, 8, TOK), F32), hbm),
        (shape(blocks, BF), hbm),
        (shape((PEERS, 8, TOK), F32), hbm),
        (shape(blocks, BF), hbm),
        (shape(blocks, BF), hbm),
        (shape((DP, ROWS, SLICE), BF), hbm),
        (shape((DP, ROWS, DIM), BF), hbm),
    ] + [(k, hbm) for k in KEPT]
    dma = pltpu.SemaphoreType.DMA
    return pl.pallas_call(
        first_kernel,
        out_shape=[o[0] for o in outs],
        in_specs=[hbm] * 8 + [smem] + [hbm] * 3,
        out_specs=[o[1] for o in outs],
        scratch_shapes=[pltpu.VMEM(k.shape, k.dtype) for k in KEPT]
        + [pltpu.VMEM(a.shape, a.dtype) for a in args[:4]]
        + [
            pltpu.VMEM((LOCAL, 3 * ROWS, FFE), BF),
            pltpu.VMEM((TOK, 8), jnp.int32),
            pltpu.VMEM((EXPERTS, TOK), F32),
            pltpu.VMEM((PEERS, 8, TOK), F32),
            pltpu.VMEM((PEERS, 12, SLICE), BF),
            pltpu.VMEM((PEERS, 12, SLICE), BF),
            pltpu.VMEM((PEERS, 12, DIM), BF),
            pltpu.VMEM((ROWS, SLICE), BF),
            pltpu.VMEM((ROWS, DIM), BF),
            pltpu.VMEM((DP, ROWS, SLICE), BF),
            pltpu.VMEM((DP, ROWS, DIM), BF),
            pltpu.VMEM(blocks, BF),
            pltpu.VMEM(blocks, BF),
            pltpu.VMEM((PEERS, TOK, QS), BF),
            pltpu.VMEM((PEERS, 8, TOK), F32),
            dma((1,)),
            dma((2, 16)),
            dma((len(PARTS), 16)),
            dma((1,)),
            dma((2, 16)),
            dma((len(PARTS), 16)),
            dma((3, 7)),
            dma((3, 7)),
            dma((5, 7)),
            dma((5, 7)),
            dma((40,)),
        ],
        compiler_params=pltpu.CompilerParams(
            collective_id=1, has_side_effects=True, vmem_limit_bytes=63 << 20
        ),
        cost_estimate=lasting(120),
    )(*args)


def dot(a, b, contract):
    return lax.dot_general(a, b, ((contract[0], contract[1]), ((), ())), preferred_element_type=F32)


class Reduce:
    def __init__(self, src, own, landed, send, recv):
        self.src, self.own, self.landed = src, own, landed
        self.send, self.recv = send, recv
        me = lax.axis_index("expert")
        z, x = me // 2, me % 2
        self.place = lambda dz, dx: (z + dz) % 4 * 2 + (x + dx) % 2
        self.targets = {"up": self.place(1, 0), "down": self.place(3, 0), "x": self.place(0, 1)}
        self.started = []

    def copy(self, k, src, where):
        c = pltpu.make_async_remote_copy(
            src_ref=src,
            dst_ref=self.landed.at[k],
            send_sem=self.send.at[k],
            recv_sem=self.recv.at[k],
            device_id={"expert": self.targets[where]},
            device_id_type=MESH,
        )
        c.start()
        self.started.append(c)

    def got(self, k):
        pltpu.make_async_remote_copy(
            src_ref=self.landed.at[k],
            dst_ref=self.landed.at[k],
            send_sem=self.send.at[k],
            recv_sem=self.recv.at[k],
            device_id={"expert": self.targets["x"]},
            device_id_type=MESH,
        ).wait_recv()
        return self.landed[k].astype(F32)

    def begin(self):
        self.copy(0, self.src.at[self.place(2, 1)], "up")
        self.copy(1, self.src.at[self.place(2, 0)], "down")
        self.copy(3, self.src.at[self.place(3, 1)], "down")

    def relay(self):
        self.landed[0] = (self.own(1, 1) + self.got(0)).astype(BF)
        self.copy(2, self.landed.at[0], "up")
        self.copy(4, self.src.at[self.place(1, 0)], "up")
        self.landed[1] = (self.own(3, 0) + self.got(1)).astype(BF)
        self.copy(5, self.landed.at[1], "down")

    def cross(self):
        self.landed[2] = (self.own(0, 1) + self.got(2) + self.got(3)).astype(BF)
        self.copy(6, self.landed.at[2], "x")

    def total(self):
        return self.own(0, 0) + self.got(4) + self.got(5) + self.got(6)

    def finish(self):
        for c in self.started:
            c.wait_send()


class DenseSum:
    def __init__(self, grads, theirs, landed, send, recv):
        self.grads, self.theirs, self.landed, self.send, self.recv = grads, theirs, landed, send, recv
        x, y, core = dp_place()
        self.targets = {
            "x": dp_index(x + 1, y, core),
            "up": dp_index(x, y + 1, core),
            "down": dp_index(x, y + 3, core),
            "core": dp_index(x, y, core + 1),
        }
        self.slots = [dp_index(x + rx, y + ry, core) for rx, ry in SLOTS]
        self.others = [dp_index(x + rx, y + ry, core + 1) for rx, ry in SLOTS]
        self.started = []

    def descriptor(self, k, src, dst, where):
        return pltpu.make_async_remote_copy(
            src_ref=src,
            dst_ref=dst,
            send_sem=self.send.at[k],
            recv_sem=self.recv.at[k],
            device_id={"dp": self.targets[where]},
            device_id_type=MESH,
        )

    def copy(self, k, src, dst, where):
        c = self.descriptor(k, src, dst, where)
        c.start()
        self.started.append(c)

    def begin(self):
        for k in (6, 7, 4, 5, 2, 3, 1, 0):
            self.copy(8 + k, self.grads.at[self.others[k]], self.theirs.at[k], "core")

    def got(self, k):
        self.descriptor(k, self.landed.at[k], self.landed.at[k], "x").wait_recv()
        return self.landed[k].astype(F32)

    def both(self, k):
        self.descriptor(8 + k, self.theirs.at[k], self.theirs.at[k], "core").wait_recv()
        return self.grads[self.slots[k]].astype(F32) + self.theirs[k].astype(F32)

    def put(self, k, value, j, where):
        self.grads[self.slots[k]] = value.astype(BF)
        self.copy(j, self.grads.at[self.slots[k]], self.landed.at[j], where)

    def first(self):
        self.put(6, self.both(6), 0, "up")
        self.put(7, self.both(7), 1, "down")
        self.put(4, self.both(4), 2, "up")

    def second(self):
        self.put(5, self.both(5) + self.got(1), 3, "down")
        self.put(2, self.both(2) + self.got(0), 4, "up")
        self.put(3, self.both(3), 5, "down")

    def third(self):
        self.put(1, self.both(1) + self.got(2) + self.got(3), 6, "x")

    def total(self):
        return self.both(0) + self.got(4) + self.got(5) + self.got(6)

    def finish(self):
        for c in self.started:
            c.wait_send()


class ExpertSum:
    def __init__(self, keep, given, near, far, stage, sends, far_sends, ends, s_near, r_near, s_far, r_far, l_sem):
        self.keep, self.given, self.near, self.far, self.stage = keep, given, near, far, stage
        self.sends, self.far_sends, self.ends = sends, far_sends, ends
        self.s_near, self.r_near, self.s_far, self.r_far, self.l_sem = s_near, r_near, s_far, r_far, l_sem
        x, y, core = dp_place()
        self.targets = {
            "x": dp_index(x + 1, y, core),
            "up": dp_index(x, y + 1, core),
            "down": dp_index(x, y + 3, core),
        }
        self.started = []

    def descriptor(self, src, dst, send, recv, where):
        return pltpu.make_async_remote_copy(
            src_ref=src,
            dst_ref=dst,
            send_sem=send,
            recv_sem=recv,
            device_id={"dp": self.targets[where]},
            device_id_type=MESH,
        )

    def add(self, refs, out, count):
        def load(e):
            return [
                pltpu.make_async_copy(r.at[e], self.stage.at[e % 2, i], self.l_sem.at[e % 2, i])
                for i, r in enumerate(refs)
            ]

        for c in load(0):
            c.start()
        for e in range(count):
            if e + 1 < count:
                for c in load(e + 1):
                    c.start()
            for c in load(e):
                c.wait()
            acc = self.stage[e % 2, 0].astype(F32)
            for i in range(1, len(refs)):
                acc = acc + self.stage[e % 2, i].astype(F32)
            out[e] = acc.astype(out.dtype)

    def parts(self, k, first, count):
        span = pl.ds(first, count)
        return [self.keep.at[k, span], self.given.at[k, span]]

    def near_send(self, k, j, where, more=()):
        for i in more:
            self.near_got(i)
        out = self.sends.at[j]
        self.add(self.parts(k, 0, 3) + [self.near.at[i] for i in more], out, 3)
        c = self.descriptor(out, self.near.at[j], self.s_near.at[j], self.r_near.at[j], where)
        c.start()
        self.started.append(c)

    def near_got(self, j):
        self.descriptor(
            self.near.at[j], self.near.at[j], self.s_near.at[j], self.r_near.at[j], "x"
        ).wait_recv()

    def far_send(self, k, j, where, which=(0, 1), more=()):
        for i in which:
            for m in more:
                if m < 4 or m == 4 + i:
                    self.far_got(m, i)
            out = self.far_sends.at[j, pl.ds(i, 1)]
            self.add(
                self.parts(k, 3 + i, 1)
                + [self.far.at[m, pl.ds(i, 1)] for m in more if m < 4 or m == 4 + i],
                out,
                1,
            )
            c = self.descriptor(
                out,
                self.far.at[j, pl.ds(i, 1)],
                self.s_far.at[j, i],
                self.r_far.at[j, i],
                where,
            )
            c.start()
            self.started.append(c)

    def far_got(self, j, i):
        ref = self.far.at[j, pl.ds(i, 1)]
        self.descriptor(ref, ref, self.s_far.at[j, i], self.r_far.at[j, i], "x").wait_recv()

    def near_end(self):
        for j in (4, 5, 6):
            self.near_got(j)
        self.add(
            self.parts(0, 0, 3) + [self.near.at[j] for j in (4, 5, 6)],
            self.ends,
            3,
        )

    def far_end(self):
        for j in (0, 6, 7):
            for i in range(2):
                self.far_got(j, i)
        self.add(
            self.parts(0, 3, 2) + [self.far.at[j] for j in (0, 6, 7)], self.ends, 2
        )

    def finish(self):
        for c in self.started:
            c.wait_send()


def last_kernel(*refs):
    (
        back_part,
        inner_part,
        out_part,
        keep,
        given,
        tokens_all,
        normed_all,
        small_hbm,
        dense_hbm,
        tokens_hbm,
        cot_hbm,
    ) = refs[:11]
    kept_in = refs[11:22]
    mixed_out, grad_tokens_out, expert_ref, small_own, output_out, near, far = refs[22:29]
    kept_refs = refs[29:40]
    (
        query_ref,
        key_ref,
        value_ref,
        log_ref,
        attended_ref,
        middle_ref,
        normed_two_ref,
        gates_ref,
        cos_ref,
        sin_ref,
        start_ref,
    ) = kept_refs
    (
        tokens,
        cot,
        mixed_ref,
        grad_tokens_ref,
        output_own,
        inner_in,
        gates_grad,
        logits_grad,
        small,
        dense,
        grad_small,
        normed,
        token_rows,
        grad_normed,
        att_send,
        att_in,
        grad_query,
        grad_key,
        grad_value,
        grad_qkv,
        gain_sum,
        grad_middle_ref,
        z_own,
        z_landed,
        y_landed,
        stage,
        sends,
        far_sends,
        ends,
        small_theirs,
        small_landed,
        dense_theirs,
        dense_landed,
        small_cut,
        dense_cut,
        dense_in,
        s_direct,
        r_direct,
        s_reduce,
        r_reduce,
        s_dense,
        r_dense,
        s_near,
        r_near,
        s_far,
        r_far,
        l_sem,
        l_add,
    ) = refs[40:]
    _, peers = expert_peers()
    x, y, core = dp_place()
    me = lax.axis_index("expert")
    signal_all(
        peers,
        [
            dp_index(x + 1, y, core),
            dp_index(x, y + 1, core),
            dp_index(x, y + 3, core),
            dp_index(x, y, core + 1),
        ],
    )

    def direct(i, src, out, mode):
        part = expert_copies(
            [src], [out], [mode], s_direct.at[pl.ds(i, 1)], r_direct.at[pl.ds(i, 1)]
        ) + own_copies([src], [out], [mode], l_sem.at[pl.ds(i, 1)])
        for c in part:
            c.start()
        return part

    def settle(part):
        for c in part:
            c.wait()

    def load(src, dst, i):
        c = pltpu.make_async_copy(src, dst, l_sem.at[i])
        c.start()
        return c

    OWN = ((1, 1), (3, 0), (0, 1), (0, 0))

    def own_blocks(reduce, src, base):
        return [
            load(src.at[reduce.place(*d)], z_own.at[i], base + i) for i, d in enumerate(OWN)
        ]

    def from_own(dz, dx):
        return z_own[OWN.index((dz, dx))].astype(F32)

    back = Reduce(back_part, from_own, z_landed, s_reduce.at[0], r_reduce.at[0])
    back.begin()
    loads = own_blocks(back, back_part, 8)
    inner = direct(0, inner_part, inner_in, "exchange")
    kept = [load(a, b, 16 + i) for i, (a, b) in enumerate(zip(kept_in, kept_refs))]
    kept = kept + [load(tokens_hbm, tokens, 27), load(cot_hbm, cot, 28)]
    loads_small = load(small_hbm, small, 4)
    loads_dense = load(dense_hbm, dense, 5)
    loads_normed = load(normed_all, normed, 6)
    experts = ExpertSum(
        keep, given, near, far, stage, sends, far_sends, ends, s_near, r_near, s_far, r_far, l_add
    )
    experts.near_send(6, 0, "up")
    experts.near_send(7, 1, "down")
    settle(loads)
    back.relay()
    experts.far_send(7, 3, "x")
    experts.far_send(4, 1, "x", (0,))
    experts.near_send(4, 2, "up")
    back.cross()
    experts.near_send(5, 3, "down", (1,))
    experts.far_send(6, 4, "up", (0,), (3,))
    experts.far_send(6, 5, "down", (1,), (3,))
    experts.near_send(2, 4, "up", (0,))
    experts.near_send(3, 5, "down")
    experts.far_send(4, 1, "x", (1,))
    settle(inner)
    settle([loads_small, loads_dense] + kept)

    for j in range(PEERS):
        gates_grad[LOCAL * j : LOCAL * (j + 1), :] = inner_in[j, 0:LOCAL, :]
    gates = gates_ref[...]
    grad_gates = gates_grad[...]
    logits_grad[...] = jnp.zeros_like(logits_grad)
    logits_grad[ROUTER - 256 : GAINS - 256, :] = gates * (
        grad_gates - jnp.sum(gates * grad_gates, axis=0, keepdims=True)
    )
    pick = (
        lax.broadcasted_iota(jnp.int32, (8, SLICE), 1)
        == lax.broadcasted_iota(jnp.int32, (8, SLICE), 0) + GAINS
    )
    gains = dot(pick.astype(F32).astype(BF), small[...].reshape(DIM, SLICE), ((1,), (1,)))
    gain_one, gain_two = gains[0:1], gains[1:2]
    grad_logits = logits_grad[...].astype(BF)
    router = small[:, :, 256:SLICE].reshape(DIM, SLICE - 256)
    grad = back.total() + dot(grad_logits, router, ((0,), (1,)))
    middle = middle_ref[...]
    scale_two = lax.rsqrt(jnp.mean(middle * middle, axis=-1, keepdims=True) + epsilon)
    gain_sum[0] = jnp.sum((grad * middle * scale_two).reshape(TOK // 8, 8, DIM), axis=0)
    grad_middle = cot[...].astype(F32) + norm_back(middle, scale_two, gain_two, grad)
    grad_middle_ref[...] = grad_middle
    grad_branch = grad_middle.astype(BF)
    for j in range(PEERS):
        att_send[j] = dot(
            grad_branch, dense[2 * j : 2 * j + 2].reshape(QS, DIM), ((1,), (1,))
        ).astype(BF)
    back.finish()
    exchanged = direct(1, att_send, att_in, "exchange")
    experts.far_send(5, 2, "x")
    for j in range(PEERS):
        dense[2 * j : 2 * j + 2] = (
            dot(attended_ref[j], grad_branch, ((0,), (0,))).astype(BF).reshape(2, ROWS, DIM)
        )
    settle(exchanged)
    out = Reduce(out_part, from_own, y_landed, s_reduce.at[1], r_reduce.at[1])
    out.begin()
    loads = own_blocks(out, out_part, 8)
    sums = [
        DenseSum(dense, dense_theirs, dense_landed, s_dense.at[0], r_dense.at[0]),
        DenseSum(grad_small, small_theirs, small_landed, s_dense.at[1], r_dense.at[1]),
    ]
    sums[0].begin()
    experts.far_send(1, 0, "x")

    grad_key[...] = jnp.zeros_like(grad_key)
    grad_value[...] = jnp.zeros_like(grad_value)

    def attend(width, i, _):
        queries = query_ref[i]
        incoming = att_in[i]
        incoming = jnp.concatenate(
            [incoming[:, h * HEAD : (h + 1) * HEAD] for h in range(REP)], axis=0
        )
        scores = dot(queries, key_ref[0:width, :], ((1,), (1,))) * HEAD ** (-0.5)
        keys = lax.broadcasted_iota(jnp.int32, (TOK, width), 1)
        rows = lax.broadcasted_iota(jnp.int32, (TOK, width), 0) + i * TOK
        begins = start_ref[pl.ds(pl.multiple_of(i * TOK, TOK), TOK), :][:, :1]
        allowed = (keys <= rows) & (keys >= begins)
        scores = jnp.where(allowed[None], scores.reshape(REP, TOK, width), masked_score)
        probs = jnp.exp(scores.reshape(REP * TOK, width) - log_ref[i][:, :1])
        grad_probs = dot(incoming, value_ref[0:width, :], ((1,), (1,)))
        inner_sum = jnp.sum(probs * grad_probs, axis=-1, keepdims=True)
        grad_scores = (probs * (grad_probs - inner_sum)).astype(BF)
        grad_query[i] = dot(grad_scores, key_ref[0:width, :], ((1,), (0,))) * HEAD ** (-0.5)
        grad_key[0:width, :] += dot(grad_scores, queries, ((0,), (0,))) * HEAD ** (-0.5)
        grad_value[0:width, :] += dot(probs.astype(BF), incoming, ((0,), (0,)))
        return _

    lax.fori_loop(0, 4, functools.partial(attend, GROUP // 2), 0)
    settle(loads)
    out.relay()
    experts.near_send(1, 6, "x", (2, 3))
    sums[0].first()
    lax.fori_loop(4, 8, functools.partial(attend, GROUP), 0)
    out.cross()

    settle([loads_normed])
    gain_sum[1] = jnp.zeros((8, DIM), F32)

    def project(i, _):
        span = pl.ds(pl.multiple_of(i * 2 * TOK, 2 * TOK), 2 * TOK)
        rows = load(tokens_all.at[pl.ds(2 * i, 2)], token_rows, 7)
        cosine, sine = cos_ref[span, :], sin_ref[span, :]
        lane = lax.broadcasted_iota(jnp.int32, (2 * TOK, 128), 1)
        heads = [
            jnp.concatenate(
                [grad_query[2 * i + b, h * TOK : (h + 1) * TOK, :] for b in range(2)], axis=0
            )
            for h in range(REP)
        ]
        turned = []
        for pair in ((heads[0], heads[1]), (heads[2], grad_key[span, :])):
            v = jnp.concatenate(pair, axis=1)
            other = jnp.where(lane % HEAD < HEAD // 2, pltpu.roll(v, 96, 1), pltpu.roll(v, 32, 1))
            turned.append((v * cosine - other * sine).astype(BF))
        tail = jnp.concatenate(
            [grad_value[span, :], jnp.zeros((2 * TOK, SLICE - ROUTER), F32)], axis=1
        ).astype(BF)
        low = jnp.concatenate(turned + [tail], axis=1)
        grad_qkv[span, :] = low
        grad = dot(low, small[...].reshape(DIM, SLICE), ((1,), (1,)))
        grad_normed[pl.ds(2 * i, 2)] = grad.astype(BF).reshape(2, TOK, DIM)
        rows.wait()
        values = token_rows[...].reshape(2 * TOK, DIM).astype(F32)
        scale = lax.rsqrt(jnp.mean(values * values, axis=-1, keepdims=True) + epsilon)
        gain_sum[1] += jnp.sum((grad * values * scale).reshape(2 * TOK // 8, 8, DIM), axis=0)
        return _

    lax.fori_loop(0, 4, project, 0)

    def from_grad(dz, dx):
        return grad_normed[first.place(dz, dx)].astype(F32)

    first = Reduce(grad_normed, from_grad, z_landed, s_reduce.at[2], r_reduce.at[2])
    first.begin()

    lanes = lax.broadcasted_iota(jnp.int32, (8, 128), 1)
    marks = [(lanes == GAINS - 256 + i).astype(F32).astype(BF) for i in range(2)]
    for c in range(4):
        span = slice(c * 384, (c + 1) * 384)
        part = dot(normed[:, :, span].reshape(GROUP, 384), grad_qkv[...], ((0,), (0,)))
        extra = dot(normed_two_ref[:, span], grad_logits, ((0,), (1,)))
        for i in range(2):
            value = gain_sum[1 - i, :, span]
            high = value.astype(BF)
            rest = (value - high.astype(F32)).astype(BF)
            extra = extra + dot(high, marks[i], ((0,), (0,))) + dot(rest, marks[i], ((0,), (0,)))
        grad_small[4 * c : 4 * c + 4, :, 0:256] = (
            part[:, 0:256].astype(BF).reshape(4, ROWS, 256)
        )
        grad_small[4 * c : 4 * c + 4, :, 256:SLICE] = (
            (part[:, 256:SLICE] + extra).astype(BF).reshape(4, ROWS, SLICE - 256)
        )
    sums[1].begin()
    first.relay()
    sums[0].second()
    sums[1].first()
    experts.far_send(2, 6, "up", (0, 1), (1, 4))
    experts.far_send(3, 7, "down", (0, 1), (2, 5))
    mixed_ref[...] = (middle_ref[...] + out.total()).astype(BF)
    saves = [load(mixed_ref, mixed_out, 29)]
    first.cross()
    sums[0].third()
    sums[1].second()
    sums[1].third()
    values = tokens[...].astype(F32)
    scale = lax.rsqrt(jnp.mean(values * values, axis=-1, keepdims=True) + epsilon)
    grad_tokens_ref[...] = grad_middle_ref[...] + norm_back(values, scale, gain_one, first.total())
    saves.append(load(grad_tokens_ref, grad_tokens_out, 30))
    total = sums[0].total()
    for j in range(PEERS):
        dense_cut[j] = total[12 * j : 12 * (j + 1)]
    total = sums[1].total()
    for j in range(PEERS):
        small_cut[j] = total[12 * j : 12 * (j + 1)]
    cuts = direct(2, dense_cut, dense_in, "exchange") + direct(3, small_cut, small_own, "exchange")
    experts.far_end()
    saved = load(ends.at[pl.ds(0, 2)], expert_ref.at[pl.ds(3, 2)], 4)
    saved.wait()
    experts.near_end()
    saved = load(ends, expert_ref.at[pl.ds(0, 3)], 4)
    settle(cuts)
    acc = dense_in[0]
    for j in range(1, PEERS):
        acc = acc + dense_in[j]
    output_own[...] = acc
    saves.append(load(output_own, output_out, 31))
    for part in (out, first, sums[0], sums[1], experts):
        part.finish()
    settle(saves + [saved])


def last_phase(*args):
    hbm = pl.BlockSpec(memory_space=pltpu.HBM)
    shape, dma = jax.ShapeDtypeStruct, pltpu.SemaphoreType.DMA
    blocks = (PEERS, TOK, DIM)
    piece = (3 * ROWS, FFE)
    outs = [
        (shape((TOK, DIM), BF), hbm),
        (shape((TOK, DIM), F32), hbm),
        (shape((LOCAL,) + piece, F32), hbm),
        (shape((PEERS, 12, SLICE), F32), hbm),
        (shape((12, DIM), F32), hbm),
        (shape((7, 3) + piece, BF), hbm),
        (shape((8, 2) + piece, BF), hbm),
    ]
    return pl.pallas_call(
        last_kernel,
        out_shape=[o[0] for o in outs],
        in_specs=[hbm] * 22,
        out_specs=[o[1] for o in outs],
        scratch_shapes=[pltpu.VMEM(k.shape, k.dtype) for k in KEPT]
        + [
            pltpu.VMEM((TOK, DIM), BF),
            pltpu.VMEM((TOK, DIM), BF),
            pltpu.VMEM((TOK, DIM), BF),
            pltpu.VMEM((TOK, DIM), F32),
            pltpu.VMEM((12, DIM), F32),
            pltpu.VMEM((PEERS, 8, TOK), F32),
            pltpu.VMEM((EXPERTS, TOK), F32),
            pltpu.VMEM((SLICE - 256, TOK), F32),
            pltpu.VMEM((DP, ROWS, SLICE), BF),
            pltpu.VMEM((DP, ROWS, DIM), BF),
            pltpu.VMEM((DP, ROWS, SLICE), BF),
            pltpu.VMEM(blocks, BF),
            pltpu.VMEM((2, TOK, DIM), BF),
            pltpu.VMEM(blocks, BF),
            pltpu.VMEM((PEERS, TOK, QS), BF),
            pltpu.VMEM((PEERS, TOK, QS), BF),
            pltpu.VMEM((PEERS, REP * TOK, HEAD), F32),
            pltpu.VMEM((GROUP, HEAD), F32),
            pltpu.VMEM((GROUP, HEAD), F32),
            pltpu.VMEM((GROUP, SLICE), BF),
            pltpu.VMEM((2, 8, DIM), F32),
            pltpu.VMEM((TOK, DIM), F32),
            pltpu.VMEM((4, TOK, DIM), BF),
            pltpu.VMEM((7, TOK, DIM), BF),
            pltpu.VMEM((7, TOK, DIM), BF),
            pltpu.VMEM((2, 5) + piece, BF),
            pltpu.VMEM((7, 3) + piece, BF),
            pltpu.VMEM((8, 2) + piece, BF),
            pltpu.VMEM((3,) + piece, F32),
            pltpu.VMEM((8, ROWS, SLICE), BF),
            pltpu.VMEM((7, ROWS, SLICE), BF),
            pltpu.VMEM((8, ROWS, DIM), BF),
            pltpu.VMEM((7, ROWS, DIM), BF),
            pltpu.VMEM((PEERS, 12, SLICE), F32),
            pltpu.VMEM((PEERS, 12, DIM), F32),
            pltpu.VMEM((PEERS, 12, DIM), F32),
            dma((4, 7)),
            dma((4, 7)),
            dma((3, 7)),
            dma((3, 7)),
            dma((2, 16)),
            dma((2, 16)),
            dma((7,)),
            dma((7,)),
            dma((8, 2)),
            dma((8, 2)),
            dma((32,)),
            dma((2, 5)),
        ],
        compiler_params=pltpu.CompilerParams(
            collective_id=3, has_side_effects=True, vmem_limit_bytes=63 << 20
        ),
        cost_estimate=lasting(120),
    )(*args)


def experts_kernel(*refs):
    (rows_ref, cot_ref, slot_ref, gate_ref), refs = refs[:4], refs[4:]
    pieces, refs = refs[0], refs[1:]
    (out_ref, back_ref, inner_ref, keep_ref, given_ref), refs = refs[:5], refs[5:]
    xg, cg, weights, grads, gates, inners, wsem, gsem, rsem = refs
    x, y, core = dp_place()
    other = dp_index(x, y, core + 1)
    signal_all([], [other])

    def load(e, b):
        return pltpu.make_async_copy(pieces.at[:, e], weights.at[b], wsem.at[b])

    def kept(e, b):
        return [
            pltpu.make_async_copy(
                grads.at[b, dp_index(x + rx, y + ry, core)], keep_ref.at[k, e], gsem.at[b, k]
            )
            for k, (rx, ry) in enumerate(SLOTS)
        ]

    def given(e, b):
        return [
            pltpu.make_async_remote_copy(
                src_ref=grads.at[b, dp_index(x + rx, y + ry, core + 1)],
                dst_ref=given_ref.at[k, e],
                send_sem=gsem.at[b, 8 + k],
                recv_sem=rsem.at[e, k],
                device_id={"dp": other},
                device_id_type=MESH,
            )
            for k, (rx, ry) in enumerate(SLOTS)
        ]

    def stored(e, b):
        for c in kept(e, b):
            c.wait()
        for c in given(e, b):
            c.wait_send()

    load(0, 0).start()

    def onehot(b):
        places = lax.broadcasted_iota(jnp.int32, (CAP, TOK), 0).astype(F32)
        return [(places == slot_ref[b, e : e + 1, :]) for e in range(LOCAL)]

    def collect(b, _):
        hot = onehot(b)
        pick = jnp.concatenate([h.astype(F32) for h in hot], axis=0).astype(BF)
        xg[b] = dot(pick, rows_ref[b], ((1,), (0,))).astype(BF)
        cg[b] = dot(pick, cot_ref[b], ((1,), (0,))).astype(BF)
        for e in range(LOCAL):
            g = jnp.sum(jnp.where(hot[e], gate_ref[b, e : e + 1, :], 0.0), axis=1, keepdims=True)
            gates[e, pl.ds(b * CAP, CAP), :] = jnp.broadcast_to(g, (CAP, 128))
        return _

    lax.fori_loop(0, PEERS, collect, 0)

    def expert(e, _):
        b = lax.rem(e, 2)
        load(e, b).wait()

        @pl.when(e + 1 < LOCAL)
        def _next():
            load(e + 1, 1 - b).start()

        @pl.when(e >= 2)
        def _free():
            stored(e - 2, b)

        span = pl.ds(pl.multiple_of(e * CAP, CAP), CAP)
        rows = xg[:, span, :].reshape(PEERS * CAP, DIM)
        cot = cg[:, span, :].reshape(PEERS * CAP, DIM)
        gate = gates[e][:, :1]
        w_gate = weights[b, :, 0:96, :].reshape(DIM, FFE)
        gate_act = dot(rows, w_gate, ((1,), (0,)))
        w_up = weights[b, :, 96:192, :].reshape(DIM, FFE)
        up_act = dot(rows, w_up, ((1,), (0,)))
        sig = 1.0 / (1.0 + jnp.exp(-gate_act))
        silu = gate_act * sig
        hidden = (silu * up_act).astype(BF)
        grad_out = (cot.astype(F32) * gate).astype(BF)
        inner = jnp.zeros((PEERS * CAP, 1), F32)
        grad_hidden = jnp.zeros((PEERS * CAP, FFE), F32)
        gated = []
        for k in range(3):
            lanes = slice(k * FFE, (k + 1) * FFE)
            w_down = weights[b, :, 192 + 32 * k : 224 + 32 * k, :].reshape(FFE, FFE)
            part = dot(hidden, w_down, ((1,), (0,))).astype(BF).astype(F32)
            inner = inner + jnp.sum(part * cot[:, lanes].astype(F32), axis=1, keepdims=True)
            gated.append((part * gate).astype(BF))
            grad_hidden = grad_hidden + dot(grad_out[:, lanes], w_down, ((1,), (1,)))
            grads[b, :, 192 + 32 * k : 224 + 32 * k, :] = (
                dot(hidden, grad_out[:, lanes], ((0,), (0,))).astype(BF).reshape(DP, 32, FFE)
            )
        inners[e] = jnp.broadcast_to(inner, (PEERS * CAP, 128))
        grad_gate = (grad_hidden * up_act * sig * (1.0 + gate_act * (1.0 - sig))).astype(BF)
        grad_up = (grad_hidden * silu).astype(BF)
        grads[b, :, 0:96, :] = (
            dot(rows, grad_gate, ((0,), (0,))).astype(BF).reshape(DP, ROWS, FFE)
        )
        grads[b, :, 96:192, :] = (
            dot(rows, grad_up, ((0,), (0,))).astype(BF).reshape(DP, ROWS, FFE)
        )
        for c in kept(e, b) + given(e, b):
            c.start()
        back = dot(grad_gate, w_gate, ((1,), (1,))) + dot(grad_up, w_up, ((1,), (1,)))
        xg[:, span, :] = back.astype(BF).reshape(PEERS, CAP, DIM)
        for k in range(3):
            cg[:, span, k * FFE : (k + 1) * FFE] = gated[k].reshape(PEERS, CAP, FFE)
        return _

    lax.fori_loop(0, LOCAL, expert, 0)

    def combine(b, _):
        hot = onehot(b)
        pick = jnp.concatenate([h.astype(F32) for h in hot], axis=0).astype(BF)
        out_ref[b] = dot(pick, cg[b], ((0,), (0,))).astype(BF)
        back_ref[b] = dot(pick, xg[b], ((0,), (0,))).astype(BF)
        lines = []
        for e in range(LOCAL):
            value = inners[e, pl.ds(b * CAP, CAP), :][:, :1]
            lines.append(jnp.sum(jnp.where(hot[e], value, 0.0), axis=0, keepdims=True))
        inner_ref[b] = jnp.concatenate(lines + [jnp.zeros((8 - LOCAL, TOK), F32)], axis=0)
        return _

    lax.fori_loop(0, PEERS, combine, 0)
    for e in (LOCAL - 2, LOCAL - 1):
        stored(e, e % 2)
    for e in range(LOCAL):
        for c in given(e, e % 2):
            c.wait_recv()


def run_experts(rows, cot, slots, gates, pieces):
    vmem = pl.BlockSpec(memory_space=pltpu.VMEM)
    piece = (LOCAL, 3 * ROWS, FFE)
    return pl.pallas_call(
        experts_kernel,
        out_shape=[
            jax.ShapeDtypeStruct((PEERS, TOK, DIM), BF),
            jax.ShapeDtypeStruct((PEERS, TOK, DIM), BF),
            jax.ShapeDtypeStruct((PEERS, 8, TOK), F32),
            jax.ShapeDtypeStruct((8,) + piece, BF),
            jax.ShapeDtypeStruct((8,) + piece, BF),
        ],
        in_specs=[vmem] * 4 + any_specs(1),
        out_specs=[vmem] * 3 + any_specs(2),
        scratch_shapes=[
            pltpu.VMEM((PEERS, LOCAL * CAP, DIM), BF),
            pltpu.VMEM((PEERS, LOCAL * CAP, DIM), BF),
            pltpu.VMEM((2, DP, 3 * ROWS, FFE), BF),
            pltpu.VMEM((2, DP, 3 * ROWS, FFE), BF),
            pltpu.VMEM((LOCAL, PEERS * CAP, 128), F32),
            pltpu.VMEM((LOCAL, PEERS * CAP, 128), F32),
            pltpu.SemaphoreType.DMA((2,)),
            pltpu.SemaphoreType.DMA((2, 16)),
            pltpu.SemaphoreType.DMA((LOCAL, 8)),
        ],
        compiler_params=pltpu.CompilerParams(
            collective_id=2, has_side_effects=True, vmem_limit_bytes=63 << 20
        ),
        cost_estimate=pl.CostEstimate(
            flops=20_000_000_000, bytes_accessed=60_000_000, transcendentals=700_000
        ),
    )(rows, cot, slots, gates, pieces)


def finish_kernel(mixed, tokens, experts, small, output, *refs):
    outs, (mixed_ref, tokens_ref, experts_ref, small_ref, output_ref, cut_ref, sem) = (
        refs[:10],
        refs[10:],
    )
    mixed_out, tokens_out, q_out, k_out, v_out, output_out, tail_out, gate, up, down = outs
    loads = [
        pltpu.make_async_copy(src, dst, sem.at[13 + i])
        for i, (src, dst) in enumerate(
            (
                (small, small_ref),
                (experts, experts_ref),
                (tokens, tokens_ref),
                (mixed, mixed_ref),
                (output, output_ref),
            )
        )
    ]
    for c in loads:
        c.start()
    for c in loads[1:]:
        c.wait()
    copies = [
        pltpu.make_async_copy(mixed_ref, mixed_out, sem.at[1]),
        pltpu.make_async_copy(tokens_ref, tokens_out, sem.at[2]),
        pltpu.make_async_copy(output_ref, output_out, sem.at[3]),
        pltpu.make_async_copy(experts_ref.at[:, pl.ds(0, ROWS)], gate, sem.at[4]),
        pltpu.make_async_copy(experts_ref.at[:, pl.ds(ROWS, ROWS)], up, sem.at[5]),
    ] + [
        pltpu.make_async_copy(
            experts_ref.at[:, pl.ds(2 * ROWS + 32 * k, 32)],
            down.at[:, :, pl.ds(k * FFE, FFE)],
            sem.at[6 + k],
        )
        for k in range(3)
    ]
    for c in copies:
        c.start()
    loads[0].wait()
    total = small_ref[0]
    for j in range(1, PEERS):
        total = total + small_ref[j]
    cut_ref[...] = jnp.concatenate(
        [small_ref[j, :, :QS] for j in range(PEERS)]
        + [small_ref[j, :, QS : QS + HEAD] for j in range(PEERS)]
        + [small_ref[j, :, QS + HEAD : ROUTER] for j in range(PEERS)]
        + [total[:, 256:SLICE]],
        axis=1,
    )
    widths = (DIM, KV_HEADS * HEAD, KV_HEADS * HEAD, SLICE - 256)
    begins = (0, DIM, DIM + KV_HEADS * HEAD, DIM + 2 * KV_HEADS * HEAD)
    for i, ref in enumerate((q_out, k_out, v_out, tail_out)):
        c = pltpu.make_async_copy(cut_ref.at[:, pl.ds(begins[i], widths[i])], ref, sem.at[9 + i])
        c.start()
        copies.append(c)
    for c in copies:
        c.wait()


def finish(*args):
    shape = jax.ShapeDtypeStruct
    width = KV_HEADS * HEAD
    return pl.pallas_call(
        finish_kernel,
        out_shape=[
            shape((TOK, DIM), BF),
            shape((TOK, DIM), F32),
            shape((12, DIM), F32),
            shape((12, width), F32),
            shape((12, width), F32),
            shape((12, DIM), F32),
            shape((12, SLICE - 256), F32),
            shape((LOCAL, ROWS, FFE), F32),
            shape((LOCAL, ROWS, FFE), F32),
            shape((LOCAL, 32, DIM), F32),
        ],
        in_specs=any_specs(5),
        out_specs=any_specs(10),
        scratch_shapes=[
            pltpu.VMEM((TOK, DIM), BF),
            pltpu.VMEM((TOK, DIM), F32),
            pltpu.VMEM((LOCAL, 3 * ROWS, FFE), F32),
            pltpu.VMEM((PEERS, 12, SLICE), F32),
            pltpu.VMEM((12, DIM), F32),
            pltpu.VMEM((12, DIM + 2 * width + SLICE - 256), F32),
            pltpu.SemaphoreType.DMA((18,)),
        ],
        compiler_params=pltpu.CompilerParams(vmem_limit_bytes=63 << 20),
    )(*args)


def norm_back(values, row_scale, gain_vector, grad_normed):
    weighted = grad_normed * gain_vector
    return row_scale * weighted - values * row_scale**3 * jnp.mean(
        weighted * values, axis=-1, keepdims=True
    )


def local(
    tokens,
    cotangent,
    seq_lengths,
    expert_ids,
    w_query,
    w_key,
    w_value,
    w_output,
    norm_one,
    norm_two,
    w_router,
    w_gate,
    w_up,
    w_down,
):
    tail = jnp.concatenate(
        [w_router, norm_one[:, None], norm_two[:, None], jnp.zeros((12, SLICE - GAINS - 2), BF)],
        axis=1,
    )
    (
        pieces,
        cot_all,
        slots_all,
        rows_all,
        gates_all,
        tokens_all,
        normed_all,
        slices_all,
        output_all,
        *kept,
    ) = first_phase(
        w_query,
        w_key,
        w_value,
        tail,
        w_output,
        tokens,
        cotangent,
        expert_ids,
        seq_lengths,
        w_gate,
        w_up,
        w_down,
    )
    out_part, back_part, inner_part, keep, given = run_experts(
        rows_all, cot_all, slots_all, gates_all, pieces
    )
    mixed, grad_tokens, expert_grads, small_own, output_own, _, _ = last_phase(
        back_part,
        inner_part,
        out_part,
        keep,
        given,
        tokens_all,
        normed_all,
        slices_all,
        output_all,
        tokens,
        cotangent,
        *kept,
    )
    mixed, grad_tokens, query, key, value, output, rest, gate, up, down = finish(
        mixed, grad_tokens, expert_grads, small_own, output_own
    )
    rest = rest[:, ROUTER - 256 :]
    return (
        mixed,
        grad_tokens,
        query,
        key,
        value,
        output,
        rest[:, EXPERTS],
        rest[:, EXPERTS + 1],
        rest[:, :EXPERTS],
        gate,
        up,
        down,
    )


def solution(mesh):
    both = P(("dp", "expert"), None)
    line = P(("dp", "expert"))
    cube = P("expert", "dp", None)
    in_specs = (both, both, P("dp", None), both, both, both, both, both)
    in_specs = in_specs + (line, line, both, cube, cube, cube)
    out_specs = (both,) * 6 + (line, line, both, cube, cube, cube)
    return jax.shard_map(local, mesh=mesh, in_specs=in_specs, out_specs=out_specs, check_vma=False)
```

```python
import functools
import math

import jax
import jax.numpy as jnp
from jax import lax
from jax.experimental import pallas as pl
from jax.experimental.pallas import tpu as pltpu
from jax.sharding import PartitionSpec as P

HEADS = 24
KV_HEADS = 8
HEAD = 64
DIM = 1536
FFE = 512
EXPERTS = 40
LOCAL = 5
CAP = 32
TOK = 128
PEERS = 8
DP = 16
GROUP = TOK * PEERS
REP = HEADS // KV_HEADS
SLICE = 384
QS = REP * HEAD
ROWS = 96
ROUTER = QS + 2 * HEAD
GAINS = ROUTER + EXPERTS

epsilon = 1e-06
rope_base = 10000.0
masked_score = -1e30
MESH = pl.DeviceIdType.MESH
BF = jnp.bfloat16
F32 = jnp.float32

RELATIVE = ((2, 1), (2, 0), (1, 1), (3, 1), (0, 1), (1, 0), (3, 0))
SLOTS = ((0, 0), (1, 0), (0, 1), (0, 3), (1, 1), (1, 3), (0, 2), (1, 2))


def expert_peers():
    me = lax.axis_index("expert")
    z, x = me // 2, me % 2
    return me, [(z + rz) % 4 * 2 + (x + rx) % 2 for rz, rx in RELATIVE]


def dp_place():
    d = lax.axis_index("dp")
    return d // 8, (d // 2) % 4, d % 2


def dp_index(x, y, core):
    return (x % 2 * 4 + y % 4) * 2 + core % 2


def signal_all(expert_ids, dp_ids):
    barrier = pltpu.get_barrier_semaphore()
    for p in expert_ids:
        pl.semaphore_signal(barrier, inc=1, device_id={"expert": p}, device_id_type=MESH)
    for p in dp_ids:
        pl.semaphore_signal(barrier, inc=1, device_id={"dp": p}, device_id_type=MESH)
    pl.semaphore_wait(barrier, len(expert_ids) + len(dp_ids))


def any_specs(count):
    return [pl.BlockSpec(memory_space=pltpu.HBM)] * count


def expert_copies(ins, outs, modes, send, recv):
    me, peers = expert_peers()
    copies = []
    for r, p in enumerate(peers):
        for i, mode in enumerate(modes):
            copies.append(
                pltpu.make_async_remote_copy(
                    src_ref=ins[i] if mode == "gather" else ins[i].at[p],
                    dst_ref=outs[i].at[me],
                    send_sem=send.at[i, r],
                    recv_sem=recv.at[i, r],
                    device_id={"expert": p},
                    device_id_type=MESH,
                )
            )
    return copies


def own_copies(ins, outs, modes, sems):
    me = lax.axis_index("expert")
    return [
        pltpu.make_async_copy(
            ins[i] if mode == "gather" else ins[i].at[me], outs[i].at[me], sems.at[i]
        )
        for i, mode in enumerate(modes)
    ]


def lasting(us):
    return pl.CostEstimate(flops=us * 1_000_000_000, bytes_accessed=0, transcendentals=0)


class Gather:
    def __init__(self, src, out, send, recv, local):
        self.src, self.out, self.send, self.recv, self.local = src, out, send, recv, local
        me = lax.axis_index("expert")
        z, x = me // 2, me % 2

        def place(dz, dx):
            return (z + dz) % 4 * 2 + (x + dx) % 2

        self.slots = [
            place(0, 1),
            place(3, 0),
            place(1, 0),
            place(3, 1),
            place(1, 1),
            place(2, 0),
            place(2, 1),
        ]
        self.me = me
        x, up, down = place(0, 1), place(1, 0), place(3, 0)
        self.moves = ((None, x), (None, up), (None, down), (0, up), (0, down), (1, up), (4, down))
        self.started = []

    def descriptor(self, k, src, slot, target):
        return pltpu.make_async_remote_copy(
            src_ref=src,
            dst_ref=self.out.at[slot],
            send_sem=self.send.at[k],
            recv_sem=self.recv.at[k],
            device_id={"expert": target},
            device_id_type=MESH,
        )

    def begin(self):
        self.own = pltpu.make_async_copy(self.src, self.out.at[self.me], self.local)
        self.own.start()

    def issue(self, k):
        source, target = self.moves[k]
        slot = self.me if source is None else self.slots[source]
        src = self.src if source is None else self.out.at[slot]
        c = self.descriptor(k, src, slot, target)
        c.start()
        self.started.append(c)

    def arrive(self, k):
        self.descriptor(k, self.src, self.slots[k], self.moves[0][1]).wait_recv()


class Line:
    def __init__(self, src, view, moves, send, recv):
        self.src, self.view, self.send, self.recv = src, view, send, recv
        x, y, core = dp_place()
        self.targets = {
            "x": dp_index(x + 1, y, core),
            "up": dp_index(x, y + 1, core),
            "down": dp_index(x, y + 3, core),
            "core": dp_index(x, y, core + 1),
        }
        self.moves = dict(moves)
        for k in range(8):
            self.moves[8 + k] = (k, "core")
        self.slots = [dp_index(x + rx, y + ry, core + c) for c in range(2) for rx, ry in SLOTS]
        self.started = []

    def descriptor(self, k, src, slot, where):
        return pltpu.make_async_remote_copy(
            src_ref=src,
            dst_ref=self.view(slot),
            send_sem=self.send.at[k],
            recv_sem=self.recv.at[k],
            device_id={"dp": self.targets[where]},
            device_id_type=MESH,
        )

    def issue(self, k):
        source, where = self.moves[k]
        slot = self.slots[source]
        src = self.src if source == 0 else self.view(slot)
        c = self.descriptor(k, src, slot, where)
        c.start()
        self.started.append(c)

    def arrive(self, k):
        slot = self.slots[k]
        self.descriptor(k, self.view(slot), slot, "x").wait_recv()


X_FIRST = {
    1: (0, "x"),
    2: (0, "down"),
    3: (0, "up"),
    4: (1, "down"),
    5: (1, "up"),
    6: (3, "up"),
    7: (4, "down"),
}
Y_FIRST = {
    1: (0, "x"),
    2: (0, "down"),
    3: (0, "up"),
    4: (2, "x"),
    5: (3, "x"),
    6: (3, "up"),
    7: (6, "x"),
}
Y_FIRST_DOWN = {**Y_FIRST, 6: (2, "down")}
PARTS = (
    ((0, 1), (0, 288), X_FIRST),
    ((1, 1), (0, 288), X_FIRST),
    ((2, 1), (0, 288), X_FIRST),
    ((3, 1), (0, 288), Y_FIRST),
    ((4, 1), (0, 192), Y_FIRST_DOWN),
    ((4, 1), (192, 96), X_FIRST),
)
KEPT = tuple(
    jax.ShapeDtypeStruct(shape, kind)
    for shape, kind in (
        ((PEERS, REP * TOK, HEAD), BF),
        ((GROUP, HEAD), BF),
        ((GROUP, HEAD), BF),
        ((PEERS, REP * TOK, 128), F32),
        ((PEERS, TOK, QS), BF),
        ((TOK, DIM), F32),
        ((TOK, DIM), BF),
        ((EXPERTS, TOK), F32),
        ((GROUP, 128), F32),
        ((GROUP, 128), F32),
        ((GROUP, 128), jnp.int32),
    )
)
FIRST_STEPS = ("ss", "so", "sl", "a", "g", "ls", "lo", "P0", "P1", "A0", "A1", "A2", "C2", "gt", "tb")
FIRST_STEPS = FIRST_STEPS + tuple("tr%d" % i for i in range(4))
FIRST_LINES = ("t", "c", "r", "s", "o") + tuple("p%d." % i for i in range(len(PARTS)))
FIRST_STEPS = FIRST_STEPS + tuple(n + str(k) for n in FIRST_LINES for k in range(16))
FIRST_ORDER = (
    1, -1, 2, 6, 76, 69, 70, 71, -2, 135, 166, 20, 108, 188, 38, 156, 124, 15, 3, -69, 77, -71, 79,
    172, 21, -70, 78, 140, 7, 102, 92, -166, 174, 74, 73, -135, 143, 101, 22, 119, 16, -74, 82, 37,
    150, 17, -73, 81, -102, 110, 149, 103, 72, -101, 109, 18, -20, 24, -119, 127, 170, -150, 158,
    23, 19, -72, 80, 152, 105, 134, -149, 157, -103, 111, -170, 178, -21, 25, 85, -24, 26, 183, 75,
    -152, 160, -105, 113, 87, 118, -134, 142, -183, 191, -75, 83, 181, -37, 41, -85, 93, 36, 89,
    88, -22, -23, -25, -26, -76, -77, -78, -79, -80, -81, -82, -83, 8, -87, 90, 95, -118, 126,
    -181, 184, 133, 189, 9, 185, 86, 10, -184, 187, -36, 40, -89, 97, 138, 39, 192, -88, 96, 91,
    117, 11, -185, 193, -86, 94, -133, 141, 137, -187, 195, 136, 168, -90, 98, 12, 4, -138, 146,
    -117, 125, -40, 42, -91, 99, -168, 176, 165, 151, 122, 120, 171, 104, -4, -92, -93, -94, -95,
    -96, -97, -98, -99, 13, -151, 159, -165, 173, 53, 54, 52, -136, 144, -137, 145, 14, 5, -171,
    179, -120, 128, 154, -122, 130, 139, -104, 112, 153, -53, 57, 106, -52, 56, -154, 162, 107,
    -139, 147, 155, 167, -153, 161, 55, -106, 114, 123, -56, 58, -107, 115, 121, -167, 175, 169,
    -155, 163, 182, -123, 131, 186, -169, 177, -121, 129, -182, 190, -186, 194, -108, -188, -156,
    -124, -172, -140, -174, -143, -38, -3, -110, -109, -127, -158, -157, -111, -178, -160, -113,
    -142, -191, -126, -189, -41, -192, -193, -141, -195, -39, -146, -125, -176, -42, -159, -173,
    -144, -145, -179, -128, -130, -54, -112, -5, -162, -147, -161, -57, -114, -115, -175, -163,
    -55, -131, -58, -177, -129, -190, -194,
)


def first_kernel(*refs):
    w_dense, (output, tokens, cot, ids, lengths, w_gate, w_up, w_down) = refs[:4], refs[4:12]
    (
        pieces_out,
        cot_all,
        slots_all,
        rows_all,
        gates_all,
        tokens_out,
        normed_out,
        small_out,
        output_out,
    ) = refs[12:21]
    kept_out = refs[21:32]
    kept_refs = refs[32:43]
    (
        query_ref,
        key_ref,
        value_ref,
        log_ref,
        attended_ref,
        middle_ref,
        normed_two_ref,
        gates_ref,
        cos_ref,
        sin_ref,
        start_ref,
    ) = kept_refs
    w_query, w_key, w_value, tail = refs[43:47]
    (
        piece,
        ids_ref,
        member_ref,
        slot_send,
        slices,
        small_in,
        output_in,
        small_rows,
        output_rows,
        small,
        dense,
        tokens_in,
        normed,
        att_send,
        gate_send,
        s_small,
        s_dense,
        s_piece,
        r_small,
        r_dense,
        r_piece,
        s_gather,
        r_gather,
        s_direct,
        r_direct,
        l_sem,
    ) = refs[47:]
    x, y, core = dp_place()
    me = lax.axis_index("expert")
    mine = dp_index(x, y, core)
    loads = [
        pltpu.make_async_copy(src, dst, l_sem.at[20 + i])
        for i, (src, dst) in enumerate(
            zip(w_dense + (ids,), (w_query, w_key, w_value, tail, ids_ref))
        )
    ]
    own = [
        pltpu.make_async_copy(w_gate, piece.at[:, pl.ds(0, ROWS)], l_sem.at[15]),
        pltpu.make_async_copy(w_up, piece.at[:, pl.ds(ROWS, ROWS)], l_sem.at[16]),
    ] + [
        pltpu.make_async_copy(
            w_down.at[:, :, pl.ds(k * FFE, FFE)],
            piece.at[:, pl.ds(2 * ROWS + 32 * k, 32)],
            l_sem.at[17 + k],
        )
        for k in range(3)
    ]
    for c in loads + own:
        c.start()
    _, peers = expert_peers()
    signal_all(
        peers,
        [
            dp_index(x + 1, y, core),
            dp_index(x, y + 1, core),
            dp_index(x, y + 3, core),
            dp_index(x, y, core + 1),
        ],
    )
    for c in loads + own:
        c.wait()
    for j in range(PEERS):
        slices[j] = jnp.concatenate(
            [
                w_query[:, QS * j : QS * (j + 1)],
                w_key[:, HEAD * j : HEAD * (j + 1)],
                w_value[:, HEAD * j : HEAD * (j + 1)],
                tail[...],
            ],
            axis=1,
        )

    def direct(i, src, out, mode):
        part = expert_copies(
            [src], [out], [mode], s_direct.at[pl.ds(i, 1)], r_direct.at[pl.ds(i, 1)]
        ) + own_copies([src], [out], [mode], l_sem.at[pl.ds(i, 1)])

        def start():
            for c in part:
                c.start()

        def wait():
            for c in part:
                c.wait()

        return start, wait

    saved = []

    def save(src, dst, i):
        c = pltpu.make_async_copy(src, dst, l_sem.at[i])
        c.start()
        saved.append(c)

    issue, arrive = {}, {}
    for i, (name, src, out, mode) in enumerate(
        (
            ("ss", slices, small_in, "exchange"),
            ("so", output, output_in, "gather"),
            ("sl", slot_send, slots_all, "exchange"),
            ("a", att_send, attended_ref, "exchange"),
            ("g", gate_send, gates_all, "exchange"),
        )
    ):
        issue[name], arrive[name] = direct(i, src, out, mode)
    lines = {}
    for i, (name, src, out) in enumerate(
        (("t", tokens, tokens_in), ("c", cot, cot_all), ("r", normed_two_ref, rows_all))
    ):
        lines[name] = Gather(src, out, s_gather.at[i], r_gather.at[i], l_sem.at[5 + i])
    for i, (name, src, out) in enumerate((("s", small_rows, small), ("o", output_rows, dense))):
        lines[name] = Line(src, lambda k, out=out: out.at[k], X_FIRST, s_dense.at[i], r_dense.at[i])
    for i, ((expert, count), (row, rows), moves) in enumerate(PARTS):
        def view(k, span=pl.ds(expert, count), part=pl.ds(row, rows)):
            return pieces_out.at[k, span, part]

        own_part = piece.at[pl.ds(expert, count), pl.ds(row, rows)]
        lines["p%d." % i] = Line(own_part, view, moves, s_piece.at[i], r_piece.at[i])
    for name, line in lines.items():
        for k in range(16):
            issue[name + str(k)] = functools.partial(line.issue, k)
            arrive[name + str(k)] = functools.partial(line.arrive, k)

    kept = {}

    def lay_out(name, landed, rows, out, i):
        rows[...] = jnp.concatenate([landed[j] for j in range(PEERS)], axis=0)
        kept[name] = pltpu.make_async_copy(rows, out.at[mine], l_sem.at[8 + i])
        kept[name].start()

    def tables():
        named = jnp.zeros((TOK, 128), F32)
        experts = lax.broadcasted_iota(jnp.int32, (TOK, 128), 1)
        for k in range(ids_ref.shape[1]):
            named = named + (ids_ref[:, k : k + 1] == experts).astype(F32)
        before = (lax.broadcasted_iota(jnp.int32, (TOK, 128), 0) > experts).astype(F32)
        places = dot(before.astype(BF), named.astype(BF), ((1,), (0,)))
        member_ref[...] = jnp.transpose(jnp.where(named > 0.0, places, -1.0))[:EXPERTS]
        slot_send[...] = jnp.full_like(slot_send, -1.0)
        for j in range(PEERS):
            slot_send[j, 0:LOCAL, :] = member_ref[LOCAL * j : LOCAL * (j + 1), :]

    def turns(first, last):
        second = lengths[0, 0]
        third = second + lengths[0, 1]
        fourth = third + lengths[0, 2]

        def block(i, _):
            span = pl.ds(pl.multiple_of(i * TOK, TOK), TOK)
            place = lax.broadcasted_iota(jnp.int32, (TOK, 128), 0) + i * TOK
            begins = jnp.where(
                place >= fourth,
                fourth,
                jnp.where(place >= third, third, jnp.where(place >= second, second, 0)),
            )
            start_ref[span, :] = begins
            lane = lax.broadcasted_iota(jnp.int32, (TOK, 128), 1)
            step = (lane % (HEAD // 2)).astype(F32) * (2.0 / HEAD)
            angle = (place - begins).astype(F32) * jnp.exp(-step * math.log(rope_base))
            cos_ref[span, :] = jnp.cos(angle)
            sin_ref[span, :] = jnp.where(lane % HEAD < HEAD // 2, -1.0, 1.0) * jnp.sin(angle)
            return _

        lax.fori_loop(first, last, block, 0)

    issue["ls"] = functools.partial(lay_out, "s", small_in, small_rows, small, 0)
    issue["lo"] = functools.partial(lay_out, "o", output_in, output_rows, dense, 1)

    def project(i, _):
        values = tokens_in[pl.ds(2 * i, 2)].reshape(2 * TOK, DIM).astype(F32)
        scale = lax.rsqrt(jnp.mean(values * values, axis=-1, keepdims=True) + epsilon)
        low = (values * scale * kept["gains"][0:1]).astype(BF)
        normed[pl.ds(2 * i, 2)] = low.reshape(2, TOK, DIM)
        qkv = dot(low, small[...].reshape(DIM, SLICE), ((1,), (0,)))
        span = pl.ds(pl.multiple_of(i * 2 * TOK, 2 * TOK), 2 * TOK)
        cosine, sine = cos_ref[span, :], sin_ref[span, :]
        lane = lax.broadcasted_iota(jnp.int32, (2 * TOK, 128), 1)
        turned = []
        for h in range(2):
            v = qkv[:, 128 * h : 128 * h + 128]
            other = jnp.where(lane % HEAD < HEAD // 2, pltpu.roll(v, 96, 1), pltpu.roll(v, 32, 1))
            turned.append((v * cosine + other * sine).astype(BF))
        heads = (turned[0][:, :HEAD], turned[0][:, HEAD:], turned[1][:, :HEAD])
        for b in range(2):
            for h in range(REP):
                query_ref[2 * i + b, h * TOK : (h + 1) * TOK, :] = heads[h][
                    b * TOK : (b + 1) * TOK
                ]
        key_ref[span, :] = turned[1][:, HEAD:]
        value_ref[span, :] = qkv[:, QS + HEAD : ROUTER].astype(BF)
        return _

    def project_first():
        lines["t"].own.wait()
        kept["s"].wait()
        pick = (
            lax.broadcasted_iota(jnp.int32, (8, SLICE), 1)
            == lax.broadcasted_iota(jnp.int32, (8, SLICE), 0) + GAINS
        )
        kept["gains"] = dot(
            pick.astype(F32).astype(BF), small[...].reshape(DIM, SLICE), ((1,), (1,))
        )
        lax.fori_loop(0, 2, project, 0)

    def project_rest():
        lax.fori_loop(2, 4, project, 0)
        save(tokens_in, tokens_out, 10)
        save(normed, normed_out, 11)
        save(small, small_out, 12)

    def attend(width, i, _):
        scores = dot(query_ref[i], key_ref[0:width, :], ((1,), (1,))) * HEAD ** (-0.5)
        keys = lax.broadcasted_iota(jnp.int32, (TOK, width), 1)
        rows = lax.broadcasted_iota(jnp.int32, (TOK, width), 0) + i * TOK
        begins = start_ref[pl.ds(pl.multiple_of(i * TOK, TOK), TOK), :][:, :1]
        allowed = (keys <= rows) & (keys >= begins)
        scores = jnp.where(allowed[None], scores.reshape(REP, TOK, width), masked_score)
        top = jnp.max(scores, axis=-1, keepdims=True)
        terms = jnp.exp(scores - top)
        total = jnp.sum(terms, axis=-1, keepdims=True)
        probs = (terms / total).astype(BF).reshape(REP * TOK, width)
        out = dot(probs, value_ref[0:width, :], ((1,), (0,))).astype(BF)
        att_send[i] = jnp.concatenate([out[h * TOK : (h + 1) * TOK] for h in range(REP)], axis=1)
        log_ref[i] = jnp.broadcast_to(
            (top + jnp.log(total)).reshape(REP * TOK, 1), (REP * TOK, 128)
        )
        return _

    issue["P0"], issue["P1"] = project_first, project_rest
    for name, first, last, width in (("A0", 0, 4, 512), ("A1", 4, 6, 1024), ("A2", 6, 8, 1024)):
        issue[name] = functools.partial(
            lax.fori_loop, first, last, functools.partial(attend, width), 0
        )

    def out_project():
        kept["o"].wait()
        save(dense, output_out, 13)
        middle = tokens_in[me].astype(F32)
        for j in range(PEERS):
            middle = middle + dot(
                attended_ref[j], dense[2 * j : 2 * j + 2].reshape(QS, DIM), ((1,), (0,))
            )
        middle_ref[...] = middle
        scale_two = lax.rsqrt(jnp.mean(middle * middle, axis=-1, keepdims=True) + epsilon)
        normed_two_ref[...] = (middle * scale_two * kept["gains"][1:2]).astype(BF)
        lines["r"].begin()

    def choose():
        router = small[:, :, 256:SLICE].reshape(DIM, SLICE - 256)
        logits = dot(router, normed_two_ref[...], ((0,), (1,)))[ROUTER - 256 : GAINS - 256]
        member = member_ref[...] >= 0.0
        chosen = jnp.where(member, logits, masked_score)
        weight = jnp.where(member, jnp.exp(chosen - jnp.max(chosen, axis=0, keepdims=True)), 0.0)
        gates_ref[...] = weight / jnp.sum(weight, axis=0, keepdims=True)
        gate_send[...] = jnp.zeros_like(gate_send)
        for j in range(PEERS):
            gate_send[j, 0:LOCAL, :] = gates_ref[LOCAL * j : LOCAL * (j + 1), :]

    issue["C2"], issue["gt"] = out_project, choose
    save(piece, pieces_out.at[mine], 14)
    lines["t"].begin()
    lines["c"].begin()
    issue["tb"] = tables
    for i in range(4):
        issue["tr%d" % i] = functools.partial(turns, 2 * i, 2 * i + 2)
    for step in FIRST_ORDER:
        (issue if step > 0 else arrive)[FIRST_STEPS[abs(step) - 1]]()
    lines["c"].own.wait()
    lines["r"].own.wait()
    for line in lines.values():
        for c in line.started:
            c.wait_send()
    for i, (src, dst) in enumerate(zip(kept_refs, kept_out)):
        save(src, dst, 25 + i)
    for c in saved:
        c.wait()


def first_phase(*args):
    hbm, smem = pl.BlockSpec(memory_space=pltpu.HBM), pl.BlockSpec(memory_space=pltpu.SMEM)
    shape = jax.ShapeDtypeStruct
    blocks = (PEERS, TOK, DIM)
    outs = [
        (shape((DP, LOCAL, 3 * ROWS, FFE), BF), hbm),
        (shape(blocks, BF), hbm),
        (shape((PEERS, 8, TOK), F32), hbm),
        (shape(blocks, BF), hbm),
        (shape((PEERS, 8, TOK), F32), hbm),
        (shape(blocks, BF), hbm),
        (shape(blocks, BF), hbm),
        (shape((DP, ROWS, SLICE), BF), hbm),
        (shape((DP, ROWS, DIM), BF), hbm),
    ] + [(k, hbm) for k in KEPT]
    dma = pltpu.SemaphoreType.DMA
    return pl.pallas_call(
        first_kernel,
        out_shape=[o[0] for o in outs],
        in_specs=[hbm] * 8 + [smem] + [hbm] * 3,
        out_specs=[o[1] for o in outs],
        scratch_shapes=[pltpu.VMEM(k.shape, k.dtype) for k in KEPT]
        + [pltpu.VMEM(a.shape, a.dtype) for a in args[:4]]
        + [
            pltpu.VMEM((LOCAL, 3 * ROWS, FFE), BF),
            pltpu.VMEM((TOK, 8), jnp.int32),
            pltpu.VMEM((EXPERTS, TOK), F32),
            pltpu.VMEM((PEERS, 8, TOK), F32),
            pltpu.VMEM((PEERS, 12, SLICE), BF),
            pltpu.VMEM((PEERS, 12, SLICE), BF),
            pltpu.VMEM((PEERS, 12, DIM), BF),
            pltpu.VMEM((ROWS, SLICE), BF),
            pltpu.VMEM((ROWS, DIM), BF),
            pltpu.VMEM((DP, ROWS, SLICE), BF),
            pltpu.VMEM((DP, ROWS, DIM), BF),
            pltpu.VMEM(blocks, BF),
            pltpu.VMEM(blocks, BF),
            pltpu.VMEM((PEERS, TOK, QS), BF),
            pltpu.VMEM((PEERS, 8, TOK), F32),
            dma((1,)),
            dma((2, 16)),
            dma((len(PARTS), 16)),
            dma((1,)),
            dma((2, 16)),
            dma((len(PARTS), 16)),
            dma((3, 7)),
            dma((3, 7)),
            dma((5, 7)),
            dma((5, 7)),
            dma((40,)),
        ],
        compiler_params=pltpu.CompilerParams(
            collective_id=1, has_side_effects=True, vmem_limit_bytes=63 << 20
        ),
        cost_estimate=lasting(120),
    )(*args)


def dot(a, b, contract):
    return lax.dot_general(a, b, ((contract[0], contract[1]), ((), ())), preferred_element_type=F32)


class Reduce:
    def __init__(self, src, own, landed, send, recv):
        self.src, self.own, self.landed = src, own, landed
        self.send, self.recv = send, recv
        me = lax.axis_index("expert")
        z, x = me // 2, me % 2
        self.place = lambda dz, dx: (z + dz) % 4 * 2 + (x + dx) % 2
        up, down, across = self.place(1, 0), self.place(3, 0), self.place(0, 1)
        self.moves = {
            0: ((2, 1), up),
            1: ((2, 0), down),
            2: (0, up),
            3: ((3, 1), down),
            4: ((1, 0), up),
            5: (1, down),
            6: (2, across),
        }
        self.started = []

    def issue(self, k):
        source, target = self.moves[k]
        relayed = isinstance(source, int)
        c = pltpu.make_async_remote_copy(
            src_ref=self.landed.at[source] if relayed else self.src.at[self.place(*source)],
            dst_ref=self.landed.at[k],
            send_sem=self.send.at[k],
            recv_sem=self.recv.at[k],
            device_id={"expert": target},
            device_id_type=MESH,
        )
        c.start()
        self.started.append(c)

    def arrive(self, k):
        pltpu.make_async_remote_copy(
            src_ref=self.landed.at[k],
            dst_ref=self.landed.at[k],
            send_sem=self.send.at[k],
            recv_sem=self.recv.at[k],
            device_id={"expert": self.moves[6][1]},
            device_id_type=MESH,
        ).wait_recv()

    def sum(self, block, *landed):
        total = self.own(*block)
        for k in landed:
            total = total + self.landed[k].astype(F32)
        return total

    def add(self, k):
        block, landed = (((1, 1), (0,)), ((3, 0), (1,)), ((0, 1), (2, 3)))[k]
        self.landed[k] = self.sum(block, *landed).astype(BF)

    def total(self):
        return self.sum((0, 0), 4, 5, 6)

    def finish(self):
        for c in self.started:
            c.wait_send()
        self.started = []


RING = {
    6: (0, "up", ()),
    7: (1, "down", ()),
    4: (2, "up", ()),
    5: (3, "down", (1,)),
    2: (4, "up", (0,)),
    3: (5, "down", ()),
    1: (6, "x", (2, 3)),
    0: (None, None, (4, 5, 6)),
}
ACROSS = {
    7: (3, "x", ()),
    4: (1, "x", ()),
    5: (2, "x", ()),
    1: (0, "x", ()),
    6: (4, "up", (3,)),
    2: (6, "up", (1, 4)),
    3: (7, "down", (2,)),
    0: (None, None, (0, 6, 7)),
}
ACROSS_DOWN = {**ACROSS, 6: (4, "down", (3,)), 2: (6, "up", (1,)), 3: (7, "down", (2, 4))}
WAYS = (RING, RING, RING, ACROSS, ACROSS_DOWN, RING)


def dp_targets():
    x, y, core = dp_place()
    return {
        "x": dp_index(x + 1, y, core),
        "up": dp_index(x, y + 1, core),
        "down": dp_index(x, y + 3, core),
        "core": dp_index(x, y, core + 1),
    }


class DenseSum:
    def __init__(self, grads, theirs, landed, send, recv):
        self.grads, self.theirs, self.landed, self.send, self.recv = grads, theirs, landed, send, recv
        self.targets = dp_targets()
        x, y, core = dp_place()
        self.slots = [dp_index(x + rx, y + ry, core) for rx, ry in SLOTS]
        self.others = [dp_index(x + rx, y + ry, core + 1) for rx, ry in SLOTS]
        self.carried = {j: (k, where) for k, (j, where, _) in RING.items()}
        self.started = []

    def descriptor(self, k, src, dst, where):
        return pltpu.make_async_remote_copy(
            src_ref=src,
            dst_ref=dst,
            send_sem=self.send.at[k],
            recv_sem=self.recv.at[k],
            device_id={"dp": self.targets[where]},
            device_id_type=MESH,
        )

    def issue(self, k):
        if k >= 8:
            src, dst, where = self.grads.at[self.others[k - 8]], self.theirs.at[k - 8], "core"
        else:
            slot, where = self.carried[k]
            src, dst = self.grads.at[self.slots[slot]], self.landed.at[k]
        c = self.descriptor(k, src, dst, where)
        c.start()
        self.started.append(c)

    def arrive(self, k):
        ref = self.theirs.at[k - 8] if k >= 8 else self.landed.at[k]
        self.descriptor(k, ref, ref, "x").wait_recv()

    def sum(self, k):
        total = self.grads[self.slots[k]].astype(F32) + self.theirs[k].astype(F32)
        for j in RING[k][2]:
            total = total + self.landed[j].astype(F32)
        return total

    def add(self, k):
        self.grads[self.slots[k]] = self.sum(k).astype(BF)

    def finish(self):
        for c in self.started:
            c.wait_send()


class Stage:
    def __init__(self, buffers, sems):
        self.buffers, self.sems = buffers, sems
        self.free = list(range(buffers.shape[0]))
        self.held = {}

    def fetch(self, name, src, rows):
        i = self.free.pop(0)
        ref = self.buffers.at[i, pl.ds(0, rows)]
        c = pltpu.make_async_copy(src, ref, self.sems.at[i])
        c.start()
        self.held[name] = (i, ref, c)

    def wait(self, name):
        self.held[name][2].wait()

    def take(self, name):
        i, ref, _ = self.held.pop(name)
        self.free.append(i)
        return ref


class ExpertSum:
    def __init__(self, own, given, landed, out, ends, way, stage, send, recv, store):
        self.own, self.given, self.landed, self.out, self.ends = own, given, landed, out, ends
        self.way, self.stage, self.send, self.recv, self.store = way, stage, send, recv, store
        self.rows = own(0).shape[0]
        self.targets = dp_targets()
        self.carried = {j: (k, where) for k, (j, where, _) in way.items()}
        self.started = []

    def descriptor(self, j, src, where):
        return pltpu.make_async_remote_copy(
            src_ref=src,
            dst_ref=self.landed(j),
            send_sem=self.send.at[j],
            recv_sem=self.recv.at[j],
            device_id={"dp": self.targets[where]},
            device_id_type=MESH,
        )

    def issue(self, j):
        k, where = self.carried[j]
        c = self.descriptor(j, self.own(k), where)
        c.start()
        self.started.append(c)

    def arrive(self, j):
        self.descriptor(j, self.landed(j), "x").wait_recv()

    def fetch_given(self, k):
        self.stage.fetch((id(self), "l", k), self.given(k), self.rows)

    def fetch_landed(self, j):
        self.stage.fetch((id(self), "h", j), self.landed(j), self.rows)

    def wait_given(self, k):
        self.stage.wait((id(self), "l", k))

    def wait_landed(self, j):
        self.stage.wait((id(self), "h", j))

    def accumulate(self, k, names, out):
        refs = [self.stage.take((id(self),) + n) for n in names]

        def body(i, _):
            span = pl.ds(pl.multiple_of(i * 32, 32), 32)
            total = self.own(k)[span, :].astype(F32)
            for r in refs:
                total = total + r[span, :].astype(F32)
            out[span, :] = total.astype(out.dtype)
            return _

        lax.fori_loop(0, self.rows // 32, body, 0)

    def add_given(self, k):
        self.accumulate(k, [("l", k)], self.own(k))

    def add_landed(self, k):
        out = self.own(k) if k > 0 else self.ends
        self.accumulate(k, [("h", j) for j in self.way[k][2]], out)

    def write(self):
        self.save = pltpu.make_async_copy(self.ends, self.out, self.store)
        self.save.start()

    def finish(self):
        for c in self.started:
            c.wait_send()


LAST_STEPS = ("in", "e", "qo", "qs", "C4", "GO", "A0", "A1", "A2", "P0", "P1", "GS", "MX", "GT", "CO")
LAST_STEPS = LAST_STEPS + ("CS", "FI", "lz", "lw", "ly")
LAST_STEPS = LAST_STEPS + tuple(f + k for f in "zyg" for k in "0123456ABC")
for family in "os":
    LAST_STEPS = LAST_STEPS + tuple(family + str(k) for k in range(16))
    LAST_STEPS = LAST_STEPS + tuple(family + "a%d" % k for k in range(8)) + (family + "t",)
for part in range(len(PARTS)):
    LAST_STEPS = LAST_STEPS + tuple("u%d." % part + f + str(k) for f in ("", "l", "S", "R", "h") for k in range(8))
    LAST_STEPS = LAST_STEPS + ("u%d.w" % part,)
LAST_ORDER = (
    197, 277, 157, 21, 18, 22, 1, 19, -197, 205, 279, 183, -277, 285, 111, 266, -157, 165, 239,
    143, -279, 287, 156, -111, 119, 315, -239, 247, 321, -156, 164, 198, 35, 142, 24, 227, -183,
    -266, -22, -18, 29, -315, 323, 114, -321, 329, 110, 307, -198, 206, 236, -114, 122, 317, -21,
    28, -143, 184, -110, 118, 154, -236, 244, 192, -317, 325, 280, -154, 162, 193, 144, -192, 200,
    215, -280, 288, 273, -193, 201, 237, 225, -215, 209, 232, -273, 281, 155, -237, 245, 175, -307,
    -232, 240, 115, 23, 26, -155, 163, 194, -142, -175, 171, 195, -115, 123, 316, -194, 202, 152,
    -227, -195, 203, 314, -316, 324, 278, -152, 160, 319, -314, 322, 339, -278, 286, 174, -319,
    327, 234, -339, 335, 318, -174, 168, 320, -234, 242, 113, -318, 326, 112, -320, 328, 275, -113,
    121, 298, -112, 120, 153, -275, 283, 196, -298, 291, 151, -153, 161, 274, -196, 204, 233, -151,
    159, 150, -274, 282, 276, 309, -233, 241, 191, -150, 158, 116, 306, -276, 284, 109, -191, 199,
    235, -116, 124, 238, -109, 117, 259, 224, -235, 243, -238, 246, -259, 254, -184, 216, 145,
    -144, 176, 228, -225, -216, 212, 257, -309, 25, 34, -306, 338, -338, 332, -23, -24, 30, 27,
    186, 103, -224, -145, 177, -228, 260, -176, -177, 167, 31, -257, -260, 250, 32, 106, 308, 267,
    -186, 218, -103, 135, 185, 146, 265, 102, 268, -25, -26, -27, -1, -19, 5, -267, -106, 20, 2,
    -185, 217, 147, -308, 6, -265, 63, 61, 62, 230, -102, 134, 148, -31, -20, 38, 33, 64, -268,
    -217, -218, 208, 59, -63, 71, 65, -146, -134, 130, 300, 53, 189, 104, 66, 60, -2, 7, -147, -66,
    74, 52, 101, -230, 8, -104, 136, 226, -148, 188, 9, -189, -135, -136, 126, 178, 179, 180, 107,
    187, 10, -101, 133, 311, -226, 11, 41, 44, -188, -133, 127, 340, 341, 105, -300, 295, 138, 269,
    -178, -179, -180, 166, 299, 182, -64, -52, 72, -311, -65, 73, -187, -33, -34, 40, 54, -107,
    139, 51, 37, 45, 42, 12, 86, 91, 89, 87, -105, 137, 84, -269, 301, 90, 85, 88, -340, -341, 331,
    219, 220, 221, -32, 39, -91, 99, 77, -87, 95, -137, -138, -139, 125, 258, 141, -88, 96, 312,
    81, -41, 48, 78, -60, -53, -54, 68, -90, 98, 76, 57, -89, -77, 97, 79, -62, 70, 271, 43, 56,
    36, -61, -51, 69, -312, -299, -301, 292, 297, -219, -220, -221, 207, 343, 344, 223, -258, 251,
    256, 262, -85, -78, -79, 93, -42, 49, -86, -76, 94, 80, 82, 55, 272, -271, 303, 46, -84, -80,
    -81, -82, 100, 16, 4, 231, -43, -44, 50, 47, 310, -35, -36, -37, 13, -272, 304, -59, -55, -56,
    -57, 75, 15, 3, -310, 342, -297, -303, -304, 289, 305, -342, -343, -344, 330, -231, 263, 346,
    -256, -262, -263, 248, 264, -45, -46, -47, 14, -3, -4, 17, -182, -141, -223, -305, -346, -264,
)


def last_kernel(*refs):
    (
        back_part,
        inner_part,
        out_part,
        keep,
        given,
        tokens_all,
        normed_all,
        small_hbm,
        dense_hbm,
        tokens_hbm,
        cot_hbm,
    ) = refs[:11]
    kept_in = refs[11:22]
    mixed_out, grad_tokens_out, expert_ref, small_own, output_out, landed = refs[22:28]
    kept_refs = refs[28:39]
    (
        query_ref,
        key_ref,
        value_ref,
        log_ref,
        attended_ref,
        middle_ref,
        normed_two_ref,
        gates_ref,
        cos_ref,
        sin_ref,
        start_ref,
    ) = kept_refs
    (
        tokens,
        cot,
        mixed_ref,
        grad_tokens_ref,
        output_own,
        inner_in,
        gates_grad,
        logits_grad,
        small,
        dense,
        grad_small,
        normed,
        token_rows,
        grad_normed,
        att_send,
        att_in,
        grad_query,
        grad_key,
        grad_value,
        grad_qkv,
        gain_sum,
        grad_middle_ref,
        z_own,
        z_landed,
        y_landed,
        stage,
        terms,
        ends,
        small_theirs,
        small_landed,
        dense_theirs,
        dense_landed,
        small_cut,
        dense_cut,
        dense_in,
        s_direct,
        r_direct,
        s_reduce,
        r_reduce,
        s_dense,
        r_dense,
        s_part,
        r_part,
        l_sem,
        l_stage,
    ) = refs[39:]
    _, peers = expert_peers()
    x, y, core = dp_place()
    me = lax.axis_index("expert")
    signal_all(
        peers,
        [
            dp_index(x + 1, y, core),
            dp_index(x, y + 1, core),
            dp_index(x, y + 3, core),
            dp_index(x, y, core + 1),
        ],
    )

    def direct(i, src, out, mode):
        part = expert_copies(
            [src], [out], [mode], s_direct.at[pl.ds(i, 1)], r_direct.at[pl.ds(i, 1)]
        ) + own_copies([src], [out], [mode], l_sem.at[pl.ds(i, 1)])

        def start():
            for c in part:
                c.start()

        def wait():
            for c in part:
                c.wait()

        return start, wait

    def load(src, dst, i):
        c = pltpu.make_async_copy(src, dst, l_sem.at[i])
        c.start()
        return c

    def settle(part):
        for c in part:
            c.wait()

    OWN = ((1, 1), (3, 0), (0, 1), (0, 0))

    def from_own(dz, dx):
        return z_own[OWN.index((dz, dx))].astype(F32)

    def from_grad(dz, dx):
        return grad_normed[sums["g"].place(dz, dx)].astype(F32)

    sums = {
        "z": Reduce(back_part, from_own, z_landed, s_reduce.at[0], r_reduce.at[0]),
        "y": Reduce(out_part, from_own, y_landed, s_reduce.at[1], r_reduce.at[1]),
        "g": Reduce(grad_normed, from_grad, z_landed, s_reduce.at[2], r_reduce.at[2]),
        "o": DenseSum(dense, dense_theirs, dense_landed, s_dense.at[0], r_dense.at[0]),
        "s": DenseSum(grad_small, small_theirs, small_landed, s_dense.at[1], r_dense.at[1]),
    }
    fetched = Stage(stage, l_stage)
    for i, ((expert, _), (row, rows), _) in enumerate(PARTS):
        span = pl.ds(row, rows)
        sums["u%d." % i] = ExpertSum(
            lambda k, e=expert, r=span: terms.at[e, k, r],
            lambda k, e=expert, r=span: given.at[k, e, r],
            lambda j, e=expert, r=span: landed.at[j, e, r],
            expert_ref.at[expert, span],
            ends.at[expert, span],
            WAYS[i],
            fetched,
            s_part.at[i],
            r_part.at[i],
            l_sem.at[32 + i],
        )
    issue, arrive, done = {}, {}, {}
    for i, (name, src, out) in enumerate(
        (
            ("in", inner_part, inner_in),
            ("e", att_send, att_in),
            ("qo", dense_cut, dense_in),
            ("qs", small_cut, small_own),
        )
    ):
        issue[name], arrive[name] = direct(i, src, out, "exchange")
    for name, part in sums.items():
        for k in range(16):
            issue[name + str(k)] = functools.partial(part.issue, k)
            arrive[name + str(k)] = functools.partial(part.arrive, k)
        for k in range(8):
            if name in "zyg":
                issue[name + "ABCDEFGH"[k]] = functools.partial(part.add, k)
            elif name in "os":
                issue[name + "a%d" % k] = functools.partial(part.add, k)
            else:
                issue[name + "l%d" % k] = functools.partial(part.fetch_given, k)
                arrive[name + "l%d" % k] = functools.partial(part.wait_given, k)
                issue[name + "h%d" % k] = functools.partial(part.fetch_landed, k)
                arrive[name + "h%d" % k] = functools.partial(part.wait_landed, k)
                issue[name + "S%d" % k] = functools.partial(part.add_given, k)
                issue[name + "R%d" % k] = functools.partial(part.add_landed, k)

    def own_blocks(name, src, base):
        def start():
            done[name] = [
                load(src.at[sums["z"].place(*d)], z_own.at[i], base + i) for i, d in enumerate(OWN)
            ]

        return start, lambda: settle(done[name])

    issue["lz"], arrive["lz"] = own_blocks("lz", back_part, 8)
    issue["ly"], arrive["ly"] = own_blocks("ly", out_part, 8)

    def load_kept():
        done["lw"] = [load(a, b, 16 + i) for i, (a, b) in enumerate(zip(kept_in, kept_refs))] + [
            load(tokens_hbm, tokens, 27),
            load(cot_hbm, cot, 28),
            load(small_hbm, small, 4),
            load(dense_hbm, dense, 5),
            load(normed_all, normed, 6),
        ]

    issue["lw"], arrive["lw"] = load_kept, lambda: settle(done["lw"])

    def back_to_middle():
        for j in range(PEERS):
            gates_grad[LOCAL * j : LOCAL * (j + 1), :] = inner_in[j, 0:LOCAL, :]
        gates = gates_ref[...]
        grad_gates = gates_grad[...]
        logits_grad[...] = jnp.zeros_like(logits_grad)
        logits_grad[ROUTER - 256 : GAINS - 256, :] = gates * (
            grad_gates - jnp.sum(gates * grad_gates, axis=0, keepdims=True)
        )
        pick = (
            lax.broadcasted_iota(jnp.int32, (8, SLICE), 1)
            == lax.broadcasted_iota(jnp.int32, (8, SLICE), 0) + GAINS
        )
        gains = dot(pick.astype(F32).astype(BF), small[...].reshape(DIM, SLICE), ((1,), (1,)))
        done["gain_one"], gain_two = gains[0:1], gains[1:2]
        grad_logits = logits_grad[...].astype(BF)
        done["grad_logits"] = grad_logits
        router = small[:, :, 256:SLICE].reshape(DIM, SLICE - 256)
        grad = sums["z"].total() + dot(grad_logits, router, ((0,), (1,)))
        middle = middle_ref[...]
        scale_two = lax.rsqrt(jnp.mean(middle * middle, axis=-1, keepdims=True) + epsilon)
        gain_sum[0] = jnp.sum((grad * middle * scale_two).reshape(TOK // 8, 8, DIM), axis=0)
        grad_middle = cot[...].astype(F32) + norm_back(middle, scale_two, gain_two, grad)
        grad_middle_ref[...] = grad_middle
        grad_branch = grad_middle.astype(BF)
        done["grad_branch"] = grad_branch
        for j in range(PEERS):
            att_send[j] = dot(
                grad_branch, dense[2 * j : 2 * j + 2].reshape(QS, DIM), ((1,), (1,))
            ).astype(BF)
        sums["z"].finish()

    def output_grads():
        for j in range(PEERS):
            dense[2 * j : 2 * j + 2] = (
                dot(attended_ref[j], done["grad_branch"], ((0,), (0,)))
                .astype(BF)
                .reshape(2, ROWS, DIM)
            )

    def attend(width, i, _):
        queries = query_ref[i]
        incoming = att_in[i]
        incoming = jnp.concatenate(
            [incoming[:, h * HEAD : (h + 1) * HEAD] for h in range(REP)], axis=0
        )
        scores = dot(queries, key_ref[0:width, :], ((1,), (1,))) * HEAD ** (-0.5)
        keys = lax.broadcasted_iota(jnp.int32, (TOK, width), 1)
        rows = lax.broadcasted_iota(jnp.int32, (TOK, width), 0) + i * TOK
        begins = start_ref[pl.ds(pl.multiple_of(i * TOK, TOK), TOK), :][:, :1]
        allowed = (keys <= rows) & (keys >= begins)
        scores = jnp.where(allowed[None], scores.reshape(REP, TOK, width), masked_score)
        probs = jnp.exp(scores.reshape(REP * TOK, width) - log_ref[i][:, :1])
        grad_probs = dot(incoming, value_ref[0:width, :], ((1,), (1,)))
        inner_sum = jnp.sum(probs * grad_probs, axis=-1, keepdims=True)
        grad_scores = (probs * (grad_probs - inner_sum)).astype(BF)
        grad_query[i] = dot(grad_scores, key_ref[0:width, :], ((1,), (0,))) * HEAD ** (-0.5)
        grad_key[0:width, :] += dot(grad_scores, queries, ((0,), (0,))) * HEAD ** (-0.5)
        grad_value[0:width, :] += dot(probs.astype(BF), incoming, ((0,), (0,)))
        return _

    def attend_blocks(first, last, width):
        if first == 0:
            grad_key[...] = jnp.zeros_like(grad_key)
            grad_value[...] = jnp.zeros_like(grad_value)
        lax.fori_loop(first, last, functools.partial(attend, width), 0)

    def project(i, _):
        span = pl.ds(pl.multiple_of(i * 2 * TOK, 2 * TOK), 2 * TOK)
        rows = load(tokens_all.at[pl.ds(2 * i, 2)], token_rows, 7)
        cosine, sine = cos_ref[span, :], sin_ref[span, :]
        lane = lax.broadcasted_iota(jnp.int32, (2 * TOK, 128), 1)
        heads = [
            jnp.concatenate(
                [grad_query[2 * i + b, h * TOK : (h + 1) * TOK, :] for b in range(2)], axis=0
            )
            for h in range(REP)
        ]
        turned = []
        for pair in ((heads[0], heads[1]), (heads[2], grad_key[span, :])):
            v = jnp.concatenate(pair, axis=1)
            other = jnp.where(lane % HEAD < HEAD // 2, pltpu.roll(v, 96, 1), pltpu.roll(v, 32, 1))
            turned.append((v * cosine - other * sine).astype(BF))
        tail = jnp.concatenate(
            [grad_value[span, :], jnp.zeros((2 * TOK, SLICE - ROUTER), F32)], axis=1
        ).astype(BF)
        low = jnp.concatenate(turned + [tail], axis=1)
        grad_qkv[span, :] = low
        grad = dot(low, small[...].reshape(DIM, SLICE), ((1,), (1,)))
        grad_normed[pl.ds(2 * i, 2)] = grad.astype(BF).reshape(2, TOK, DIM)
        rows.wait()
        values = token_rows[...].reshape(2 * TOK, DIM).astype(F32)
        scale = lax.rsqrt(jnp.mean(values * values, axis=-1, keepdims=True) + epsilon)
        gain_sum[1] += jnp.sum((grad * values * scale).reshape(2 * TOK // 8, 8, DIM), axis=0)
        return _

    def project_blocks(first, last):
        if first == 0:
            gain_sum[1] = jnp.zeros((8, DIM), F32)
        lax.fori_loop(first, last, project, 0)

    def small_grads():
        lanes = lax.broadcasted_iota(jnp.int32, (8, 128), 1)
        marks = [(lanes == GAINS - 256 + i).astype(F32).astype(BF) for i in range(2)]
        for c in range(4):
            span = slice(c * 384, (c + 1) * 384)
            part = dot(normed[:, :, span].reshape(GROUP, 384), grad_qkv[...], ((0,), (0,)))
            extra = dot(normed_two_ref[:, span], done["grad_logits"], ((0,), (1,)))
            for i in range(2):
                value = gain_sum[1 - i, :, span]
                high = value.astype(BF)
                rest = (value - high.astype(F32)).astype(BF)
                extra = extra + dot(high, marks[i], ((0,), (0,)))
                extra = extra + dot(rest, marks[i], ((0,), (0,)))
            grad_small[4 * c : 4 * c + 4, :, 0:256] = (
                part[:, 0:256].astype(BF).reshape(4, ROWS, 256)
            )
            grad_small[4 * c : 4 * c + 4, :, 256:SLICE] = (
                (part[:, 256:SLICE] + extra).astype(BF).reshape(4, ROWS, SLICE - 256)
            )

    saves = []

    def mix():
        mixed_ref[...] = (middle_ref[...] + sums["y"].total()).astype(BF)
        saves.append(load(mixed_ref, mixed_out, 29))

    def token_grads():
        values = tokens[...].astype(F32)
        scale = lax.rsqrt(jnp.mean(values * values, axis=-1, keepdims=True) + epsilon)
        grad_tokens_ref[...] = grad_middle_ref[...] + norm_back(
            values, scale, done["gain_one"], sums["g"].total()
        )
        saves.append(load(grad_tokens_ref, grad_tokens_out, 30))

    def total_of(name):
        done[name] = sums[name].sum(0)

    def cut(name, ref):
        for j in range(PEERS):
            ref[j] = done[name][12 * j : 12 * (j + 1)]

    def own_output():
        acc = dense_in[0]
        for j in range(1, PEERS):
            acc = acc + dense_in[j]
        output_own[...] = acc
        saves.append(load(output_own, output_out, 31))

    issue["C4"], issue["GO"], issue["GS"] = back_to_middle, output_grads, small_grads
    issue["A0"] = functools.partial(attend_blocks, 0, 4, GROUP // 2)
    issue["A1"] = functools.partial(attend_blocks, 4, 6, GROUP)
    issue["A2"] = functools.partial(attend_blocks, 6, 8, GROUP)
    issue["P0"] = functools.partial(project_blocks, 0, 2)
    issue["P1"] = functools.partial(project_blocks, 2, 4)
    issue["MX"], issue["GT"], issue["FI"] = mix, token_grads, own_output
    issue["ot"], issue["st"] = functools.partial(total_of, "o"), functools.partial(total_of, "s")
    issue["CO"] = functools.partial(cut, "o", dense_cut)
    issue["CS"] = functools.partial(cut, "s", small_cut)

    mine = [load(keep.at[:, e], terms.at[e], 38 + e) for e in range(LOCAL)]
    held = set()
    for step in LAST_ORDER:
        name = LAST_STEPS[abs(step) - 1]
        if name[0] == "u" and name[3] == "S":
            expert = PARTS[int(name[1])][0][0]
            if expert not in held:
                held.add(expert)
                mine[expert].wait()
        if name[0] == "u" and name[3:] == "w":
            part = sums[name[:3]]
            if step > 0:
                part.write()
            else:
                part.save.wait()
            continue
        (issue if step > 0 else arrive)[name]()
    for part in sums.values():
        part.finish()
    settle(saves)


def last_phase(*args):
    hbm = pl.BlockSpec(memory_space=pltpu.HBM)
    shape, dma = jax.ShapeDtypeStruct, pltpu.SemaphoreType.DMA
    blocks = (PEERS, TOK, DIM)
    piece = (3 * ROWS, FFE)
    outs = [
        (shape((TOK, DIM), BF), hbm),
        (shape((TOK, DIM), F32), hbm),
        (shape((LOCAL,) + piece, F32), hbm),
        (shape((PEERS, 12, SLICE), F32), hbm),
        (shape((12, DIM), F32), hbm),
        (shape((8, LOCAL) + piece, BF), hbm),
    ]
    return pl.pallas_call(
        last_kernel,
        out_shape=[o[0] for o in outs],
        in_specs=[hbm] * 22,
        out_specs=[o[1] for o in outs],
        scratch_shapes=[pltpu.VMEM(k.shape, k.dtype) for k in KEPT]
        + [
            pltpu.VMEM((TOK, DIM), BF),
            pltpu.VMEM((TOK, DIM), BF),
            pltpu.VMEM((TOK, DIM), BF),
            pltpu.VMEM((TOK, DIM), F32),
            pltpu.VMEM((12, DIM), F32),
            pltpu.VMEM((PEERS, 8, TOK), F32),
            pltpu.VMEM((EXPERTS, TOK), F32),
            pltpu.VMEM((SLICE - 256, TOK), F32),
            pltpu.VMEM((DP, ROWS, SLICE), BF),
            pltpu.VMEM((DP, ROWS, DIM), BF),
            pltpu.VMEM((DP, ROWS, SLICE), BF),
            pltpu.VMEM(blocks, BF),
            pltpu.VMEM((2, TOK, DIM), BF),
            pltpu.VMEM(blocks, BF),
            pltpu.VMEM((PEERS, TOK, QS), BF),
            pltpu.VMEM((PEERS, TOK, QS), BF),
            pltpu.VMEM((PEERS, REP * TOK, HEAD), F32),
            pltpu.VMEM((GROUP, HEAD), F32),
            pltpu.VMEM((GROUP, HEAD), F32),
            pltpu.VMEM((GROUP, SLICE), BF),
            pltpu.VMEM((2, 8, DIM), F32),
            pltpu.VMEM((TOK, DIM), F32),
            pltpu.VMEM((4, TOK, DIM), BF),
            pltpu.VMEM((7, TOK, DIM), BF),
            pltpu.VMEM((7, TOK, DIM), BF),
            pltpu.VMEM((8,) + piece, BF),
            pltpu.VMEM((LOCAL, 8) + piece, BF),
            pltpu.VMEM((LOCAL,) + piece, F32),
            pltpu.VMEM((8, ROWS, SLICE), BF),
            pltpu.VMEM((7, ROWS, SLICE), BF),
            pltpu.VMEM((8, ROWS, DIM), BF),
            pltpu.VMEM((7, ROWS, DIM), BF),
            pltpu.VMEM((PEERS, 12, SLICE), F32),
            pltpu.VMEM((PEERS, 12, DIM), F32),
            pltpu.VMEM((PEERS, 12, DIM), F32),
            dma((4, 7)),
            dma((4, 7)),
            dma((3, 7)),
            dma((3, 7)),
            dma((2, 16)),
            dma((2, 16)),
            dma((len(PARTS), 8)),
            dma((len(PARTS), 8)),
            dma((43,)),
            dma((8,)),
        ],
        compiler_params=pltpu.CompilerParams(
            collective_id=3, has_side_effects=True, vmem_limit_bytes=63 << 20
        ),
        cost_estimate=lasting(120),
    )(*args)


def experts_kernel(*refs):
    (rows_ref, cot_ref, slot_ref, gate_ref), refs = refs[:4], refs[4:]
    pieces, refs = refs[0], refs[1:]
    (out_ref, back_ref, inner_ref, keep_ref, given_ref), refs = refs[:5], refs[5:]
    xg, cg, weights, grads, gates, inners, wsem, gsem, rsem = refs
    x, y, core = dp_place()
    other = dp_index(x, y, core + 1)
    signal_all([], [other])

    def load(e, b):
        return pltpu.make_async_copy(pieces.at[:, e], weights.at[b], wsem.at[b])

    def kept(e, b):
        return [
            pltpu.make_async_copy(
                grads.at[b, dp_index(x + rx, y + ry, core)], keep_ref.at[k, e], gsem.at[b, k]
            )
            for k, (rx, ry) in enumerate(SLOTS)
        ]

    def given(e, b):
        return [
            pltpu.make_async_remote_copy(
                src_ref=grads.at[b, dp_index(x + rx, y + ry, core + 1)],
                dst_ref=given_ref.at[k, e],
                send_sem=gsem.at[b, 8 + k],
                recv_sem=rsem.at[e, k],
                device_id={"dp": other},
                device_id_type=MESH,
            )
            for k, (rx, ry) in enumerate(SLOTS)
        ]

    def stored(e, b):
        for c in kept(e, b):
            c.wait()
        for c in given(e, b):
            c.wait_send()

    load(0, 0).start()

    def onehot(b):
        places = lax.broadcasted_iota(jnp.int32, (CAP, TOK), 0).astype(F32)
        return [(places == slot_ref[b, e : e + 1, :]) for e in range(LOCAL)]

    def collect(b, _):
        hot = onehot(b)
        pick = jnp.concatenate([h.astype(F32) for h in hot], axis=0).astype(BF)
        xg[b] = dot(pick, rows_ref[b], ((1,), (0,))).astype(BF)
        cg[b] = dot(pick, cot_ref[b], ((1,), (0,))).astype(BF)
        for e in range(LOCAL):
            g = jnp.sum(jnp.where(hot[e], gate_ref[b, e : e + 1, :], 0.0), axis=1, keepdims=True)
            gates[e, pl.ds(b * CAP, CAP), :] = jnp.broadcast_to(g, (CAP, 128))
        return _

    lax.fori_loop(0, PEERS, collect, 0)

    def expert(e, _):
        b = lax.rem(e, 2)
        load(e, b).wait()

        @pl.when(e + 1 < LOCAL)
        def _next():
            load(e + 1, 1 - b).start()

        @pl.when(e >= 2)
        def _free():
            stored(e - 2, b)

        span = pl.ds(pl.multiple_of(e * CAP, CAP), CAP)
        rows = xg[:, span, :].reshape(PEERS * CAP, DIM)
        cot = cg[:, span, :].reshape(PEERS * CAP, DIM)
        gate = gates[e][:, :1]
        w_gate = weights[b, :, 0:96, :].reshape(DIM, FFE)
        gate_act = dot(rows, w_gate, ((1,), (0,)))
        w_up = weights[b, :, 96:192, :].reshape(DIM, FFE)
        up_act = dot(rows, w_up, ((1,), (0,)))
        sig = 1.0 / (1.0 + jnp.exp(-gate_act))
        silu = gate_act * sig
        hidden = (silu * up_act).astype(BF)
        grad_out = (cot.astype(F32) * gate).astype(BF)
        inner = jnp.zeros((PEERS * CAP, 1), F32)
        grad_hidden = jnp.zeros((PEERS * CAP, FFE), F32)
        gated = []
        for k in range(3):
            lanes = slice(k * FFE, (k + 1) * FFE)
            w_down = weights[b, :, 192 + 32 * k : 224 + 32 * k, :].reshape(FFE, FFE)
            part = dot(hidden, w_down, ((1,), (0,))).astype(BF).astype(F32)
            inner = inner + jnp.sum(part * cot[:, lanes].astype(F32), axis=1, keepdims=True)
            gated.append((part * gate).astype(BF))
            grad_hidden = grad_hidden + dot(grad_out[:, lanes], w_down, ((1,), (1,)))
            grads[b, :, 192 + 32 * k : 224 + 32 * k, :] = (
                dot(hidden, grad_out[:, lanes], ((0,), (0,))).astype(BF).reshape(DP, 32, FFE)
            )
        inners[e] = jnp.broadcast_to(inner, (PEERS * CAP, 128))
        grad_gate = (grad_hidden * up_act * sig * (1.0 + gate_act * (1.0 - sig))).astype(BF)
        grad_up = (grad_hidden * silu).astype(BF)
        grads[b, :, 0:96, :] = (
            dot(rows, grad_gate, ((0,), (0,))).astype(BF).reshape(DP, ROWS, FFE)
        )
        grads[b, :, 96:192, :] = (
            dot(rows, grad_up, ((0,), (0,))).astype(BF).reshape(DP, ROWS, FFE)
        )
        for c in kept(e, b) + given(e, b):
            c.start()
        back = dot(grad_gate, w_gate, ((1,), (1,))) + dot(grad_up, w_up, ((1,), (1,)))
        xg[:, span, :] = back.astype(BF).reshape(PEERS, CAP, DIM)
        for k in range(3):
            cg[:, span, k * FFE : (k + 1) * FFE] = gated[k].reshape(PEERS, CAP, FFE)
        return _

    lax.fori_loop(0, LOCAL, expert, 0)

    def combine(b, _):
        hot = onehot(b)
        pick = jnp.concatenate([h.astype(F32) for h in hot], axis=0).astype(BF)
        out_ref[b] = dot(pick, cg[b], ((0,), (0,))).astype(BF)
        back_ref[b] = dot(pick, xg[b], ((0,), (0,))).astype(BF)
        lines = []
        for e in range(LOCAL):
            value = inners[e, pl.ds(b * CAP, CAP), :][:, :1]
            lines.append(jnp.sum(jnp.where(hot[e], value, 0.0), axis=0, keepdims=True))
        inner_ref[b] = jnp.concatenate(lines + [jnp.zeros((8 - LOCAL, TOK), F32)], axis=0)
        return _

    lax.fori_loop(0, PEERS, combine, 0)
    for e in (LOCAL - 2, LOCAL - 1):
        stored(e, e % 2)
    for e in range(LOCAL):
        for c in given(e, e % 2):
            c.wait_recv()


def run_experts(rows, cot, slots, gates, pieces):
    vmem = pl.BlockSpec(memory_space=pltpu.VMEM)
    piece = (LOCAL, 3 * ROWS, FFE)
    return pl.pallas_call(
        experts_kernel,
        out_shape=[
            jax.ShapeDtypeStruct((PEERS, TOK, DIM), BF),
            jax.ShapeDtypeStruct((PEERS, TOK, DIM), BF),
            jax.ShapeDtypeStruct((PEERS, 8, TOK), F32),
            jax.ShapeDtypeStruct((8,) + piece, BF),
            jax.ShapeDtypeStruct((8,) + piece, BF),
        ],
        in_specs=[vmem] * 4 + any_specs(1),
        out_specs=[vmem] * 3 + any_specs(2),
        scratch_shapes=[
            pltpu.VMEM((PEERS, LOCAL * CAP, DIM), BF),
            pltpu.VMEM((PEERS, LOCAL * CAP, DIM), BF),
            pltpu.VMEM((2, DP, 3 * ROWS, FFE), BF),
            pltpu.VMEM((2, DP, 3 * ROWS, FFE), BF),
            pltpu.VMEM((LOCAL, PEERS * CAP, 128), F32),
            pltpu.VMEM((LOCAL, PEERS * CAP, 128), F32),
            pltpu.SemaphoreType.DMA((2,)),
            pltpu.SemaphoreType.DMA((2, 16)),
            pltpu.SemaphoreType.DMA((LOCAL, 8)),
        ],
        compiler_params=pltpu.CompilerParams(
            collective_id=2, has_side_effects=True, vmem_limit_bytes=63 << 20
        ),
        cost_estimate=pl.CostEstimate(
            flops=20_000_000_000, bytes_accessed=60_000_000, transcendentals=700_000
        ),
    )(rows, cot, slots, gates, pieces)


def finish_kernel(mixed, tokens, experts, small, output, *refs):
    outs, (mixed_ref, tokens_ref, experts_ref, small_ref, output_ref, cut_ref, sem) = (
        refs[:10],
        refs[10:],
    )
    mixed_out, tokens_out, q_out, k_out, v_out, output_out, tail_out, gate, up, down = outs
    loads = [
        pltpu.make_async_copy(src, dst, sem.at[13 + i])
        for i, (src, dst) in enumerate(
            (
                (small, small_ref),
                (experts, experts_ref),
                (tokens, tokens_ref),
                (mixed, mixed_ref),
                (output, output_ref),
            )
        )
    ]
    for c in loads:
        c.start()
    for c in loads[1:]:
        c.wait()
    copies = [
        pltpu.make_async_copy(mixed_ref, mixed_out, sem.at[1]),
        pltpu.make_async_copy(tokens_ref, tokens_out, sem.at[2]),
        pltpu.make_async_copy(output_ref, output_out, sem.at[3]),
        pltpu.make_async_copy(experts_ref.at[:, pl.ds(0, ROWS)], gate, sem.at[4]),
        pltpu.make_async_copy(experts_ref.at[:, pl.ds(ROWS, ROWS)], up, sem.at[5]),
    ] + [
        pltpu.make_async_copy(
            experts_ref.at[:, pl.ds(2 * ROWS + 32 * k, 32)],
            down.at[:, :, pl.ds(k * FFE, FFE)],
            sem.at[6 + k],
        )
        for k in range(3)
    ]
    for c in copies:
        c.start()
    loads[0].wait()
    total = small_ref[0]
    for j in range(1, PEERS):
        total = total + small_ref[j]
    cut_ref[...] = jnp.concatenate(
        [small_ref[j, :, :QS] for j in range(PEERS)]
        + [small_ref[j, :, QS : QS + HEAD] for j in range(PEERS)]
        + [small_ref[j, :, QS + HEAD : ROUTER] for j in range(PEERS)]
        + [total[:, 256:SLICE]],
        axis=1,
    )
    widths = (DIM, KV_HEADS * HEAD, KV_HEADS * HEAD, SLICE - 256)
    begins = (0, DIM, DIM + KV_HEADS * HEAD, DIM + 2 * KV_HEADS * HEAD)
    for i, ref in enumerate((q_out, k_out, v_out, tail_out)):
        c = pltpu.make_async_copy(cut_ref.at[:, pl.ds(begins[i], widths[i])], ref, sem.at[9 + i])
        c.start()
        copies.append(c)
    for c in copies:
        c.wait()


def finish(*args):
    shape = jax.ShapeDtypeStruct
    width = KV_HEADS * HEAD
    return pl.pallas_call(
        finish_kernel,
        out_shape=[
            shape((TOK, DIM), BF),
            shape((TOK, DIM), F32),
            shape((12, DIM), F32),
            shape((12, width), F32),
            shape((12, width), F32),
            shape((12, DIM), F32),
            shape((12, SLICE - 256), F32),
            shape((LOCAL, ROWS, FFE), F32),
            shape((LOCAL, ROWS, FFE), F32),
            shape((LOCAL, 32, DIM), F32),
        ],
        in_specs=any_specs(5),
        out_specs=any_specs(10),
        scratch_shapes=[
            pltpu.VMEM((TOK, DIM), BF),
            pltpu.VMEM((TOK, DIM), F32),
            pltpu.VMEM((LOCAL, 3 * ROWS, FFE), F32),
            pltpu.VMEM((PEERS, 12, SLICE), F32),
            pltpu.VMEM((12, DIM), F32),
            pltpu.VMEM((12, DIM + 2 * width + SLICE - 256), F32),
            pltpu.SemaphoreType.DMA((18,)),
        ],
        compiler_params=pltpu.CompilerParams(vmem_limit_bytes=63 << 20),
    )(*args)


def norm_back(values, row_scale, gain_vector, grad_normed):
    weighted = grad_normed * gain_vector
    return row_scale * weighted - values * row_scale**3 * jnp.mean(
        weighted * values, axis=-1, keepdims=True
    )


def local(
    tokens,
    cotangent,
    seq_lengths,
    expert_ids,
    w_query,
    w_key,
    w_value,
    w_output,
    norm_one,
    norm_two,
    w_router,
    w_gate,
    w_up,
    w_down,
):
    tail = jnp.concatenate(
        [w_router, norm_one[:, None], norm_two[:, None], jnp.zeros((12, SLICE - GAINS - 2), BF)],
        axis=1,
    )
    (
        pieces,
        cot_all,
        slots_all,
        rows_all,
        gates_all,
        tokens_all,
        normed_all,
        slices_all,
        output_all,
        *kept,
    ) = first_phase(
        w_query,
        w_key,
        w_value,
        tail,
        w_output,
        tokens,
        cotangent,
        expert_ids,
        seq_lengths,
        w_gate,
        w_up,
        w_down,
    )
    out_part, back_part, inner_part, keep, given = run_experts(
        rows_all, cot_all, slots_all, gates_all, pieces
    )
    mixed, grad_tokens, expert_grads, small_own, output_own, _ = last_phase(
        back_part,
        inner_part,
        out_part,
        keep,
        given,
        tokens_all,
        normed_all,
        slices_all,
        output_all,
        tokens,
        cotangent,
        *kept,
    )
    mixed, grad_tokens, query, key, value, output, rest, gate, up, down = finish(
        mixed, grad_tokens, expert_grads, small_own, output_own
    )
    rest = rest[:, ROUTER - 256 :]
    return (
        mixed,
        grad_tokens,
        query,
        key,
        value,
        output,
        rest[:, EXPERTS],
        rest[:, EXPERTS + 1],
        rest[:, :EXPERTS],
        gate,
        up,
        down,
    )


def solution(mesh):
    both = P(("dp", "expert"), None)
    line = P(("dp", "expert"))
    cube = P("expert", "dp", None)
    in_specs = (both, both, P("dp", None), both, both, both, both, both)
    in_specs = in_specs + (line, line, both, cube, cube, cube)
    out_specs = (both,) * 6 + (line, line, both, cube, cube, cube)
    return jax.shard_map(local, mesh=mesh, in_specs=in_specs, out_specs=out_specs, check_vma=False)
```

```python
import functools
import math

import jax
import jax.numpy as jnp
from jax import lax
from jax.experimental import pallas as pl
from jax.experimental.pallas import tpu as pltpu
from jax.sharding import PartitionSpec as P

HEADS = 24
KV_HEADS = 8
HEAD = 64
DIM = 1536
FFE = 512
EXPERTS = 40
LOCAL = 5
CAP = 32
TOK = 128
PEERS = 8
DP = 16
GROUP = TOK * PEERS
REP = HEADS // KV_HEADS
SLICE = 384
QS = REP * HEAD
ROWS = 96
ROUTER = QS + 2 * HEAD
GAINS = ROUTER + EXPERTS

epsilon = 1e-06
rope_base = 10000.0
masked_score = -1e30
MESH = pl.DeviceIdType.MESH
BF = jnp.bfloat16
F32 = jnp.float32

RELATIVE = ((2, 1), (2, 0), (1, 1), (3, 1), (0, 1), (1, 0), (3, 0))
SLOTS = ((0, 0), (1, 0), (0, 1), (0, 3), (1, 1), (1, 3), (0, 2), (1, 2))


def expert_peers():
    me = lax.axis_index("expert")
    z, x = me // 2, me % 2
    return me, [(z + rz) % 4 * 2 + (x + rx) % 2 for rz, rx in RELATIVE]


def dp_place():
    d = lax.axis_index("dp")
    return d // 8, (d // 2) % 4, d % 2


def dp_index(x, y, core):
    return (x % 2 * 4 + y % 4) * 2 + core % 2


def signal_all(expert_ids, dp_ids):
    barrier = pltpu.get_barrier_semaphore()
    for p in expert_ids:
        pl.semaphore_signal(barrier, inc=1, device_id={"expert": p}, device_id_type=MESH)
    for p in dp_ids:
        pl.semaphore_signal(barrier, inc=1, device_id={"dp": p}, device_id_type=MESH)
    return lambda: pl.semaphore_wait(barrier, len(expert_ids) + len(dp_ids))


def any_specs(count):
    return [pl.BlockSpec(memory_space=pltpu.HBM)] * count


def expert_copies(ins, outs, modes, send, recv):
    me, peers = expert_peers()
    copies = []
    for r, p in enumerate(peers):
        for i, mode in enumerate(modes):
            copies.append(
                pltpu.make_async_remote_copy(
                    src_ref=ins[i] if mode == "gather" else ins[i].at[p],
                    dst_ref=outs[i].at[me],
                    send_sem=send.at[i, r],
                    recv_sem=recv.at[i, r],
                    device_id={"expert": p},
                    device_id_type=MESH,
                )
            )
    return copies


def own_copies(ins, outs, modes, sems):
    me = lax.axis_index("expert")
    return [
        pltpu.make_async_copy(
            ins[i] if mode == "gather" else ins[i].at[me], outs[i].at[me], sems.at[i]
        )
        for i, mode in enumerate(modes)
    ]


def lasting(us):
    return pl.CostEstimate(flops=us * 1_000_000_000, bytes_accessed=0, transcendentals=0)


class Gather:
    def __init__(self, src, out, send, recv, local):
        self.src, self.out, self.send, self.recv, self.local = src, out, send, recv, local
        me = lax.axis_index("expert")
        z, x = me // 2, me % 2

        def place(dz, dx):
            return (z + dz) % 4 * 2 + (x + dx) % 2

        self.slots = [
            place(0, 1),
            place(3, 0),
            place(1, 0),
            place(3, 1),
            place(1, 1),
            place(2, 0),
            place(2, 1),
        ]
        self.me = me
        x, up, down = place(0, 1), place(1, 0), place(3, 0)
        self.moves = ((None, x), (None, up), (None, down), (0, up), (0, down), (1, up), (4, down))
        self.started = []

    def descriptor(self, k, src, slot, target):
        return pltpu.make_async_remote_copy(
            src_ref=src,
            dst_ref=self.out.at[slot],
            send_sem=self.send.at[k],
            recv_sem=self.recv.at[k],
            device_id={"expert": target},
            device_id_type=MESH,
        )

    def begin(self):
        self.own = pltpu.make_async_copy(self.src, self.out.at[self.me], self.local)
        self.own.start()

    def issue(self, k):
        source, target = self.moves[k]
        slot = self.me if source is None else self.slots[source]
        src = self.src if source is None else self.out.at[slot]
        c = self.descriptor(k, src, slot, target)
        c.start()
        self.started.append(c)

    def arrive(self, k):
        self.descriptor(k, self.src, self.slots[k], self.moves[0][1]).wait_recv()


class Line:
    def __init__(self, src, view, moves, send, recv):
        self.src, self.view, self.send, self.recv = src, view, send, recv
        x, y, core = dp_place()
        self.targets = {
            "x": dp_index(x + 1, y, core),
            "up": dp_index(x, y + 1, core),
            "down": dp_index(x, y + 3, core),
            "core": dp_index(x, y, core + 1),
        }
        self.moves = dict(moves)
        for k in range(8):
            self.moves[8 + k] = (k, "core")
        self.slots = [dp_index(x + rx, y + ry, core + c) for c in range(2) for rx, ry in SLOTS]
        self.started = []

    def descriptor(self, k, src, slot, where):
        return pltpu.make_async_remote_copy(
            src_ref=src,
            dst_ref=self.view(slot),
            send_sem=self.send.at[k],
            recv_sem=self.recv.at[k],
            device_id={"dp": self.targets[where]},
            device_id_type=MESH,
        )

    def issue(self, k):
        source, where = self.moves[k]
        slot = self.slots[source]
        src = self.src if source == 0 else self.view(slot)
        c = self.descriptor(k, src, slot, where)
        c.start()
        self.started.append(c)

    def arrive(self, k):
        slot = self.slots[k]
        self.descriptor(k, self.view(slot), slot, "x").wait_recv()


X_FIRST = {
    1: (0, "x"),
    2: (0, "down"),
    3: (0, "up"),
    4: (1, "down"),
    5: (1, "up"),
    6: (3, "up"),
    7: (4, "down"),
}
Y_FIRST = {
    1: (0, "x"),
    2: (0, "down"),
    3: (0, "up"),
    4: (2, "x"),
    5: (3, "x"),
    6: (3, "up"),
    7: (6, "x"),
}
Y_FIRST_DOWN = {**Y_FIRST, 6: (2, "down")}
PARTS = (
    ((0, 1), (0, 288), X_FIRST),
    ((1, 1), (0, 288), X_FIRST),
    ((2, 1), (0, 288), X_FIRST),
    ((3, 1), (0, 288), Y_FIRST),
    ((4, 1), (0, 192), Y_FIRST_DOWN),
    ((4, 1), (192, 96), X_FIRST),
)
KEPT = tuple(
    jax.ShapeDtypeStruct(shape, kind)
    for shape, kind in (
        ((PEERS, REP * TOK, HEAD), BF),
        ((GROUP, HEAD), BF),
        ((GROUP, HEAD), BF),
        ((PEERS, REP * TOK, 128), F32),
        ((PEERS, TOK, QS), BF),
        ((TOK, DIM), F32),
        ((TOK, DIM), BF),
        ((EXPERTS, TOK), F32),
        ((GROUP, 128), F32),
        ((GROUP, 128), F32),
        ((GROUP, 128), jnp.int32),
    )
)
FIRST_STEPS = ("ss", "so", "sl", "a", "g", "ls", "lo", "P0", "P1", "A0", "A1", "A2", "C2", "gt", "tb")
FIRST_STEPS = FIRST_STEPS + tuple("tr%d" % i for i in range(4))
FIRST_LINES = ("t", "c", "r", "s", "o") + tuple("p%d." % i for i in range(len(PARTS)))
FIRST_STEPS = FIRST_STEPS + tuple(n + str(k) for n in FIRST_LINES for k in range(16))
FIRST_ORDER = (
    1, -1, 2, 6, 76, 69, 70, 71, -2, 135, 166, 20, 108, 188, 38, 156, 124, 15, 3, -69, 77, -71, 79,
    172, 21, -70, 78, 140, 7, 102, 92, -166, 174, 74, 73, -135, 143, 101, 22, 119, 16, -74, 82, 37,
    150, 17, -73, 81, -102, 110, 149, 103, 72, -101, 109, 18, -20, 24, -119, 127, 170, -150, 158,
    23, 19, -72, 80, 152, 105, 134, -149, 157, -103, 111, -170, 178, -21, 25, 85, -24, 26, 183, 75,
    -152, 160, -105, 113, 87, 118, -134, 142, -183, 191, -75, 83, 181, -37, 41, -85, 93, 36, 89,
    88, -22, -23, -25, -26, -76, -77, -78, -79, -80, -81, -82, -83, 8, -87, 90, 95, -118, 126,
    -181, 184, 133, 189, 9, 185, 86, 10, -184, 187, -36, 40, -89, 97, 138, 39, 192, -88, 96, 91,
    117, 11, -185, 193, -86, 94, -133, 141, 137, -187, 195, 136, 168, -90, 98, 12, 4, -138, 146,
    -117, 125, -40, 42, -91, 99, -168, 176, 165, 151, 122, 120, 171, 104, -4, -92, -93, -94, -95,
    -96, -97, -98, -99, 13, -151, 159, -165, 173, 53, 54, 52, -136, 144, -137, 145, 14, 5, -171,
    179, -120, 128, 154, -122, 130, 139, -104, 112, 153, -53, 57, 106, -52, 56, -154, 162, 107,
    -139, 147, 155, 167, -153, 161, 55, -106, 114, 123, -56, 58, -107, 115, 121, -167, 175, 169,
    -155, 163, 182, -123, 131, 186, -169, 177, -121, 129, -182, 190, -186, 194, -108, -188, -156,
    -124, -172, -140, -174, -143, -38, -3, -110, -109, -127, -158, -157, -111, -178, -160, -113,
    -142, -191, -126, -189, -41, -192, -193, -141, -195, -39, -146, -125, -176, -42, -159, -173,
    -144, -145, -179, -128, -130, -54, -112, -5, -162, -147, -161, -57, -114, -115, -175, -163,
    -55, -131, -58, -177, -129, -190, -194,
)


def first_kernel(*refs):
    w_dense, (output, tokens, cot, ids, lengths, w_gate, w_up, w_down) = refs[:4], refs[4:12]
    (
        pieces_out,
        cot_all,
        slots_all,
        rows_all,
        gates_all,
        tokens_out,
        normed_out,
        small_out,
        output_out,
    ) = refs[12:21]
    kept_out = refs[21:32]
    kept_refs = refs[32:43]
    (
        query_ref,
        key_ref,
        value_ref,
        log_ref,
        attended_ref,
        middle_ref,
        normed_two_ref,
        gates_ref,
        cos_ref,
        sin_ref,
        start_ref,
    ) = kept_refs
    w_query, w_key, w_value, tail = refs[43:47]
    (
        piece,
        ids_ref,
        member_ref,
        slot_send,
        slices,
        small_in,
        output_in,
        small_rows,
        output_rows,
        small,
        dense,
        tokens_in,
        normed,
        att_send,
        gate_send,
        s_small,
        s_dense,
        s_piece,
        r_small,
        r_dense,
        r_piece,
        s_gather,
        r_gather,
        s_direct,
        r_direct,
        l_sem,
    ) = refs[47:]
    x, y, core = dp_place()
    me = lax.axis_index("expert")
    mine = dp_index(x, y, core)
    loads = [
        pltpu.make_async_copy(src, dst, l_sem.at[20 + i])
        for i, (src, dst) in enumerate(
            zip(w_dense + (ids,), (w_query, w_key, w_value, tail, ids_ref))
        )
    ]
    own = [
        pltpu.make_async_copy(w_gate, piece.at[:, pl.ds(0, ROWS)], l_sem.at[15]),
        pltpu.make_async_copy(w_up, piece.at[:, pl.ds(ROWS, ROWS)], l_sem.at[16]),
    ] + [
        pltpu.make_async_copy(
            w_down.at[:, :, pl.ds(k * FFE, FFE)],
            piece.at[:, pl.ds(2 * ROWS + 32 * k, 32)],
            l_sem.at[17 + k],
        )
        for k in range(3)
    ]
    for c in loads + own:
        c.start()
    _, peers = expert_peers()
    greeted = signal_all(
        peers,
        [
            dp_index(x + 1, y, core),
            dp_index(x, y + 1, core),
            dp_index(x, y + 3, core),
            dp_index(x, y, core + 1),
        ],
    )
    for c in loads + own:
        c.wait()
    for j in range(PEERS):
        slices[j] = jnp.concatenate(
            [
                w_query[:, QS * j : QS * (j + 1)],
                w_key[:, HEAD * j : HEAD * (j + 1)],
                w_value[:, HEAD * j : HEAD * (j + 1)],
                tail[...],
            ],
            axis=1,
        )
    greeted()

    def direct(i, src, out, mode):
        part = expert_copies(
            [src], [out], [mode], s_direct.at[pl.ds(i, 1)], r_direct.at[pl.ds(i, 1)]
        ) + own_copies([src], [out], [mode], l_sem.at[pl.ds(i, 1)])

        def start():
            for c in part:
                c.start()

        def wait():
            for c in part:
                c.wait()

        return start, wait

    saved = []

    def save(src, dst, i):
        c = pltpu.make_async_copy(src, dst, l_sem.at[i])
        c.start()
        saved.append(c)

    issue, arrive = {}, {}
    for i, (name, src, out, mode) in enumerate(
        (
            ("ss", slices, small_in, "exchange"),
            ("so", output, output_in, "gather"),
            ("sl", slot_send, slots_all, "exchange"),
            ("a", att_send, attended_ref, "exchange"),
            ("g", gate_send, gates_all, "exchange"),
        )
    ):
        issue[name], arrive[name] = direct(i, src, out, mode)
    lines = {}
    for i, (name, src, out) in enumerate(
        (("t", tokens, tokens_in), ("c", cot, cot_all), ("r", normed_two_ref, rows_all))
    ):
        lines[name] = Gather(src, out, s_gather.at[i], r_gather.at[i], l_sem.at[5 + i])
    for i, (name, src, out) in enumerate((("s", small_rows, small), ("o", output_rows, dense))):
        lines[name] = Line(src, lambda k, out=out: out.at[k], X_FIRST, s_dense.at[i], r_dense.at[i])
    for i, ((expert, count), (row, rows), moves) in enumerate(PARTS):
        def view(k, span=pl.ds(expert, count), part=pl.ds(row, rows)):
            return pieces_out.at[k, span, part]

        own_part = piece.at[pl.ds(expert, count), pl.ds(row, rows)]
        lines["p%d." % i] = Line(own_part, view, moves, s_piece.at[i], r_piece.at[i])
    for name, line in lines.items():
        for k in range(16):
            issue[name + str(k)] = functools.partial(line.issue, k)
            arrive[name + str(k)] = functools.partial(line.arrive, k)

    kept = {}

    def lay_out(name, landed, rows, out, i):
        rows[...] = jnp.concatenate([landed[j] for j in range(PEERS)], axis=0)
        kept[name] = pltpu.make_async_copy(rows, out.at[mine], l_sem.at[8 + i])
        kept[name].start()

    def tables():
        named = jnp.zeros((TOK, 128), F32)
        experts = lax.broadcasted_iota(jnp.int32, (TOK, 128), 1)
        for k in range(ids_ref.shape[1]):
            named = named + (ids_ref[:, k : k + 1] == experts).astype(F32)
        before = (lax.broadcasted_iota(jnp.int32, (TOK, 128), 0) > experts).astype(F32)
        places = dot(before.astype(BF), named.astype(BF), ((1,), (0,)))
        member_ref[...] = jnp.transpose(jnp.where(named > 0.0, places, -1.0))[:EXPERTS]
        slot_send[...] = jnp.full_like(slot_send, -1.0)
        for j in range(PEERS):
            slot_send[j, 0:LOCAL, :] = member_ref[LOCAL * j : LOCAL * (j + 1), :]

    def turns(first, last):
        second = lengths[0, 0]
        third = second + lengths[0, 1]
        fourth = third + lengths[0, 2]

        def block(i, _):
            span = pl.ds(pl.multiple_of(i * TOK, TOK), TOK)
            place = lax.broadcasted_iota(jnp.int32, (TOK, 128), 0) + i * TOK
            begins = jnp.where(
                place >= fourth,
                fourth,
                jnp.where(place >= third, third, jnp.where(place >= second, second, 0)),
            )
            start_ref[span, :] = begins
            lane = lax.broadcasted_iota(jnp.int32, (TOK, 128), 1)
            step = (lane % (HEAD // 2)).astype(F32) * (2.0 / HEAD)
            angle = (place - begins).astype(F32) * jnp.exp(-step * math.log(rope_base))
            cos_ref[span, :] = jnp.cos(angle)
            sin_ref[span, :] = jnp.where(lane % HEAD < HEAD // 2, -1.0, 1.0) * jnp.sin(angle)
            return _

        lax.fori_loop(first, last, block, 0)

    issue["ls"] = functools.partial(lay_out, "s", small_in, small_rows, small, 0)
    issue["lo"] = functools.partial(lay_out, "o", output_in, output_rows, dense, 1)

    def project(i, _):
        values = tokens_in[pl.ds(2 * i, 2)].reshape(2 * TOK, DIM).astype(F32)
        scale = lax.rsqrt(jnp.mean(values * values, axis=-1, keepdims=True) + epsilon)
        low = (values * scale * kept["gains"][0:1]).astype(BF)
        normed[pl.ds(2 * i, 2)] = low.reshape(2, TOK, DIM)
        qkv = dot(low, small[...].reshape(DIM, SLICE), ((1,), (0,)))
        span = pl.ds(pl.multiple_of(i * 2 * TOK, 2 * TOK), 2 * TOK)
        cosine, sine = cos_ref[span, :], sin_ref[span, :]
        lane = lax.broadcasted_iota(jnp.int32, (2 * TOK, 128), 1)
        turned = []
        for h in range(2):
            v = qkv[:, 128 * h : 128 * h + 128]
            other = jnp.where(lane % HEAD < HEAD // 2, pltpu.roll(v, 96, 1), pltpu.roll(v, 32, 1))
            turned.append((v * cosine + other * sine).astype(BF))
        heads = (turned[0][:, :HEAD], turned[0][:, HEAD:], turned[1][:, :HEAD])
        for b in range(2):
            for h in range(REP):
                query_ref[2 * i + b, h * TOK : (h + 1) * TOK, :] = heads[h][
                    b * TOK : (b + 1) * TOK
                ]
        key_ref[span, :] = turned[1][:, HEAD:]
        value_ref[span, :] = qkv[:, QS + HEAD : ROUTER].astype(BF)
        return _

    def project_first():
        lines["t"].own.wait()
        kept["s"].wait()
        pick = (
            lax.broadcasted_iota(jnp.int32, (8, SLICE), 1)
            == lax.broadcasted_iota(jnp.int32, (8, SLICE), 0) + GAINS
        )
        kept["gains"] = dot(
            pick.astype(F32).astype(BF), small[...].reshape(DIM, SLICE), ((1,), (1,))
        )
        lax.fori_loop(0, 2, project, 0)

    def project_rest():
        lax.fori_loop(2, 4, project, 0)
        save(tokens_in, tokens_out, 10)
        save(normed, normed_out, 11)
        save(small, small_out, 12)

    def attend(width, i, _):
        scores = dot(query_ref[i], key_ref[0:width, :], ((1,), (1,))) * HEAD ** (-0.5)
        keys = lax.broadcasted_iota(jnp.int32, (TOK, width), 1)
        rows = lax.broadcasted_iota(jnp.int32, (TOK, width), 0) + i * TOK
        begins = start_ref[pl.ds(pl.multiple_of(i * TOK, TOK), TOK), :][:, :1]
        allowed = (keys <= rows) & (keys >= begins)
        scores = jnp.where(allowed[None], scores.reshape(REP, TOK, width), masked_score)
        top = jnp.max(scores, axis=-1, keepdims=True)
        terms = jnp.exp(scores - top)
        total = jnp.sum(terms, axis=-1, keepdims=True)
        probs = (terms / total).astype(BF).reshape(REP * TOK, width)
        out = dot(probs, value_ref[0:width, :], ((1,), (0,))).astype(BF)
        att_send[i] = jnp.concatenate([out[h * TOK : (h + 1) * TOK] for h in range(REP)], axis=1)
        log_ref[i] = jnp.broadcast_to(
            (top + jnp.log(total)).reshape(REP * TOK, 1), (REP * TOK, 128)
        )
        return _

    issue["P0"], issue["P1"] = project_first, project_rest
    for name, first, last, width in (("A0", 0, 4, 512), ("A1", 4, 6, 1024), ("A2", 6, 8, 1024)):
        issue[name] = functools.partial(
            lax.fori_loop, first, last, functools.partial(attend, width), 0
        )

    def out_project():
        kept["o"].wait()
        save(dense, output_out, 13)
        middle = tokens_in[me].astype(F32)
        for j in range(PEERS):
            middle = middle + dot(
                attended_ref[j], dense[2 * j : 2 * j + 2].reshape(QS, DIM), ((1,), (0,))
            )
        middle_ref[...] = middle
        scale_two = lax.rsqrt(jnp.mean(middle * middle, axis=-1, keepdims=True) + epsilon)
        normed_two_ref[...] = (middle * scale_two * kept["gains"][1:2]).astype(BF)
        lines["r"].begin()

    def choose():
        router = small[:, :, 256:SLICE].reshape(DIM, SLICE - 256)
        logits = dot(router, normed_two_ref[...], ((0,), (1,)))[ROUTER - 256 : GAINS - 256]
        member = member_ref[...] >= 0.0
        chosen = jnp.where(member, logits, masked_score)
        weight = jnp.where(member, jnp.exp(chosen - jnp.max(chosen, axis=0, keepdims=True)), 0.0)
        gates_ref[...] = weight / jnp.sum(weight, axis=0, keepdims=True)
        gate_send[...] = jnp.zeros_like(gate_send)
        for j in range(PEERS):
            gate_send[j, 0:LOCAL, :] = gates_ref[LOCAL * j : LOCAL * (j + 1), :]

    issue["C2"], issue["gt"] = out_project, choose
    save(piece, pieces_out.at[mine], 14)
    lines["t"].begin()
    lines["c"].begin()
    issue["tb"] = tables
    for i in range(4):
        issue["tr%d" % i] = functools.partial(turns, 2 * i, 2 * i + 2)
    for step in FIRST_ORDER:
        (issue if step > 0 else arrive)[FIRST_STEPS[abs(step) - 1]]()
    lines["c"].own.wait()
    lines["r"].own.wait()
    for line in lines.values():
        for c in line.started:
            c.wait_send()
    for i, (src, dst) in enumerate(zip(kept_refs, kept_out)):
        save(src, dst, 25 + i)
    for c in saved:
        c.wait()


def first_phase(*args):
    hbm, smem = pl.BlockSpec(memory_space=pltpu.HBM), pl.BlockSpec(memory_space=pltpu.SMEM)
    shape = jax.ShapeDtypeStruct
    blocks = (PEERS, TOK, DIM)
    outs = [
        (shape((DP, LOCAL, 3 * ROWS, FFE), BF), hbm),
        (shape(blocks, BF), hbm),
        (shape((PEERS, 8, TOK), F32), hbm),
        (shape(blocks, BF), hbm),
        (shape((PEERS, 8, TOK), F32), hbm),
        (shape(blocks, BF), hbm),
        (shape(blocks, BF), hbm),
        (shape((DP, ROWS, SLICE), BF), hbm),
        (shape((DP, ROWS, DIM), BF), hbm),
    ] + [(k, hbm) for k in KEPT]
    dma = pltpu.SemaphoreType.DMA
    return pl.pallas_call(
        first_kernel,
        out_shape=[o[0] for o in outs],
        in_specs=[hbm] * 8 + [smem] + [hbm] * 3,
        out_specs=[o[1] for o in outs],
        scratch_shapes=[pltpu.VMEM(k.shape, k.dtype) for k in KEPT]
        + [pltpu.VMEM(a.shape, a.dtype) for a in args[:4]]
        + [
            pltpu.VMEM((LOCAL, 3 * ROWS, FFE), BF),
            pltpu.VMEM((TOK, 8), jnp.int32),
            pltpu.VMEM((EXPERTS, TOK), F32),
            pltpu.VMEM((PEERS, 8, TOK), F32),
            pltpu.VMEM((PEERS, 12, SLICE), BF),
            pltpu.VMEM((PEERS, 12, SLICE), BF),
            pltpu.VMEM((PEERS, 12, DIM), BF),
            pltpu.VMEM((ROWS, SLICE), BF),
            pltpu.VMEM((ROWS, DIM), BF),
            pltpu.VMEM((DP, ROWS, SLICE), BF),
            pltpu.VMEM((DP, ROWS, DIM), BF),
            pltpu.VMEM(blocks, BF),
            pltpu.VMEM(blocks, BF),
            pltpu.VMEM((PEERS, TOK, QS), BF),
            pltpu.VMEM((PEERS, 8, TOK), F32),
            dma((1,)),
            dma((2, 16)),
            dma((len(PARTS), 16)),
            dma((1,)),
            dma((2, 16)),
            dma((len(PARTS), 16)),
            dma((3, 7)),
            dma((3, 7)),
            dma((5, 7)),
            dma((5, 7)),
            dma((40,)),
        ],
        compiler_params=pltpu.CompilerParams(
            collective_id=1, has_side_effects=True, vmem_limit_bytes=63 << 20
        ),
        cost_estimate=lasting(120),
    )(*args)


def dot(a, b, contract):
    return lax.dot_general(a, b, ((contract[0], contract[1]), ((), ())), preferred_element_type=F32)


class Reduce:
    def __init__(self, src, own, landed, send, recv):
        self.src, self.own, self.landed = src, own, landed
        self.send, self.recv = send, recv
        me = lax.axis_index("expert")
        z, x = me // 2, me % 2
        self.place = lambda dz, dx: (z + dz) % 4 * 2 + (x + dx) % 2
        up, down, across = self.place(1, 0), self.place(3, 0), self.place(0, 1)
        self.moves = {
            0: ((2, 1), up),
            1: ((2, 0), down),
            2: (0, up),
            3: ((3, 1), down),
            4: ((1, 0), up),
            5: (1, down),
            6: (2, across),
        }
        self.started = []

    def issue(self, k):
        source, target = self.moves[k]
        relayed = isinstance(source, int)
        c = pltpu.make_async_remote_copy(
            src_ref=self.landed.at[source] if relayed else self.src.at[self.place(*source)],
            dst_ref=self.landed.at[k],
            send_sem=self.send.at[k],
            recv_sem=self.recv.at[k],
            device_id={"expert": target},
            device_id_type=MESH,
        )
        c.start()
        self.started.append(c)

    def arrive(self, k):
        pltpu.make_async_remote_copy(
            src_ref=self.landed.at[k],
            dst_ref=self.landed.at[k],
            send_sem=self.send.at[k],
            recv_sem=self.recv.at[k],
            device_id={"expert": self.moves[6][1]},
            device_id_type=MESH,
        ).wait_recv()

    def sum(self, block, *landed):
        total = self.own(*block)
        for k in landed:
            total = total + self.landed[k].astype(F32)
        return total

    def add(self, k):
        block, landed = (((1, 1), (0,)), ((3, 0), (1,)), ((0, 1), (2, 3)))[k]
        self.landed[k] = self.sum(block, *landed).astype(BF)

    def total(self):
        return self.sum((0, 0), 4, 5, 6)

    def finish(self):
        for c in self.started:
            c.wait_send()
        self.started = []


RING = {
    6: (0, "up", ()),
    7: (1, "down", ()),
    4: (2, "up", ()),
    5: (3, "down", (1,)),
    2: (4, "up", (0,)),
    3: (5, "down", ()),
    1: (6, "x", (2, 3)),
    0: (None, None, (4, 5, 6)),
}
ACROSS = {
    7: (3, "x", ()),
    4: (1, "x", ()),
    5: (2, "x", ()),
    1: (0, "x", ()),
    6: (4, "up", (3,)),
    2: (6, "up", (1, 4)),
    3: (7, "down", (2,)),
    0: (None, None, (0, 6, 7)),
}
ACROSS_DOWN = {**ACROSS, 6: (4, "down", (3,)), 2: (6, "up", (1,)), 3: (7, "down", (2, 4))}
WAYS = (RING, RING, RING, ACROSS, ACROSS_DOWN, RING)


def dp_targets():
    x, y, core = dp_place()
    return {
        "x": dp_index(x + 1, y, core),
        "up": dp_index(x, y + 1, core),
        "down": dp_index(x, y + 3, core),
        "core": dp_index(x, y, core + 1),
    }


class DenseSum:
    def __init__(self, grads, theirs, landed, send, recv):
        self.grads, self.theirs, self.landed, self.send, self.recv = grads, theirs, landed, send, recv
        self.targets = dp_targets()
        x, y, core = dp_place()
        self.slots = [dp_index(x + rx, y + ry, core) for rx, ry in SLOTS]
        self.others = [dp_index(x + rx, y + ry, core + 1) for rx, ry in SLOTS]
        self.carried = {j: (k, where) for k, (j, where, _) in RING.items()}
        self.started = []

    def descriptor(self, k, src, dst, where):
        return pltpu.make_async_remote_copy(
            src_ref=src,
            dst_ref=dst,
            send_sem=self.send.at[k],
            recv_sem=self.recv.at[k],
            device_id={"dp": self.targets[where]},
            device_id_type=MESH,
        )

    def issue(self, k):
        if k >= 8:
            src, dst, where = self.grads.at[self.others[k - 8]], self.theirs.at[k - 8], "core"
        else:
            slot, where = self.carried[k]
            src, dst = self.grads.at[self.slots[slot]], self.landed.at[k]
        c = self.descriptor(k, src, dst, where)
        c.start()
        self.started.append(c)

    def arrive(self, k):
        ref = self.theirs.at[k - 8] if k >= 8 else self.landed.at[k]
        self.descriptor(k, ref, ref, "x").wait_recv()

    def sum(self, k):
        total = self.grads[self.slots[k]].astype(F32) + self.theirs[k].astype(F32)
        for j in RING[k][2]:
            total = total + self.landed[j].astype(F32)
        return total

    def add(self, k):
        self.grads[self.slots[k]] = self.sum(k).astype(BF)

    def finish(self):
        for c in self.started:
            c.wait_send()


class Stage:
    def __init__(self, buffers, sems):
        self.buffers, self.sems = buffers, sems
        self.free = list(range(buffers.shape[0]))
        self.held = {}

    def fetch(self, name, src, rows):
        i = self.free.pop(0)
        ref = self.buffers.at[i, pl.ds(0, rows)]
        c = pltpu.make_async_copy(src, ref, self.sems.at[i])
        c.start()
        self.held[name] = (i, ref, c)

    def wait(self, name):
        self.held[name][2].wait()

    def take(self, name):
        i, ref, _ = self.held.pop(name)
        self.free.append(i)
        return ref


class ExpertSum:
    def __init__(self, own, given, landed, out, ends, way, stage, send, recv, store):
        self.own, self.given, self.landed, self.out, self.ends = own, given, landed, out, ends
        self.way, self.stage, self.send, self.recv, self.store = way, stage, send, recv, store
        self.rows = own(0).shape[0]
        self.targets = dp_targets()
        self.carried = {j: (k, where) for k, (j, where, _) in way.items()}
        self.started = []

    def descriptor(self, j, src, where):
        return pltpu.make_async_remote_copy(
            src_ref=src,
            dst_ref=self.landed(j),
            send_sem=self.send.at[j],
            recv_sem=self.recv.at[j],
            device_id={"dp": self.targets[where]},
            device_id_type=MESH,
        )

    def issue(self, j):
        k, where = self.carried[j]
        c = self.descriptor(j, self.own(k), where)
        c.start()
        self.started.append(c)

    def arrive(self, j):
        self.descriptor(j, self.landed(j), "x").wait_recv()

    def fetch_given(self, k):
        self.stage.fetch((id(self), "l", k), self.given(k), self.rows)

    def fetch_landed(self, j):
        self.stage.fetch((id(self), "h", j), self.landed(j), self.rows)

    def wait_given(self, k):
        self.stage.wait((id(self), "l", k))

    def wait_landed(self, j):
        self.stage.wait((id(self), "h", j))

    def accumulate(self, k, names, out):
        refs = [self.stage.take((id(self),) + n) for n in names]

        def body(i, _):
            span = pl.ds(pl.multiple_of(i * 32, 32), 32)
            total = self.own(k)[span, :].astype(F32)
            for r in refs:
                total = total + r[span, :].astype(F32)
            out[span, :] = total.astype(out.dtype)
            return _

        lax.fori_loop(0, self.rows // 32, body, 0)

    def add_given(self, k):
        self.accumulate(k, [("l", k)], self.own(k))

    def add_landed(self, k):
        out = self.own(k) if k > 0 else self.ends
        self.accumulate(k, [("h", j) for j in self.way[k][2]], out)

    def write(self):
        self.save = pltpu.make_async_copy(self.ends, self.out, self.store)
        self.save.start()

    def finish(self):
        for c in self.started:
            c.wait_send()


LAST_STEPS = ("in", "e", "qo", "qs", "C4", "GO", "A0", "A1", "A2", "P0", "P1", "GS", "MX", "GT", "CO")
LAST_STEPS = LAST_STEPS + ("CS", "FI", "lz", "lw", "ly")
LAST_STEPS = LAST_STEPS + tuple(f + k for f in "zyg" for k in "0123456ABC")
for family in "os":
    LAST_STEPS = LAST_STEPS + tuple(family + str(k) for k in range(16))
    LAST_STEPS = LAST_STEPS + tuple(family + "a%d" % k for k in range(8)) + (family + "t",)
for part in range(len(PARTS)):
    LAST_STEPS = LAST_STEPS + tuple("u%d." % part + f + str(k) for f in ("", "l", "S", "R", "h") for k in range(8))
    LAST_STEPS = LAST_STEPS + ("u%d.w" % part,)
LAST_ORDER = (
    197, 277, 157, 21, 18, 22, 1, 19, -197, 205, 279, 183, -277, 285, 111, 266, -157, 165, 239,
    143, -279, 287, 156, -111, 119, 315, -239, 247, 321, -156, 164, 198, 35, 142, 24, 227, -183,
    -266, -22, -18, 29, -315, 323, 114, -321, 329, 110, 307, -198, 206, 236, -114, 122, 317, -21,
    28, -143, 184, -110, 118, 154, -236, 244, 192, -317, 325, 280, -154, 162, 193, 144, -192, 200,
    215, -280, 288, 273, -193, 201, 237, 225, -215, 209, 232, -273, 281, 155, -237, 245, 175, -307,
    -232, 240, 115, 23, 26, -155, 163, 194, -142, -175, 171, 195, -115, 123, 316, -194, 202, 152,
    -227, -195, 203, 314, -316, 324, 278, -152, 160, 319, -314, 322, 339, -278, 286, 174, -319,
    327, 234, -339, 335, 318, -174, 168, 320, -234, 242, 113, -318, 326, 112, -320, 328, 275, -113,
    121, 298, -112, 120, 153, -275, 283, 196, -298, 291, 151, -153, 161, 274, -196, 204, 233, -151,
    159, 150, -274, 282, 276, 309, -233, 241, 191, -150, 158, 116, 306, -276, 284, 109, -191, 199,
    235, -116, 124, 238, -109, 117, 259, 224, -235, 243, -238, 246, -259, 254, -184, 216, 145,
    -144, 176, 228, -225, -216, 212, 257, -309, 25, 34, -306, 338, -338, 332, -23, -24, 30, 27,
    186, 103, -224, -145, 177, -228, 260, -176, -177, 167, 31, -257, -260, 250, 32, 106, 308, 267,
    -186, 218, -103, 135, 185, 146, 265, 102, 268, -25, -26, -27, -1, -19, 5, -267, -106, 20, 2,
    -185, 217, 147, -308, 6, -265, 63, 61, 62, 230, -102, 134, 148, -31, -20, 38, 33, 64, -268,
    -217, -218, 208, 59, -63, 71, 65, -146, -134, 130, 300, 53, 189, 104, 66, 60, -2, 7, -147, -66,
    74, 52, 101, -230, 8, -104, 136, 226, -148, 188, 9, -189, -135, -136, 126, 178, 179, 180, 107,
    187, 10, -101, 133, 311, -226, 11, 41, 44, -188, -133, 127, 340, 341, 105, -300, 295, 138, 269,
    -178, -179, -180, 166, 299, 182, -64, -52, 72, -311, -65, 73, -187, -33, -34, 40, 54, -107,
    139, 51, 37, 45, 42, 12, 86, 91, 89, 87, -105, 137, 84, -269, 301, 90, 85, 88, -340, -341, 331,
    219, 220, 221, -32, 39, -91, 99, 77, -87, 95, -137, -138, -139, 125, 258, 141, -88, 96, 312,
    81, -41, 48, 78, -60, -53, -54, 68, -90, 98, 76, 57, -89, -77, 97, 79, -62, 70, 271, 43, 56,
    36, -61, -51, 69, -312, -299, -301, 292, 297, -219, -220, -221, 207, 343, 344, 223, -258, 251,
    256, 262, -85, -78, -79, 93, -42, 49, -86, -76, 94, 80, 82, 55, 272, -271, 303, 46, -84, -80,
    -81, -82, 100, 16, 4, 231, -43, -44, 50, 47, 310, -35, -36, -37, 13, -272, 304, -59, -55, -56,
    -57, 75, 15, 3, -310, 342, -297, -303, -304, 289, 305, -342, -343, -344, 330, -231, 263, 346,
    -256, -262, -263, 248, 264, -45, -46, -47, 14, -3, -4, 17, -182, -141, -223, -305, -346, -264,
)


def last_kernel(*refs):
    (
        back_part,
        inner_part,
        out_part,
        keep,
        given,
        tokens_all,
        normed_all,
        small_hbm,
        dense_hbm,
        tokens_hbm,
        cot_hbm,
    ) = refs[:11]
    kept_in = refs[11:22]
    mixed_out, grad_tokens_out, expert_ref, small_own, output_out, landed = refs[22:28]
    kept_refs = refs[28:39]
    (
        query_ref,
        key_ref,
        value_ref,
        log_ref,
        attended_ref,
        middle_ref,
        normed_two_ref,
        gates_ref,
        cos_ref,
        sin_ref,
        start_ref,
    ) = kept_refs
    (
        tokens,
        cot,
        mixed_ref,
        grad_tokens_ref,
        output_own,
        inner_in,
        gates_grad,
        logits_grad,
        small,
        dense,
        grad_small,
        normed,
        token_rows,
        grad_normed,
        att_send,
        att_in,
        grad_query,
        grad_key,
        grad_value,
        grad_qkv,
        gain_sum,
        grad_middle_ref,
        z_own,
        z_landed,
        y_landed,
        stage,
        terms,
        ends,
        small_theirs,
        small_landed,
        dense_theirs,
        dense_landed,
        small_cut,
        dense_cut,
        dense_in,
        s_direct,
        r_direct,
        s_reduce,
        r_reduce,
        s_dense,
        r_dense,
        s_part,
        r_part,
        l_sem,
        l_stage,
    ) = refs[39:]
    _, peers = expert_peers()
    x, y, core = dp_place()
    me = lax.axis_index("expert")
    greeted = signal_all(
        peers,
        [
            dp_index(x + 1, y, core),
            dp_index(x, y + 1, core),
            dp_index(x, y + 3, core),
            dp_index(x, y, core + 1),
        ],
    )

    def direct(i, src, out, mode):
        part = expert_copies(
            [src], [out], [mode], s_direct.at[pl.ds(i, 1)], r_direct.at[pl.ds(i, 1)]
        ) + own_copies([src], [out], [mode], l_sem.at[pl.ds(i, 1)])

        def start():
            for c in part:
                c.start()

        def wait():
            for c in part:
                c.wait()

        return start, wait

    def load(src, dst, i):
        c = pltpu.make_async_copy(src, dst, l_sem.at[i])
        c.start()
        return c

    def settle(part):
        for c in part:
            c.wait()

    OWN = ((1, 1), (3, 0), (0, 1), (0, 0))

    def from_own(dz, dx):
        return z_own[OWN.index((dz, dx))].astype(F32)

    def from_grad(dz, dx):
        return grad_normed[sums["g"].place(dz, dx)].astype(F32)

    sums = {
        "z": Reduce(back_part, from_own, z_landed, s_reduce.at[0], r_reduce.at[0]),
        "y": Reduce(out_part, from_own, y_landed, s_reduce.at[1], r_reduce.at[1]),
        "g": Reduce(grad_normed, from_grad, z_landed, s_reduce.at[2], r_reduce.at[2]),
        "o": DenseSum(dense, dense_theirs, dense_landed, s_dense.at[0], r_dense.at[0]),
        "s": DenseSum(grad_small, small_theirs, small_landed, s_dense.at[1], r_dense.at[1]),
    }
    fetched = Stage(stage, l_stage)
    for i, ((expert, _), (row, rows), _) in enumerate(PARTS):
        span = pl.ds(row, rows)
        sums["u%d." % i] = ExpertSum(
            lambda k, e=expert, r=span: terms.at[e, k, r],
            lambda k, e=expert, r=span: given.at[k, e, r],
            lambda j, e=expert, r=span: landed.at[j, e, r],
            expert_ref.at[expert, span],
            ends.at[expert, span],
            WAYS[i],
            fetched,
            s_part.at[i],
            r_part.at[i],
            l_sem.at[32 + i],
        )
    issue, arrive, done = {}, {}, {}
    for i, (name, src, out) in enumerate(
        (
            ("in", inner_part, inner_in),
            ("e", att_send, att_in),
            ("qo", dense_cut, dense_in),
            ("qs", small_cut, small_own),
        )
    ):
        issue[name], arrive[name] = direct(i, src, out, "exchange")
    for name, part in sums.items():
        for k in range(16):
            issue[name + str(k)] = functools.partial(part.issue, k)
            arrive[name + str(k)] = functools.partial(part.arrive, k)
        for k in range(8):
            if name in "zyg":
                issue[name + "ABCDEFGH"[k]] = functools.partial(part.add, k)
            elif name in "os":
                issue[name + "a%d" % k] = functools.partial(part.add, k)
            else:
                issue[name + "l%d" % k] = functools.partial(part.fetch_given, k)
                arrive[name + "l%d" % k] = functools.partial(part.wait_given, k)
                issue[name + "h%d" % k] = functools.partial(part.fetch_landed, k)
                arrive[name + "h%d" % k] = functools.partial(part.wait_landed, k)
                issue[name + "S%d" % k] = functools.partial(part.add_given, k)
                issue[name + "R%d" % k] = functools.partial(part.add_landed, k)

    def own_blocks(name, src, base):
        def start():
            done[name] = [
                load(src.at[sums["z"].place(*d)], z_own.at[i], base + i) for i, d in enumerate(OWN)
            ]

        return start, lambda: settle(done[name])

    issue["lz"], arrive["lz"] = own_blocks("lz", back_part, 8)
    issue["ly"], arrive["ly"] = own_blocks("ly", out_part, 8)

    def load_kept():
        done["lw"] = [load(a, b, 16 + i) for i, (a, b) in enumerate(zip(kept_in, kept_refs))] + [
            load(tokens_hbm, tokens, 27),
            load(cot_hbm, cot, 28),
            load(small_hbm, small, 4),
            load(dense_hbm, dense, 5),
            load(normed_all, normed, 6),
        ]

    issue["lw"], arrive["lw"] = load_kept, lambda: settle(done["lw"])

    def back_to_middle():
        for j in range(PEERS):
            gates_grad[LOCAL * j : LOCAL * (j + 1), :] = inner_in[j, 0:LOCAL, :]
        gates = gates_ref[...]
        grad_gates = gates_grad[...]
        logits_grad[...] = jnp.zeros_like(logits_grad)
        logits_grad[ROUTER - 256 : GAINS - 256, :] = gates * (
            grad_gates - jnp.sum(gates * grad_gates, axis=0, keepdims=True)
        )
        pick = (
            lax.broadcasted_iota(jnp.int32, (8, SLICE), 1)
            == lax.broadcasted_iota(jnp.int32, (8, SLICE), 0) + GAINS
        )
        gains = dot(pick.astype(F32).astype(BF), small[...].reshape(DIM, SLICE), ((1,), (1,)))
        done["gain_one"], gain_two = gains[0:1], gains[1:2]
        grad_logits = logits_grad[...].astype(BF)
        done["grad_logits"] = grad_logits
        router = small[:, :, 256:SLICE].reshape(DIM, SLICE - 256)
        grad = sums["z"].total() + dot(grad_logits, router, ((0,), (1,)))
        middle = middle_ref[...]
        scale_two = lax.rsqrt(jnp.mean(middle * middle, axis=-1, keepdims=True) + epsilon)
        gain_sum[0] = jnp.sum((grad * middle * scale_two).reshape(TOK // 8, 8, DIM), axis=0)
        grad_middle = cot[...].astype(F32) + norm_back(middle, scale_two, gain_two, grad)
        grad_middle_ref[...] = grad_middle
        grad_branch = grad_middle.astype(BF)
        done["grad_branch"] = grad_branch
        for j in range(PEERS):
            att_send[j] = dot(
                grad_branch, dense[2 * j : 2 * j + 2].reshape(QS, DIM), ((1,), (1,))
            ).astype(BF)
        sums["z"].finish()

    def output_grads():
        for j in range(PEERS):
            dense[2 * j : 2 * j + 2] = (
                dot(attended_ref[j], done["grad_branch"], ((0,), (0,)))
                .astype(BF)
                .reshape(2, ROWS, DIM)
            )

    def attend(width, i, _):
        queries = query_ref[i]
        incoming = att_in[i]
        incoming = jnp.concatenate(
            [incoming[:, h * HEAD : (h + 1) * HEAD] for h in range(REP)], axis=0
        )
        scores = dot(queries, key_ref[0:width, :], ((1,), (1,))) * HEAD ** (-0.5)
        keys = lax.broadcasted_iota(jnp.int32, (TOK, width), 1)
        rows = lax.broadcasted_iota(jnp.int32, (TOK, width), 0) + i * TOK
        begins = start_ref[pl.ds(pl.multiple_of(i * TOK, TOK), TOK), :][:, :1]
        allowed = (keys <= rows) & (keys >= begins)
        scores = jnp.where(allowed[None], scores.reshape(REP, TOK, width), masked_score)
        probs = jnp.exp(scores.reshape(REP * TOK, width) - log_ref[i][:, :1])
        grad_probs = dot(incoming, value_ref[0:width, :], ((1,), (1,)))
        inner_sum = jnp.sum(probs * grad_probs, axis=-1, keepdims=True)
        grad_scores = (probs * (grad_probs - inner_sum)).astype(BF)
        grad_query[i] = dot(grad_scores, key_ref[0:width, :], ((1,), (0,))) * HEAD ** (-0.5)
        grad_key[0:width, :] += dot(grad_scores, queries, ((0,), (0,))) * HEAD ** (-0.5)
        grad_value[0:width, :] += dot(probs.astype(BF), incoming, ((0,), (0,)))
        return _

    def attend_blocks(first, last, width):
        if first == 0:
            grad_key[...] = jnp.zeros_like(grad_key)
            grad_value[...] = jnp.zeros_like(grad_value)
        lax.fori_loop(first, last, functools.partial(attend, width), 0)

    def project(i, _):
        span = pl.ds(pl.multiple_of(i * 2 * TOK, 2 * TOK), 2 * TOK)
        rows = load(tokens_all.at[pl.ds(2 * i, 2)], token_rows, 7)
        cosine, sine = cos_ref[span, :], sin_ref[span, :]
        lane = lax.broadcasted_iota(jnp.int32, (2 * TOK, 128), 1)
        heads = [
            jnp.concatenate(
                [grad_query[2 * i + b, h * TOK : (h + 1) * TOK, :] for b in range(2)], axis=0
            )
            for h in range(REP)
        ]
        turned = []
        for pair in ((heads[0], heads[1]), (heads[2], grad_key[span, :])):
            v = jnp.concatenate(pair, axis=1)
            other = jnp.where(lane % HEAD < HEAD // 2, pltpu.roll(v, 96, 1), pltpu.roll(v, 32, 1))
            turned.append((v * cosine - other * sine).astype(BF))
        tail = jnp.concatenate(
            [grad_value[span, :], jnp.zeros((2 * TOK, SLICE - ROUTER), F32)], axis=1
        ).astype(BF)
        low = jnp.concatenate(turned + [tail], axis=1)
        grad_qkv[span, :] = low
        grad = dot(low, small[...].reshape(DIM, SLICE), ((1,), (1,)))
        grad_normed[pl.ds(2 * i, 2)] = grad.astype(BF).reshape(2, TOK, DIM)
        rows.wait()
        values = token_rows[...].reshape(2 * TOK, DIM).astype(F32)
        scale = lax.rsqrt(jnp.mean(values * values, axis=-1, keepdims=True) + epsilon)
        gain_sum[1] += jnp.sum((grad * values * scale).reshape(2 * TOK // 8, 8, DIM), axis=0)
        return _

    def project_blocks(first, last):
        if first == 0:
            gain_sum[1] = jnp.zeros((8, DIM), F32)
        lax.fori_loop(first, last, project, 0)

    def small_grads():
        lanes = lax.broadcasted_iota(jnp.int32, (8, 128), 1)
        marks = [(lanes == GAINS - 256 + i).astype(F32).astype(BF) for i in range(2)]
        for c in range(4):
            span = slice(c * 384, (c + 1) * 384)
            part = dot(normed[:, :, span].reshape(GROUP, 384), grad_qkv[...], ((0,), (0,)))
            extra = dot(normed_two_ref[:, span], done["grad_logits"], ((0,), (1,)))
            for i in range(2):
                value = gain_sum[1 - i, :, span]
                high = value.astype(BF)
                rest = (value - high.astype(F32)).astype(BF)
                extra = extra + dot(high, marks[i], ((0,), (0,)))
                extra = extra + dot(rest, marks[i], ((0,), (0,)))
            grad_small[4 * c : 4 * c + 4, :, 0:256] = (
                part[:, 0:256].astype(BF).reshape(4, ROWS, 256)
            )
            grad_small[4 * c : 4 * c + 4, :, 256:SLICE] = (
                (part[:, 256:SLICE] + extra).astype(BF).reshape(4, ROWS, SLICE - 256)
            )

    saves = []

    def mix():
        mixed_ref[...] = (middle_ref[...] + sums["y"].total()).astype(BF)
        saves.append(load(mixed_ref, mixed_out, 29))

    def token_grads():
        values = tokens[...].astype(F32)
        scale = lax.rsqrt(jnp.mean(values * values, axis=-1, keepdims=True) + epsilon)
        grad_tokens_ref[...] = grad_middle_ref[...] + norm_back(
            values, scale, done["gain_one"], sums["g"].total()
        )
        saves.append(load(grad_tokens_ref, grad_tokens_out, 30))

    def total_of(name):
        done[name] = sums[name].sum(0)

    def cut(name, ref):
        for j in range(PEERS):
            ref[j] = done[name][12 * j : 12 * (j + 1)]

    def own_output():
        acc = dense_in[0]
        for j in range(1, PEERS):
            acc = acc + dense_in[j]
        output_own[...] = acc
        saves.append(load(output_own, output_out, 31))

    issue["C4"], issue["GO"], issue["GS"] = back_to_middle, output_grads, small_grads
    issue["A0"] = functools.partial(attend_blocks, 0, 4, GROUP // 2)
    issue["A1"] = functools.partial(attend_blocks, 4, 6, GROUP)
    issue["A2"] = functools.partial(attend_blocks, 6, 8, GROUP)
    issue["P0"] = functools.partial(project_blocks, 0, 2)
    issue["P1"] = functools.partial(project_blocks, 2, 4)
    issue["MX"], issue["GT"], issue["FI"] = mix, token_grads, own_output
    issue["ot"], issue["st"] = functools.partial(total_of, "o"), functools.partial(total_of, "s")
    issue["CO"] = functools.partial(cut, "o", dense_cut)
    issue["CS"] = functools.partial(cut, "s", small_cut)

    mine = [load(keep.at[:, e], terms.at[e], 38 + e) for e in range(LOCAL)]
    greeted()
    held = set()
    for step in LAST_ORDER:
        name = LAST_STEPS[abs(step) - 1]
        if name[0] == "u" and name[3] == "S":
            expert = PARTS[int(name[1])][0][0]
            if expert not in held:
                held.add(expert)
                mine[expert].wait()
        if name[0] == "u" and name[3:] == "w":
            part = sums[name[:3]]
            if step > 0:
                part.write()
            else:
                part.save.wait()
            continue
        (issue if step > 0 else arrive)[name]()
    for part in sums.values():
        part.finish()
    settle(saves)


def last_phase(*args):
    hbm = pl.BlockSpec(memory_space=pltpu.HBM)
    shape, dma = jax.ShapeDtypeStruct, pltpu.SemaphoreType.DMA
    blocks = (PEERS, TOK, DIM)
    piece = (3 * ROWS, FFE)
    outs = [
        (shape((TOK, DIM), BF), hbm),
        (shape((TOK, DIM), F32), hbm),
        (shape((LOCAL,) + piece, F32), hbm),
        (shape((PEERS, 12, SLICE), F32), hbm),
        (shape((12, DIM), F32), hbm),
        (shape((8, LOCAL) + piece, BF), hbm),
    ]
    return pl.pallas_call(
        last_kernel,
        out_shape=[o[0] for o in outs],
        in_specs=[hbm] * 22,
        out_specs=[o[1] for o in outs],
        scratch_shapes=[pltpu.VMEM(k.shape, k.dtype) for k in KEPT]
        + [
            pltpu.VMEM((TOK, DIM), BF),
            pltpu.VMEM((TOK, DIM), BF),
            pltpu.VMEM((TOK, DIM), BF),
            pltpu.VMEM((TOK, DIM), F32),
            pltpu.VMEM((12, DIM), F32),
            pltpu.VMEM((PEERS, 8, TOK), F32),
            pltpu.VMEM((EXPERTS, TOK), F32),
            pltpu.VMEM((SLICE - 256, TOK), F32),
            pltpu.VMEM((DP, ROWS, SLICE), BF),
            pltpu.VMEM((DP, ROWS, DIM), BF),
            pltpu.VMEM((DP, ROWS, SLICE), BF),
            pltpu.VMEM(blocks, BF),
            pltpu.VMEM((2, TOK, DIM), BF),
            pltpu.VMEM(blocks, BF),
            pltpu.VMEM((PEERS, TOK, QS), BF),
            pltpu.VMEM((PEERS, TOK, QS), BF),
            pltpu.VMEM((PEERS, REP * TOK, HEAD), F32),
            pltpu.VMEM((GROUP, HEAD), F32),
            pltpu.VMEM((GROUP, HEAD), F32),
            pltpu.VMEM((GROUP, SLICE), BF),
            pltpu.VMEM((2, 8, DIM), F32),
            pltpu.VMEM((TOK, DIM), F32),
            pltpu.VMEM((4, TOK, DIM), BF),
            pltpu.VMEM((7, TOK, DIM), BF),
            pltpu.VMEM((7, TOK, DIM), BF),
            pltpu.VMEM((8,) + piece, BF),
            pltpu.VMEM((LOCAL, 8) + piece, BF),
            pltpu.VMEM((LOCAL,) + piece, F32),
            pltpu.VMEM((8, ROWS, SLICE), BF),
            pltpu.VMEM((7, ROWS, SLICE), BF),
            pltpu.VMEM((8, ROWS, DIM), BF),
            pltpu.VMEM((7, ROWS, DIM), BF),
            pltpu.VMEM((PEERS, 12, SLICE), F32),
            pltpu.VMEM((PEERS, 12, DIM), F32),
            pltpu.VMEM((PEERS, 12, DIM), F32),
            dma((4, 7)),
            dma((4, 7)),
            dma((3, 7)),
            dma((3, 7)),
            dma((2, 16)),
            dma((2, 16)),
            dma((len(PARTS), 8)),
            dma((len(PARTS), 8)),
            dma((43,)),
            dma((8,)),
        ],
        compiler_params=pltpu.CompilerParams(
            collective_id=3, has_side_effects=True, vmem_limit_bytes=63 << 20
        ),
        cost_estimate=lasting(120),
    )(*args)


def experts_kernel(*refs):
    (rows_ref, cot_ref, slot_ref, gate_ref), refs = refs[:4], refs[4:]
    pieces, refs = refs[0], refs[1:]
    (out_ref, back_ref, inner_ref, keep_ref, given_ref), refs = refs[:5], refs[5:]
    xg, cg, weights, grads, gates, inners, wsem, gsem, rsem = refs
    x, y, core = dp_place()
    other = dp_index(x, y, core + 1)
    greeted = signal_all([], [other])

    def load(e, b):
        return pltpu.make_async_copy(pieces.at[:, e], weights.at[b], wsem.at[b])

    def kept(e, b):
        return [
            pltpu.make_async_copy(
                grads.at[b, dp_index(x + rx, y + ry, core)], keep_ref.at[k, e], gsem.at[b, k]
            )
            for k, (rx, ry) in enumerate(SLOTS)
        ]

    def given(e, b):
        return [
            pltpu.make_async_remote_copy(
                src_ref=grads.at[b, dp_index(x + rx, y + ry, core + 1)],
                dst_ref=given_ref.at[k, e],
                send_sem=gsem.at[b, 8 + k],
                recv_sem=rsem.at[e, k],
                device_id={"dp": other},
                device_id_type=MESH,
            )
            for k, (rx, ry) in enumerate(SLOTS)
        ]

    def stored(e, b):
        for c in kept(e, b):
            c.wait()
        for c in given(e, b):
            c.wait_send()

    load(0, 0).start()

    def onehot(b):
        places = lax.broadcasted_iota(jnp.int32, (CAP, TOK), 0).astype(F32)
        return [(places == slot_ref[b, e : e + 1, :]) for e in range(LOCAL)]

    def collect(b, _):
        hot = onehot(b)
        pick = jnp.concatenate([h.astype(F32) for h in hot], axis=0).astype(BF)
        xg[b] = dot(pick, rows_ref[b], ((1,), (0,))).astype(BF)
        cg[b] = dot(pick, cot_ref[b], ((1,), (0,))).astype(BF)
        for e in range(LOCAL):
            g = jnp.sum(jnp.where(hot[e], gate_ref[b, e : e + 1, :], 0.0), axis=1, keepdims=True)
            gates[e, pl.ds(b * CAP, CAP), :] = jnp.broadcast_to(g, (CAP, 128))
        return _

    lax.fori_loop(0, PEERS, collect, 0)
    greeted()

    def expert(e, _):
        b = lax.rem(e, 2)
        load(e, b).wait()

        @pl.when(e + 1 < LOCAL)
        def _next():
            load(e + 1, 1 - b).start()

        @pl.when(e >= 2)
        def _free():
            stored(e - 2, b)

        span = pl.ds(pl.multiple_of(e * CAP, CAP), CAP)
        rows = xg[:, span, :].reshape(PEERS * CAP, DIM)
        cot = cg[:, span, :].reshape(PEERS * CAP, DIM)
        gate = gates[e][:, :1]
        w_gate = weights[b, :, 0:96, :].reshape(DIM, FFE)
        gate_act = dot(rows, w_gate, ((1,), (0,)))
        w_up = weights[b, :, 96:192, :].reshape(DIM, FFE)
        up_act = dot(rows, w_up, ((1,), (0,)))
        sig = 1.0 / (1.0 + jnp.exp(-gate_act))
        silu = gate_act * sig
        hidden = (silu * up_act).astype(BF)
        grad_out = (cot.astype(F32) * gate).astype(BF)
        inner = jnp.zeros((PEERS * CAP, 1), F32)
        grad_hidden = jnp.zeros((PEERS * CAP, FFE), F32)
        gated = []
        for k in range(3):
            lanes = slice(k * FFE, (k + 1) * FFE)
            w_down = weights[b, :, 192 + 32 * k : 224 + 32 * k, :].reshape(FFE, FFE)
            part = dot(hidden, w_down, ((1,), (0,))).astype(BF).astype(F32)
            inner = inner + jnp.sum(part * cot[:, lanes].astype(F32), axis=1, keepdims=True)
            gated.append((part * gate).astype(BF))
            grad_hidden = grad_hidden + dot(grad_out[:, lanes], w_down, ((1,), (1,)))
            grads[b, :, 192 + 32 * k : 224 + 32 * k, :] = (
                dot(hidden, grad_out[:, lanes], ((0,), (0,))).astype(BF).reshape(DP, 32, FFE)
            )
        inners[e] = jnp.broadcast_to(inner, (PEERS * CAP, 128))
        grad_gate = (grad_hidden * up_act * sig * (1.0 + gate_act * (1.0 - sig))).astype(BF)
        grad_up = (grad_hidden * silu).astype(BF)
        grads[b, :, 0:96, :] = (
            dot(rows, grad_gate, ((0,), (0,))).astype(BF).reshape(DP, ROWS, FFE)
        )
        grads[b, :, 96:192, :] = (
            dot(rows, grad_up, ((0,), (0,))).astype(BF).reshape(DP, ROWS, FFE)
        )
        for c in kept(e, b) + given(e, b):
            c.start()
        back = dot(grad_gate, w_gate, ((1,), (1,))) + dot(grad_up, w_up, ((1,), (1,)))
        xg[:, span, :] = back.astype(BF).reshape(PEERS, CAP, DIM)
        for k in range(3):
            cg[:, span, k * FFE : (k + 1) * FFE] = gated[k].reshape(PEERS, CAP, FFE)
        return _

    lax.fori_loop(0, LOCAL, expert, 0)

    def combine(b, _):
        hot = onehot(b)
        pick = jnp.concatenate([h.astype(F32) for h in hot], axis=0).astype(BF)
        out_ref[b] = dot(pick, cg[b], ((0,), (0,))).astype(BF)
        back_ref[b] = dot(pick, xg[b], ((0,), (0,))).astype(BF)
        lines = []
        for e in range(LOCAL):
            value = inners[e, pl.ds(b * CAP, CAP), :][:, :1]
            lines.append(jnp.sum(jnp.where(hot[e], value, 0.0), axis=0, keepdims=True))
        inner_ref[b] = jnp.concatenate(lines + [jnp.zeros((8 - LOCAL, TOK), F32)], axis=0)
        return _

    lax.fori_loop(0, PEERS, combine, 0)
    for e in (LOCAL - 2, LOCAL - 1):
        stored(e, e % 2)
    for e in range(LOCAL):
        for c in given(e, e % 2):
            c.wait_recv()


def run_experts(rows, cot, slots, gates, pieces):
    vmem = pl.BlockSpec(memory_space=pltpu.VMEM)
    piece = (LOCAL, 3 * ROWS, FFE)
    return pl.pallas_call(
        experts_kernel,
        out_shape=[
            jax.ShapeDtypeStruct((PEERS, TOK, DIM), BF),
            jax.ShapeDtypeStruct((PEERS, TOK, DIM), BF),
            jax.ShapeDtypeStruct((PEERS, 8, TOK), F32),
            jax.ShapeDtypeStruct((8,) + piece, BF),
            jax.ShapeDtypeStruct((8,) + piece, BF),
        ],
        in_specs=[vmem] * 4 + any_specs(1),
        out_specs=[vmem] * 3 + any_specs(2),
        scratch_shapes=[
            pltpu.VMEM((PEERS, LOCAL * CAP, DIM), BF),
            pltpu.VMEM((PEERS, LOCAL * CAP, DIM), BF),
            pltpu.VMEM((2, DP, 3 * ROWS, FFE), BF),
            pltpu.VMEM((2, DP, 3 * ROWS, FFE), BF),
            pltpu.VMEM((LOCAL, PEERS * CAP, 128), F32),
            pltpu.VMEM((LOCAL, PEERS * CAP, 128), F32),
            pltpu.SemaphoreType.DMA((2,)),
            pltpu.SemaphoreType.DMA((2, 16)),
            pltpu.SemaphoreType.DMA((LOCAL, 8)),
        ],
        compiler_params=pltpu.CompilerParams(
            collective_id=2, has_side_effects=True, vmem_limit_bytes=63 << 20
        ),
        cost_estimate=pl.CostEstimate(
            flops=20_000_000_000, bytes_accessed=60_000_000, transcendentals=700_000
        ),
    )(rows, cot, slots, gates, pieces)


def finish_kernel(mixed, tokens, experts, small, output, *refs):
    outs, (mixed_ref, tokens_ref, experts_ref, small_ref, output_ref, cut_ref, sem) = (
        refs[:10],
        refs[10:],
    )
    mixed_out, tokens_out, q_out, k_out, v_out, output_out, tail_out, gate, up, down = outs
    loads = [
        pltpu.make_async_copy(src, dst, sem.at[13 + i])
        for i, (src, dst) in enumerate(
            (
                (small, small_ref),
                (experts, experts_ref),
                (tokens, tokens_ref),
                (mixed, mixed_ref),
                (output, output_ref),
            )
        )
    ]
    for c in loads:
        c.start()
    for c in loads[1:]:
        c.wait()
    copies = [
        pltpu.make_async_copy(mixed_ref, mixed_out, sem.at[1]),
        pltpu.make_async_copy(tokens_ref, tokens_out, sem.at[2]),
        pltpu.make_async_copy(output_ref, output_out, sem.at[3]),
        pltpu.make_async_copy(experts_ref.at[:, pl.ds(0, ROWS)], gate, sem.at[4]),
        pltpu.make_async_copy(experts_ref.at[:, pl.ds(ROWS, ROWS)], up, sem.at[5]),
    ] + [
        pltpu.make_async_copy(
            experts_ref.at[:, pl.ds(2 * ROWS + 32 * k, 32)],
            down.at[:, :, pl.ds(k * FFE, FFE)],
            sem.at[6 + k],
        )
        for k in range(3)
    ]
    for c in copies:
        c.start()
    loads[0].wait()
    total = small_ref[0]
    for j in range(1, PEERS):
        total = total + small_ref[j]
    cut_ref[...] = jnp.concatenate(
        [small_ref[j, :, :QS] for j in range(PEERS)]
        + [small_ref[j, :, QS : QS + HEAD] for j in range(PEERS)]
        + [small_ref[j, :, QS + HEAD : ROUTER] for j in range(PEERS)]
        + [total[:, 256:SLICE]],
        axis=1,
    )
    widths = (DIM, KV_HEADS * HEAD, KV_HEADS * HEAD, SLICE - 256)
    begins = (0, DIM, DIM + KV_HEADS * HEAD, DIM + 2 * KV_HEADS * HEAD)
    for i, ref in enumerate((q_out, k_out, v_out, tail_out)):
        c = pltpu.make_async_copy(cut_ref.at[:, pl.ds(begins[i], widths[i])], ref, sem.at[9 + i])
        c.start()
        copies.append(c)
    for c in copies:
        c.wait()


def finish(*args):
    shape = jax.ShapeDtypeStruct
    width = KV_HEADS * HEAD
    return pl.pallas_call(
        finish_kernel,
        out_shape=[
            shape((TOK, DIM), BF),
            shape((TOK, DIM), F32),
            shape((12, DIM), F32),
            shape((12, width), F32),
            shape((12, width), F32),
            shape((12, DIM), F32),
            shape((12, SLICE - 256), F32),
            shape((LOCAL, ROWS, FFE), F32),
            shape((LOCAL, ROWS, FFE), F32),
            shape((LOCAL, 32, DIM), F32),
        ],
        in_specs=any_specs(5),
        out_specs=any_specs(10),
        scratch_shapes=[
            pltpu.VMEM((TOK, DIM), BF),
            pltpu.VMEM((TOK, DIM), F32),
            pltpu.VMEM((LOCAL, 3 * ROWS, FFE), F32),
            pltpu.VMEM((PEERS, 12, SLICE), F32),
            pltpu.VMEM((12, DIM), F32),
            pltpu.VMEM((12, DIM + 2 * width + SLICE - 256), F32),
            pltpu.SemaphoreType.DMA((18,)),
        ],
        compiler_params=pltpu.CompilerParams(vmem_limit_bytes=63 << 20),
    )(*args)


def norm_back(values, row_scale, gain_vector, grad_normed):
    weighted = grad_normed * gain_vector
    return row_scale * weighted - values * row_scale**3 * jnp.mean(
        weighted * values, axis=-1, keepdims=True
    )


def local(
    tokens,
    cotangent,
    seq_lengths,
    expert_ids,
    w_query,
    w_key,
    w_value,
    w_output,
    norm_one,
    norm_two,
    w_router,
    w_gate,
    w_up,
    w_down,
):
    tail = jnp.concatenate(
        [w_router, norm_one[:, None], norm_two[:, None], jnp.zeros((12, SLICE - GAINS - 2), BF)],
        axis=1,
    )
    (
        pieces,
        cot_all,
        slots_all,
        rows_all,
        gates_all,
        tokens_all,
        normed_all,
        slices_all,
        output_all,
        *kept,
    ) = first_phase(
        w_query,
        w_key,
        w_value,
        tail,
        w_output,
        tokens,
        cotangent,
        expert_ids,
        seq_lengths,
        w_gate,
        w_up,
        w_down,
    )
    out_part, back_part, inner_part, keep, given = run_experts(
        rows_all, cot_all, slots_all, gates_all, pieces
    )
    mixed, grad_tokens, expert_grads, small_own, output_own, _ = last_phase(
        back_part,
        inner_part,
        out_part,
        keep,
        given,
        tokens_all,
        normed_all,
        slices_all,
        output_all,
        tokens,
        cotangent,
        *kept,
    )
    mixed, grad_tokens, query, key, value, output, rest, gate, up, down = finish(
        mixed, grad_tokens, expert_grads, small_own, output_own
    )
    rest = rest[:, ROUTER - 256 :]
    return (
        mixed,
        grad_tokens,
        query,
        key,
        value,
        output,
        rest[:, EXPERTS],
        rest[:, EXPERTS + 1],
        rest[:, :EXPERTS],
        gate,
        up,
        down,
    )


def solution(mesh):
    both = P(("dp", "expert"), None)
    line = P(("dp", "expert"))
    cube = P("expert", "dp", None)
    in_specs = (both, both, P("dp", None), both, both, both, both, both)
    in_specs = in_specs + (line, line, both, cube, cube, cube)
    out_specs = (both,) * 6 + (line, line, both, cube, cube, cube)
    return jax.shard_map(local, mesh=mesh, in_specs=in_specs, out_specs=out_specs, check_vma=False)
```
